32 devices in a mesh: grp: 4 (over y, x), tile: 8 (over z, core).
Axes of the slice: x: 2, y: 2, z: 4, core: 2. Of those that a mesh axis runs over, the one named last changes fastest.
Arguments:
- state: float32 [64, 256, 512], P(None, ('grp', 'tile')), may hold values from -6 to 6
- vert_coef: float32 [63, 256, 512], P(None, ('grp', 'tile')), may hold values from 0.0004 to 1200
- horiz_coef: float32 [256, 512], P(('grp', 'tile')), may hold values from 0.02 to 0.24
- wet_mask: int32 [64, 512], P('tile'), may hold values 0 or 1
- coupling: float32 [4, 256, 512], P(None, ('grp', 'tile')), may hold values from 0.1 to 1
- surface_in: float32 [4, 256, 512], P(None, ('grp', 'tile')), may hold values from -6 to 6
- remap_w: bfloat16 [1024, 4, 128, 128], P(('grp', 'tile')), may hold values from -0.25 to 0.25
- dest_tile: int32 [1024, 4], P(('grp', 'tile')), may hold values from 0 to 7, all different within a row; in each aligned block of 32 rows (0 to 31, 32 to 63, ...) at most 32 rows name the same one
- dest_block: int32 [1024, 4], P(('grp', 'tile')), may hold values from 0 to 31
- dest_group: int32 [1024, 4], P(('grp', 'tile')), may hold values from 0 to 2
Outputs:
- state_out: float32 [64, 256, 512], P(None, ('grp', 'tile'))
- received: float32 [4, 256, 512], P(None, ('grp', 'tile'))
The draws below stay inside these ranges and needn't reach their ends.
Inputs may be any that keep to these rules, and one draw needn't show every extreme that they name: `dest_tile`: A row's 4 strip indices differ; within the 32 rows of one device no strip index appears more than 32 times, and some device reaches 32.
All inputs are finite; a program needn't handle non-finite values. No bound on the sum of `wet_mask` on one device may be relied on, other than what follows from the above.
Results may differ from the reference program's by a relative error of at most 0.0029.
Values sent between devices are 32-bit elements; how exact they have to be, the bound alone decides.
No kernel may reach another device: no remote copies, remote signals or barrier semaphores. Data moves between devices by JAX's collectives and lax.ppermute only.
A program may use at most 64 MiB of HBM per device.

```python
import math
import jax
import jax.numpy as jnp
import numpy as np
from jax import lax

LEV = 64
F = 4
K = 4
STEPS = 2
CY = 8
CX = 512
NB = 32
S = 32
ROWS = 256
OROWS = 64
NBLK = 1024
N_GRP = 4
N_TILE = 8


def draw_vert_coef(key, part):
    key_strength = jax.random.fold_in(key, 11)
    key_rough = jax.random.fold_in(key, 12)
    key_pulse = jax.random.fold_in(key, 13)
    key_depth = jax.random.fold_in(key, 14)
    low_log = math.log(0.3)
    high_log = math.log(500.0)
    array_shape = (LEV - 1, ROWS, CX)
    column_u = jax.random.uniform(key_strength, (1, ROWS, CX), jnp.float32)
    strength = jnp.exp(low_log + column_u * (high_log - low_log))
    rough = jnp.exp(jax.random.uniform(key_rough, array_shape, jnp.float32, -math.log(2.0), math.log(2.0)))
    flux_pulse = jax.random.bernoulli(key_pulse, 0.05, array_shape)
    ocean_depth = jnp.exp(jax.random.uniform(key_depth, array_shape, jnp.float32, math.log(0.003), math.log(0.03)))
    cutoff_value = jnp.where(flux_pulse, ocean_depth, jnp.ones(array_shape, jnp.float32))
    return (strength * rough * cutoff_value).astype(jnp.float32)


def touch_ends(drawn, key, smallest, high):
    place = [jax.random.randint(jax.random.fold_in(key, axis), (), 0, length) for axis, length in enumerate(drawn.shape)]
    main_axis = drawn.shape.index(max(drawn.shape))
    beside = place[:main_axis] + [(place[main_axis] + 1) % drawn.shape[main_axis]] + place[main_axis + 1:]
    return drawn.at[tuple(place)].set(smallest).at[tuple(beside)].set(high)


def level_of(stream_key, extent, cuts, least, top_value):
    def one(position, blocks):
        heights = jax.random.uniform(jax.random.fold_in(jax.random.fold_in(stream_key, 6), position), (blocks,), jnp.float32, least / len(cuts), top_value / len(cuts))
        return jnp.repeat(jnp.exp(heights), extent[position] // blocks).reshape((-1,) + (1,) * (len(extent) - position - 1))

    factor_of = one(*cuts[0])
    for cut in cuts[1:]:
        factor_of = factor_of * one(*cut)
    return factor_of


def assign_block(key, own, number, rows, number_of, top, reach, lean):
    sequence = jax.random.permutation(key, number_of)
    crowded, common = portions_of(number_of, rows * top, reach, lean, True), portions_of(number_of, rows * top, reach, lean, False)
    places = jnp.arange(number_of)

    def named(lengths, turn):
        used = int((lengths > 0).sum())
        fixed = max(1, used // 4)
        passed = fixed + (places - fixed + turn * (used - fixed)) % max(1, number_of - fixed)
        return jnp.zeros((number_of,), jnp.int32).at[sequence[jnp.where(places < fixed, places, passed)]].set(jnp.asarray(lengths, jnp.int32))

    lengths = jnp.where(number % 4 == 0, named(crowded, number // 4), named(common, number - number // 4 - 1))
    mixed = jax.random.permutation(jax.random.fold_in(own, 3), number_of)
    source_of, receiver = mixed[0:number_of // 2 * 2:2], mixed[1:number_of // 2 * 2:2]
    slack = jnp.minimum(lengths[source_of] - 1, reach - lengths[receiver]) // 2
    slack = jnp.where((source_of == sequence[0]) | (receiver == sequence[0]) | (lengths[receiver] == 0), 0, jnp.maximum(slack, 0))
    passed = jax.random.randint(jax.random.fold_in(own, 4), (number_of // 2,), 0, 1 << 20) % (slack + 1)
    lengths = lengths.at[source_of].add(-passed).at[receiver].add(passed)
    items = jnp.searchsorted(jnp.cumsum(lengths), jnp.arange(rows * top), side="right").astype(jnp.int32)
    grid = items.reshape(top, rows).T
    grid = grid[jax.random.permutation(jax.random.fold_in(own, 1), rows)]
    turn = jax.random.randint(jax.random.fold_in(own, 2), (rows, 1), 0, top)
    return jnp.take_along_axis(grid, (jnp.arange(top)[None, :] + turn) % top, axis=1)


def portions_of(amount, total, reach, lean, full):
    weights = [(1 << 20) // math.isqrt(rank ** lean) + 1 for rank in range(1, amount + 1)]
    largest = reach if full else min(reach, max(-(-total // amount), total * weights[0] // sum(weights)))
    least = 1 if total - largest >= amount - 1 else 0
    counts, spare = [largest] + [least] * (amount - 1), total - largest - least * (amount - 1)
    while spare > 0:
        candidates = [i for i in range(1, amount) if counts[i] < largest] or [i for i in range(1, amount) if counts[i] < reach]
        pool, remaining = sum([weights[i] for i in candidates]), spare
        for i in candidates:
            addition = min(reach - counts[i], max(1, remaining * weights[i] // pool), spare)
            counts[i] = counts[i] + addition
            spare = spare - addition
    return np.array(counts)


def noise(key, dims, scale, reach, split=(), kind=jnp.bfloat16):
    level = level_of(key, dims, split, -0.22, 0.18) if split else 1.0
    entries = jax.random.normal(key, dims, jnp.float32) * scale * level
    return jnp.minimum(jnp.maximum(entries, -reach), reach).astype(kind)


def setup_inputs(seed: int = 0) -> dict:
    splits = jax.random.split(jax.random.key(seed), 11)
    state = noise(splits[0], (LEV, ROWS, CX), 1.0, 6.0, ((1, 32),), jnp.float32)
    vert_coef = draw_vert_coef(jax.random.fold_in(splits[10], 71), 0)
    horiz_coef = jnp.clip(jnp.exp(math.log(0.24) - 2.4849066 * jax.random.uniform(splits[2], (ROWS, CX), jnp.float32) ** level_of(splits[2], (ROWS, CX), ((0, 32),), -0.2, 0.2)), 0.02, 0.24)
    wet_mask = touch_ends((jax.random.randint(splits[3], (OROWS, CX), 0, 4) < 3).astype(jnp.int32), jax.random.fold_in(splits[3], 1), 0, 1)
    coupling = jnp.clip(jnp.exp(math.log(1.0) - 2.3025851 * jax.random.uniform(splits[4], (F, ROWS, CX), jnp.float32) ** level_of(splits[4], (F, ROWS, CX), ((1, 32),), -0.2, 0.2)), 0.1, 1.0)
    surface_in = noise(splits[5], (F, ROWS, CX), 1.0, 6.0, ((1, 32),), jnp.float32)
    remap_w = noise(splits[6], (NBLK, K, 128, 128), (128 * K) ** -0.5, 0.25, ((0, 32),))
    dest_tile_keys = jax.random.split(jax.random.fold_in(splits[7], 1), NBLK // NB)
    dest_tile_turns = jax.random.permutation(jax.random.fold_in(splits[7], 3), NBLK // NB)
    dest_tile = jax.vmap(lambda own, number: assign_block(jax.random.fold_in(splits[7], 2), own, number, NB, N_TILE, K, S, 2))(dest_tile_keys, dest_tile_turns).reshape((NBLK, K))
    dest_block = touch_ends(jax.random.randint(splits[8], (NBLK, K), 0, NB), jax.random.fold_in(splits[8], 1), 0, NB - 1).astype(jnp.int32)
    dest_group = touch_ends(jax.random.randint(splits[9], (NBLK, K), 0, 3), jax.random.fold_in(splits[9], 1), 0, 2).astype(jnp.int32)
    return {"state": state, "vert_coef": vert_coef, "horiz_coef": horiz_coef, "wet_mask": wet_mask, "coupling": coupling, "surface_in": surface_in, "remap_w": remap_w, "dest_tile": dest_tile, "dest_block": dest_block, "dest_group": dest_group}


FORCING_GAIN = 0.25


def vertical_solve(column_rhs, lower, upper):
    def forward(carry, items):
        c_prev, r_prev = carry
        low, upp, rhs = items
        denom = 1.0 + low + upp + low * c_prev
        c_now = -upp / denom
        r_now = (rhs + low * r_prev) / denom
        return (c_now, r_now), (c_now, r_now)

    zero = jnp.zeros(column_rhs.shape[1:], jnp.float32)
    _, (c_all, r_all) = lax.scan(forward, (zero, zero), (lower, upper, column_rhs))

    def backward(x_next, items):
        c_now, r_now = items
        x_now = r_now - c_now * x_next
        return x_now, x_now

    _, solved = lax.scan(backward, zero, (c_all, r_all), reverse=True)
    return solved


def horizontal(field, nu, wet, above, below, wet_above, wet_underneath, keep_above, keep_below):
    left = jnp.pad(field[:, :, :-1], ((0, 0), (0, 0), (1, 0)))
    right = jnp.pad(field[:, :, 1:], ((0, 0), (0, 0), (0, 1)))
    wet_left = jnp.pad(wet[:, :-1], ((0, 0), (1, 0)))
    wet_right = jnp.pad(wet[:, 1:], ((0, 0), (0, 1)))
    total = wet_left * (left - field) + wet_right * (right - field)
    total = total + keep_above * wet_above * (above - field) + keep_below * wet_underneath * (below - field)
    return field + nu * wet * total


def reference(state, vert_coef, horiz_coef, wet_mask, coupling, surface_in, remap_w, dest_tile, dest_block, dest_group):
    levels, rows, width = state.shape
    devices = N_GRP * N_TILE
    blocks = CY * CX // 128
    ocean_start = 3 * N_TILE * CY
    wet = jnp.concatenate([jnp.ones((ocean_start, width), jnp.float32), wet_mask.astype(jnp.float32)], 0)
    send = (coupling * (state[0][None] - surface_in) * wet[None]).astype(jnp.bfloat16)
    send = send.reshape(F, devices, blocks, 128).transpose(1, 2, 0, 3)

    def contribute(items):
        piece, weights = items
        return jnp.einsum("bfi,bkij->bkfj", piece.astype(jnp.float32), weights.astype(jnp.float32))

    terms = lax.map(contribute, (send, remap_w.reshape(devices, blocks, K, 128, 128)))
    source_group = (jnp.arange(devices * blocks, dtype=jnp.int32) // (blocks * N_TILE))[:, None]
    target_group = jnp.where(source_group < 3, 3, dest_group).astype(jnp.int32)
    target = ((target_group * N_TILE + dest_tile) * blocks + dest_block).astype(jnp.int32)
    summed = jax.ops.segment_sum(terms.reshape(devices * blocks * K, F * 128), target.reshape(-1), num_segments=devices * blocks)
    received = summed.reshape(devices, blocks, F, 128).transpose(2, 0, 1, 3).reshape(F, rows, width)

    row_ids = jnp.arange(rows, dtype=jnp.int32)
    keep_above = ((row_ids > 0) & (row_ids != ocean_start)).astype(jnp.float32)[:, None]
    keep_below = ((row_ids < rows - 1) & (row_ids + 1 != ocean_start)).astype(jnp.float32)[:, None]
    wet_above = jnp.pad(wet[:-1], ((1, 0), (0, 0)))
    wet_underneath = jnp.pad(wet[1:], ((0, 1), (0, 0)))
    forcing = FORCING_GAIN * wet * jnp.sum(received, 0)
    scaled = vert_coef * wet[None]
    edge = jnp.zeros((1, rows, width), jnp.float32)
    lower = jnp.concatenate([edge, scaled], 0)
    upper = jnp.concatenate([scaled, edge], 0)
    field = state
    for step in range(STEPS):
        above = jnp.pad(field[:, :-1], ((0, 0), (1, 0), (0, 0)))
        below = jnp.pad(field[:, 1:], ((0, 0), (0, 1), (0, 0)))
        field = horizontal(field, horiz_coef, wet, above, below, wet_above, wet_underneath, keep_above, keep_below)
        field = field.at[0].add(forcing)
        field = vertical_solve(field, lower, upper)
    return field, received
```

```python
import functools

import jax
import jax.numpy as jnp
from jax import lax
from jax.experimental import pallas as pl
from jax.experimental.pallas import tpu as pltpu
from jax.sharding import PartitionSpec as P

F = 4
K = 4
FORCING_GAIN = 0.25
VM = pl.BlockSpec(memory_space=pltpu.VMEM)
MIB = 1024 * 1024


def params(mib):
    return pltpu.CompilerParams(vmem_limit_bytes=mib * MIB)


def split(x):
    hi = x.astype(jnp.bfloat16)
    return hi, (x - hi.astype(jnp.float32)).astype(jnp.bfloat16)


def wet_of(ocean, mask):
    return jnp.where(ocean, mask.astype(jnp.float32), 1.0)


def iota(shape, dim):
    return lax.broadcasted_iota(jnp.int32, shape, dim)


def pack_kernel(
    tiles, slots, state, coupling, surface, mask, dtile, dblock, dgroup, w_hbm, out, w, terms, sem
):
    height, width = mask.shape
    cols = width // 128
    blocks = height * cols
    count = blocks * K
    copies = [
        pltpu.make_async_copy(w_hbm.at[:, c], w.at[c], sem.at[c]) for c in range(cols)
    ]
    for copy in copies:
        copy.start()
    ocean = lax.axis_index("grp") == 3
    me = lax.axis_index("tile")

    block = dblock[...]
    row = (block % cols) * height + block // cols
    code = dtile[...] * 128 + row + jnp.where(ocean, dgroup[...] * blocks, 0)
    lane = iota((blocks, count), 1)
    lane_k = (lane // height) % K
    spread = jnp.zeros((blocks, count), jnp.int32)
    for k in range(K):
        spread = jnp.where(lane_k == k, code[:, k : k + 1], spread)
    own = iota((blocks, count), 0) == (lane % height) * cols + lane // (height * K)
    code_row = jnp.sum(jnp.where(own, spread, 0), 0, keepdims=True)
    up, down = iota((count, count), 0), iota((count, count), 1)
    code_col = jnp.sum(jnp.where(up == down, code_row, 0), 1, keepdims=True)
    tile_row, tile_col, tag_col = code_row // 128, code_col // 128, code_col % 128
    same = tile_row == tile_col
    place_row = jnp.sum(jnp.where(same & (up < down), 1, 0), 0, keepdims=True)
    place_col = jnp.sum(jnp.where(same & (down < up), 1, 0), 1, keepdims=True)
    slot_row = tile_row * slots + place_row
    chooser = jnp.where(iota((tiles * slots, count), 0) == slot_row, 1.0, 0.0).astype(jnp.bfloat16)
    to_tile = jnp.where(iota((tiles, count), 0) == tile_row, 1.0, 0.0).astype(jnp.bfloat16)
    labels = jnp.where(
        iota((count, tiles * slots), 1) == me * slots + place_col,
        (tag_col + 1).astype(jnp.float32),
        0.0,
    ).astype(jnp.bfloat16)
    tags = jnp.dot(to_tile, labels, preferred_element_type=jnp.float32)
    out[:, F * slots :, :] = jnp.zeros((tiles, out.shape[1] - F * slots, 128), jnp.float32)
    for t in range(tiles):
        for part in range(tiles * slots // 128):
            out[t, F * slots + part : F * slots + part + 1, :] = tags[
                t : t + 1, part * 128 : (part + 1) * 128
            ]

    send = coupling[...] * (state[...] - surface[...]) * wet_of(ocean, mask[...])[None]
    row_of = iota((F * height, 128), 0) % height
    for c in range(cols):
        piece = send[:, :, c * 128 : (c + 1) * 128].reshape(F * height, 128)
        left = jnp.concatenate(
            [jnp.where(row_of == r, piece, 0.0).astype(jnp.bfloat16) for r in range(height)], 1
        )
        copies[c].wait()
        for k in range(K):
            right = w[c, :, k].reshape(height * 128, 128)
            made = jnp.dot(left, right, preferred_element_type=jnp.float32)
            at = (c * K + k) * height
            for f in range(F):
                terms[at : at + height, f * 128 : (f + 1) * 128] = made[
                    f * height : (f + 1) * height, :
                ]
    hi, lo = split(terms[...])
    packed = jnp.dot(
        jnp.concatenate([chooser, chooser], 1),
        jnp.concatenate([hi, lo], 0),
        preferred_element_type=jnp.float32,
    )
    for t in range(tiles):
        for f in range(F):
            out[t, f * slots : (f + 1) * slots, :] = packed[
                t * slots : (t + 1) * slots, f * 128 : (f + 1) * 128
            ]


def merge_kernel(tiles, slots, blocks, groups, got, *outs):
    ocean = lax.axis_index("grp") == groups - 1
    tags = got[0, F * slots :, :]
    for t in range(1, tiles):
        tags = tags + got[t, F * slots :, :]
    rows = (groups - 1) * blocks
    total = tiles * slots
    label = jnp.concatenate([tags[p : p + 1, :] for p in range(total // 128)], 1).astype(jnp.int32)
    ids = iota((rows, total), 0)
    ids = jnp.where(ocean, ids, ids % blocks) + 1
    chooser = jnp.where(ids == label, 1.0, 0.0).astype(jnp.bfloat16)
    for f in range(F):
        data = jnp.concatenate([got[t, f * slots : (f + 1) * slots, :] for t in range(tiles)], 0)
        hi, lo = split(data)
        merged = jnp.dot(chooser, hi, preferred_element_type=jnp.float32) + jnp.dot(
            chooser, lo, preferred_element_type=jnp.float32
        )
        for g in range(groups - 1):
            outs[g][f * blocks : (f + 1) * blocks, :] = merged[g * blocks : (g + 1) * blocks, :]


def edge_kernel(state, mask, top, bottom):
    levels, height, width = state.shape
    top[...] = jnp.zeros(top.shape, jnp.float32)
    bottom[...] = jnp.zeros(bottom.shape, jnp.float32)
    top[:levels, :] = state[:, 0, :]
    bottom[:levels, :] = state[:, height - 1, :]
    wet = wet_of(lax.axis_index("grp") == 3, mask[...])
    top[levels : levels + 1, :] = wet[:1]
    bottom[levels : levels + 1, :] = wet[height - 1 :]


def weights_of(tiles, groups, horiz, wet, wet_above, wet_below):
    height, width = wet.shape
    device = lax.axis_index("grp") * tiles + lax.axis_index("tile")
    rows = device * height + iota((height, width), 0)
    start = (groups - 1) * tiles * height
    last = groups * tiles * height - 1
    above = jnp.concatenate([wet_above, wet[:-1]], 0)
    below = jnp.concatenate([wet[1:], wet_below], 0)
    above = jnp.where((rows > 0) & (rows != start), above, 0.0)
    below = jnp.where((rows < last) & (rows + 1 != start), below, 0.0)
    column = iota((height, width), 1)
    left = jnp.where(column == 0, 0.0, pltpu.roll(wet, 1, 1))
    right = jnp.where(column == width - 1, 0.0, pltpu.roll(wet, width - 1, 1))
    scale = horiz * wet
    return scale * left, scale * right, scale * above, scale * below


def stencil(field, top, bottom, weights):
    left, right, above, below = weights
    height, width = field.shape
    return (
        field
        + left * (pltpu.roll(field, 1, 1) - field)
        + right * (pltpu.roll(field, width - 1, 1) - field)
        + above * (jnp.concatenate([top, field[:-1]], 0) - field)
        + below * (jnp.concatenate([field[1:], bottom], 0) - field)
    )


def base_kernel(
    tiles, groups, state, vert, horiz, mask, from_above, from_below, upper, gain, ratio, base, impulse, weights
):
    levels, height, width = state.shape
    wet = wet_of(lax.axis_index("grp") == groups - 1, mask[...])
    made = weights_of(
        tiles,
        groups,
        horiz[...],
        wet,
        from_above[levels : levels + 1, :],
        from_below[levels : levels + 1, :],
    )
    for i in range(4):
        weights[i] = made[i]
    zero = jnp.zeros((height, width), jnp.float32)

    def forward(level, carry, last=False, first=False):
        low, c, r, e = carry
        upp = zero if last else vert[level] * wet
        inverse = 1.0 / (1.0 + low + upp + low * c)
        c = -upp * inverse
        step = low * inverse
        field = stencil(
            state[level], from_above[pl.ds(level, 1), :], from_below[pl.ds(level, 1), :], made
        )
        r = field * inverse + step * r
        e = inverse if first else step * e
        upper[level] = c
        gain[level] = inverse
        ratio[level] = step
        base[level] = r
        impulse[level] = e
        return upp, c, r, e

    carry = forward(0, (zero, zero, zero, zero), first=True)
    carry = lax.fori_loop(1, levels - 1, forward, carry, unroll=2)
    _, _, r, e = forward(levels - 1, carry, last=True)

    def backward(i, carry):
        level = levels - 2 - i
        c = upper[level]
        x = base[level] - c * carry[0]
        y = impulse[level] - c * carry[1]
        base[level] = x
        impulse[level] = y
        return x, y

    lax.fori_loop(0, levels - 1, backward, (r, e), unroll=2)


def force_kernel(cols, base, impulse, mask, r0, r1, r2, field, received, force, top, bottom):
    levels, height, width = base.shape
    wet = wet_of(lax.axis_index("grp") == 3, mask[...])
    total = r0[...] + r1[...] + r2[...]
    for f in range(F):
        for c in range(cols):
            at = (f * cols + c) * height
            received[f, :, c * 128 : (c + 1) * 128] = total[at : at + height, :]
    forcing = FORCING_GAIN * wet * jnp.sum(received[...], 0)
    force[...] = forcing

    def one(level, _):
        x = base[level] + impulse[level] * forcing
        field[level] = x
        top[pl.ds(level, 1), :] = x[:1]
        bottom[pl.ds(level, 1), :] = x[height - 1 :]
        return 0

    lax.fori_loop(0, levels, one, 0, unroll=2)


def last_kernel(field, force, from_above, from_below, upper, gain, ratio, weights, out):
    levels, height, width = field.shape
    made = tuple(weights[i] for i in range(4))

    def forward(level, r, first=False):
        x = stencil(
            field[level], from_above[pl.ds(level, 1), :], from_below[pl.ds(level, 1), :], made
        )
        if first:
            x = x + force[...]
        r = x * gain[level] + ratio[level] * r
        out[level] = r
        return r

    r = forward(0, jnp.zeros((height, width), jnp.float32), first=True)
    r = lax.fori_loop(1, levels, forward, r, unroll=2)

    def backward(i, x):
        level = levels - 2 - i
        x = out[level] - upper[level] * x
        out[level] = x
        return x

    lax.fori_loop(0, levels - 1, backward, r, unroll=2)


def f32(*shape):
    return jax.ShapeDtypeStruct(shape, jnp.float32)


def local(
    state, vert_coef, horiz_coef, wet_mask, coupling, surface_in, remap_w, dest_tile, dest_block, dest_group
):
    levels, height, width = state.shape
    groups, tiles = lax.axis_size("grp"), lax.axis_size("tile")
    cols = width // 128
    blocks = height * cols
    slots = max(8, 2 * blocks * K // tiles)
    extra = -(-(tiles * slots // 128) // 8) * 8
    around = -(-(levels + 1) // 8) * 8
    devices = groups * tiles
    start = (groups - 1) * tiles
    pairs = [(i, i + 1) for i in range(devices - 1) if i + 1 != start]
    back = [(j, i) for i, j in pairs]
    axes = ("grp", "tile")

    top, bottom = pl.pallas_call(
        edge_kernel,
        out_shape=(f32(around, width), f32(around, width)),
        compiler_params=params(16),
    )(state, wet_mask)
    from_above = lax.ppermute(bottom, axes, pairs)
    from_below = lax.ppermute(top, axes, back)

    packed = pl.pallas_call(
        functools.partial(pack_kernel, tiles, slots),
        grid=(1,),
        out_shape=f32(tiles, F * slots + extra, 128),
        in_specs=[pl.BlockSpec((1, height, width), lambda i: (0, 0, 0))]
        + [VM] * 6
        + [pl.BlockSpec(memory_space=pl.ANY)],
        out_specs=VM,
        scratch_shapes=[
            pltpu.VMEM((cols, height, K, 128, 128), jnp.bfloat16),
            pltpu.VMEM((blocks * K, F * 128), jnp.float32),
            pltpu.SemaphoreType.DMA((cols,)),
        ],
        compiler_params=params(16),
    )(
        state,
        coupling,
        surface_in,
        wet_mask,
        dest_tile,
        dest_block,
        dest_group,
        remap_w.reshape(height, cols, K, 128, 128),
    )
    got = lax.all_to_all(packed, "tile", split_axis=0, concat_axis=0, tiled=True)

    full = f32(levels, height, width)
    upper, gain, ratio, base, impulse, weights = pl.pallas_call(
        functools.partial(base_kernel, tiles, groups),
        out_shape=(full, full, full, full, full, f32(4, height, width)),
        compiler_params=params(24),
        cost_estimate=pl.CostEstimate(flops=40 * state.size, bytes_accessed=28 * state.size, transcendentals=0),
    )(state, vert_coef, horiz_coef, wet_mask, from_above, from_below)

    merged = pl.pallas_call(
        functools.partial(merge_kernel, tiles, slots, blocks, groups),
        out_shape=(f32(F * blocks, 128),) * (groups - 1),
        compiler_params=params(8),
    )(got)
    arrived = [
        lax.ppermute(merged[g], "grp", [(g, groups - 1), (groups - 1, g)])
        for g in range(groups - 1)
    ]
    field, received, force, top, bottom = pl.pallas_call(
        functools.partial(force_kernel, cols),
        out_shape=(full, f32(F, height, width), f32(height, width), f32(levels, width), f32(levels, width)),
        compiler_params=params(16),
    )(base, impulse, wet_mask, *arrived)
    from_above = lax.ppermute(bottom, axes, pairs)
    from_below = lax.ppermute(top, axes, back)
    out = pl.pallas_call(
        last_kernel,
        out_shape=full,
        compiler_params=params(24),
    )(field, force, from_above, from_below, upper, gain, ratio, weights)
    return out, received


def solution(mesh):
    in_specs = (
        P(None, ("grp", "tile"), None),
        P(None, ("grp", "tile"), None),
        P(("grp", "tile"), None),
        P("tile", None),
        P(None, ("grp", "tile"), None),
        P(None, ("grp", "tile"), None),
        P(("grp", "tile"), None, None, None),
        P(("grp", "tile"), None),
        P(("grp", "tile"), None),
        P(("grp", "tile"), None),
    )
    out_specs = (P(None, ("grp", "tile"), None), P(None, ("grp", "tile"), None))
    return jax.shard_map(local, mesh=mesh, in_specs=in_specs, out_specs=out_specs, check_vma=False)
```

```python
import functools

import jax
import jax.numpy as jnp
from jax import lax
from jax.experimental import pallas as pl
from jax.experimental.pallas import tpu as pltpu
from jax.sharding import PartitionSpec as P

F = 4
K = 4
FORCING_GAIN = 0.25
VM = pl.BlockSpec(memory_space=pltpu.VMEM)
HBM = pl.BlockSpec(memory_space=pltpu.HBM)
MIB = 1024 * 1024


def params(mib):
    return pltpu.CompilerParams(vmem_limit_bytes=mib * MIB)


def split(x):
    hi = x.astype(jnp.bfloat16)
    return hi, (x - hi.astype(jnp.float32)).astype(jnp.bfloat16)


def wet_of(ocean, mask):
    return jnp.where(ocean, mask.astype(jnp.float32), 1.0)


def iota(shape, dim):
    return lax.broadcasted_iota(jnp.int32, shape, dim)


def pack_kernel(
    tiles, slots, groups, state, coupling, surface, mask, dtile, dblock, dgroup, w_hbm, *rest
):
    outs = rest[:tiles]
    w, terms, first, gain, other, sem, sems = rest[tiles:]
    height, width = mask.shape
    cols = width // 128
    blocks = height * cols
    count = blocks * K
    copies = [pltpu.make_async_copy(w_hbm.at[:, c], w.at[c], sem.at[c]) for c in range(cols)]
    small = [
        pltpu.make_async_copy(state.at[0], first, sems.at[0]),
        pltpu.make_async_copy(coupling, gain, sems.at[1]),
        pltpu.make_async_copy(surface, other, sems.at[2]),
    ]
    for copy in small + copies:
        copy.start()
    ocean = lax.axis_index("grp") == groups - 1
    me = lax.axis_index("tile")

    block = dblock[...]
    line = block // cols
    col = block % cols
    group = jnp.where(ocean, dgroup[...], groups - 1)
    code = dtile[...] * 128 + col * height + line + jnp.where(ocean, dgroup[...] * blocks, 0)
    device = group * tiles + dtile[...]
    low = jnp.where(ocean, 0, (groups - 1) * tiles)
    high = jnp.where(ocean, (groups - 1) * tiles, groups * tiles)
    beside = jnp.where(line == height - 1, device + 1, device - 1)
    side = jnp.where(line == height - 1, 0, 1)
    reads = ((line == height - 1) | (line == 0)) & (beside >= low) & (beside < high)
    edge = (beside % tiles) * 32 + side * cols + col
    edge = edge + jnp.where(ocean, (beside // tiles) * (2 * cols), 0)
    edge = jnp.where(reads, edge, -1)

    item = iota((count, blocks), 0)
    item_k = (item // height) % K
    own = iota((count, blocks), 1) == (item % height) * cols + item // (height * K)
    up, down = iota((count, count), 0), iota((count, count), 1)

    def column(values):
        spread = jnp.broadcast_to(values[:1, :], (count, blocks))
        for k in range(1, K):
            spread = jnp.where(item_k == k, values[k : k + 1, :], spread)
        return jnp.sum(jnp.where(own, spread, 0), 1, keepdims=True)

    def turned(values):
        return jnp.sum(jnp.where(up == down, values, 0), 0, keepdims=True)

    code_col, edge_row = column(code), turned(column(edge))
    code_row = turned(code_col)
    tile_row, tile_col, tag_col = code_row // 128, code_col // 128, code_col % 128
    same = tile_row == tile_col
    place_row = jnp.sum(jnp.where(same & (up < down), 1, 0), 0, keepdims=True)
    place_col = jnp.sum(jnp.where(same & (down < up), 1, 0), 1, keepdims=True)
    slot_row = (tile_row ^ me) * slots + place_row
    chooser = jnp.where(iota((tiles * slots, count), 0) == slot_row, 1.0, 0.0).astype(jnp.bfloat16)
    to_tile = jnp.where((iota((tiles, count), 0) ^ me) == tile_row, 1.0, 0.0).astype(jnp.bfloat16)
    labels = jnp.where(
        iota((count, tiles * slots), 1) == (tile_col ^ me) * slots + place_col,
        (tag_col + 1).astype(jnp.float32),
        0.0,
    ).astype(jnp.bfloat16)
    tags = jnp.dot(to_tile, labels, preferred_element_type=jnp.float32)
    rim = 2 * cols * (groups - 1)
    rim_id = iota((tiles * rim, count), 0)
    rim_tile, rim_id = (rim_id // rim) ^ me, rim_id % rim
    rim_id = rim_tile * 32 + jnp.where(ocean, rim_id, rim_id % (2 * cols))
    rim_chooser = jnp.where(rim_id == edge_row, 1.0, 0.0).astype(jnp.bfloat16)
    base = F * slots + rim
    parts = tiles * slots // 128
    for t in range(tiles):
        outs[t][base:, :] = jnp.zeros((outs[t].shape[0] - base, 128), jnp.float32)
        for part in range(parts):
            outs[t][base + part : base + part + 1, :] = tags[
                t : t + 1, part * 128 : (part + 1) * 128
            ]

    for copy in small:
        copy.wait()
    send = gain[...] * (first[...][None] - other[...]) * wet_of(ocean, mask[...])[None]
    row_of = iota((F * height, 128), 0) % height
    for c in range(cols):
        piece = send[:, :, c * 128 : (c + 1) * 128].reshape(F * height, 128)
        left = jnp.concatenate(
            [jnp.where(row_of == r, piece, 0.0).astype(jnp.bfloat16) for r in range(height)], 1
        )
        copies[c].wait()
        for k in range(K):
            right = w[c, :, k].reshape(height * 128, 128)
            made = jnp.dot(left, right, preferred_element_type=jnp.float32)
            at = (c * K + k) * height
            for f in range(F):
                terms[at : at + height, f * 128 : (f + 1) * 128] = made[
                    f * height : (f + 1) * height, :
                ]
    total = terms[:, :128]
    for f in range(1, F):
        total = total + terms[:, f * 128 : (f + 1) * 128]
    hi, lo = split(terms[...])
    packed = jnp.dot(
        jnp.concatenate([chooser, chooser], 1),
        jnp.concatenate([hi, lo], 0),
        preferred_element_type=jnp.float32,
    )
    hi, lo = split(total)
    rims = jnp.dot(
        jnp.concatenate([rim_chooser, rim_chooser], 1),
        jnp.concatenate([hi, lo], 0),
        preferred_element_type=jnp.float32,
    )
    for t in range(tiles):
        for f in range(F):
            outs[t][f * slots : (f + 1) * slots, :] = packed[
                t * slots : (t + 1) * slots, f * 128 : (f + 1) * 128
            ]
        outs[t][F * slots : base, :] = rims[t * rim : (t + 1) * rim, :]


def merge_kernel(tiles, slots, blocks, groups, _, *refs):
    got, outs = refs[:tiles], refs[tiles:]
    ocean = lax.axis_index("grp") == groups - 1
    rim = outs[0].shape[0] - F * blocks
    base = F * slots + rim * (groups - 1)
    tail = got[0][F * slots :, :]
    for t in range(1, tiles):
        tail = tail + got[t][F * slots :, :]
    tags = tail[base - F * slots :, :]
    rows = (groups - 1) * blocks
    total = tiles * slots
    label = jnp.concatenate([tags[p : p + 1, :] for p in range(total // 128)], 1).astype(jnp.int32)
    ids = iota((rows, total), 0)
    ids = jnp.where(ocean, ids, ids % blocks) + 1
    chooser = jnp.where(ids == label, 1.0, 0.0).astype(jnp.bfloat16)
    for f in range(F):
        data = jnp.concatenate([got[t][f * slots : (f + 1) * slots, :] for t in range(tiles)], 0)
        hi, lo = split(data)
        merged = jnp.dot(chooser, hi, preferred_element_type=jnp.float32) + jnp.dot(
            chooser, lo, preferred_element_type=jnp.float32
        )
        for g in range(groups - 1):
            outs[g][f * blocks : (f + 1) * blocks, :] = merged[g * blocks : (g + 1) * blocks, :]
    for g in range(groups - 1):
        outs[g][F * blocks :, :] = tail[g * rim : (g + 1) * rim, :]


def edge_kernel(groups, state_hbm, vert_hbm, horiz, mask, down, up, state, vert, sem):
    levels, height, width = state.shape
    half = levels // 2
    copies = [
        pltpu.make_async_copy(state_hbm, state, sem.at[0]),
        pltpu.make_async_copy(vert_hbm, vert, sem.at[1]),
    ]
    for copy in copies:
        copy.start()
    wet = wet_of(lax.axis_index("grp") == groups - 1, mask[...])
    cols = width // 128
    last = height - 1
    for c in range(cols):
        at = slice(c * 128, (c + 1) * 128)
        down[levels + half, c : c + 1, :] = wet[last:, at]
        down[levels + half, cols + c : cols + c + 1, :] = wet[last - 1 : last, at]
        up[levels + half, c : c + 1, :] = wet[1:2, at]
        up[levels + half, cols + c : cols + c + 1, :] = wet[:1, at]
        for out, row in ((down, last), (up, 0)):
            out[levels + half + 1, c : c + 1, :] = horiz[row : row + 1, at]
            out[levels + half + 1, cols + c : cols + c + 1, :] = horiz[row : row + 1, at]
    copies[0].wait()
    for c in range(cols):
        at = slice(c * 128, (c + 1) * 128)
        down[:levels, c, :] = state[:, last, at]
        down[:levels, cols + c, :] = state[:, last - 1, at]
        up[:levels, c, :] = state[:, 1, at]
        up[:levels, cols + c, :] = state[:, 0, at]
    copies[1].wait()
    for c in range(cols):
        at = slice(c * 128, (c + 1) * 128)
        for out, row in ((down, last), (up, 0)):
            out[levels : levels + half, c, :] = vert[:half, row, at]
            out[levels : levels + half - 1, cols + c, :] = vert[half:, row, at]
            out[levels + half - 1, cols + c : cols + c + 1, :] = jnp.zeros((1, 128), jnp.float32)


def weights_of(tiles, groups, horiz, wet, wet_above, wet_below):
    height, width = wet.shape
    device = lax.axis_index("grp") * tiles + lax.axis_index("tile")
    rows = device * height + iota((height, width), 0)
    start = (groups - 1) * tiles * height
    last = groups * tiles * height - 1
    above = jnp.concatenate([wet_above, wet[:-1]], 0)
    below = jnp.concatenate([wet[1:], wet_below], 0)
    above = jnp.where((rows > 0) & (rows != start), above, 0.0)
    below = jnp.where((rows < last) & (rows + 1 != start), below, 0.0)
    column = iota((height, width), 1)
    left = jnp.where(column == 0, 0.0, pltpu.roll(wet, 1, 1))
    right = jnp.where(column == width - 1, 0.0, pltpu.roll(wet, width - 1, 1))
    scale = horiz * wet
    return scale * left, scale * right, scale * above, scale * below


def line_of(halo, first, cols):
    return jnp.concatenate([halo[first + c : first + c + 1, :] for c in range(cols)], 1)


def stencil(field, halo, weights):
    left, right, above, below = weights
    height, width = field.shape
    cols = width // 128
    top, bottom = line_of(halo, 0, cols), line_of(halo, cols, cols)
    return (
        field
        + left * (pltpu.roll(field, 1, 1) - field)
        + right * (pltpu.roll(field, width - 1, 1) - field)
        + above * (jnp.concatenate([top, field[:-1]], 0) - field)
        + below * (jnp.concatenate([field[1:], bottom], 0) - field)
    )


def shifted(halo, lane):
    rows = halo.shape[0]
    to_right, to_left = pltpu.roll(halo, 1, 1), pltpu.roll(halo, 127, 1)
    return (
        jnp.where(lane == 0, pltpu.roll(to_right, 1, 0), to_right),
        jnp.where(lane == 127, pltpu.roll(to_left, rows - 1, 0), to_left),
    )


def base_kernel(
    tiles, groups, state, vert, horiz, mask, down, up, above, below,
    upper, gain, ratio, base, impulse, weights, halo_base, halo_impulse, halo_wet, halo_vert, halo_upper,
):
    levels, height, width = state.shape
    cols = width // 128
    half = levels // 2
    shape = (2 * cols, 128)
    low_half = iota(shape, 0) < cols
    lane = iota(shape, 1)

    def turn(x):
        return pltpu.roll(x, cols, 0)

    def beside(i):
        return jnp.where(low_half, above[i], below[i])

    def behind(i):
        return turn(jnp.where(low_half, below[i], above[i]))

    def inside(i):
        return turn(jnp.where(low_half, down[i], up[i]))

    wet = wet_of(lax.axis_index("grp") == groups - 1, mask[...])
    wet_halo = beside(levels + half)
    halo_wet[...] = wet_halo
    made = weights_of(
        tiles, groups, horiz[...], wet, line_of(wet_halo, 0, cols), line_of(wet_halo, cols, cols)
    )
    for i in range(4):
        weights[i] = made[i]
    scale = beside(levels + half + 1) * wet_halo
    wet_left, wet_right = shifted(wet_halo, lane)
    place = iota(shape, 0) % cols
    weight_left = scale * jnp.where((place == 0) & (lane == 0), 0.0, wet_left)
    weight_right = scale * jnp.where((place == cols - 1) & (lane == 127), 0.0, wet_right)
    weight_behind = scale * behind(levels + half)
    weight_inside = scale * inside(levels + half)

    def spread(i, _):
        a, b = above[levels + i], below[levels + i]
        halo_vert[i] = jnp.where(low_half, a, turn(b)) * wet_halo
        halo_vert[half + i] = jnp.where(low_half, turn(a), b) * wet_halo
        return 0

    lax.fori_loop(0, half, spread, 0, unroll=4)
    zero = jnp.zeros((height, width), jnp.float32)
    zero_halo = jnp.zeros(shape, jnp.float32)

    def forward(level, carry, last=False, first=False):
        low, c, r, e, low_h, c_h, r_h, e_h = carry
        upp = zero if last else vert[level] * wet
        inverse = 1.0 / (1.0 + low + upp + low * c)
        c = -upp * inverse
        step = low * inverse
        halo = beside(level)
        r = stencil(state[level], halo, made) * inverse + step * r
        e = inverse if first else step * e
        upper[level] = c
        gain[level] = inverse
        ratio[level] = step
        base[level] = r
        impulse[level] = e
        upp_h = zero_halo if last else halo_vert[level]
        inverse = 1.0 / (1.0 + low_h + upp_h + low_h * c_h)
        c_h = -upp_h * inverse
        step = low_h * inverse
        left, right = shifted(halo, lane)
        field = (
            halo
            + weight_left * (left - halo)
            + weight_right * (right - halo)
            + weight_behind * (behind(level) - halo)
            + weight_inside * (inside(level) - halo)
        )
        r_h = field * inverse + step * r_h
        e_h = inverse if first else step * e_h
        halo_upper[level] = c_h
        halo_base[level] = r_h
        halo_impulse[level] = e_h
        return upp, c, r, e, upp_h, c_h, r_h, e_h

    carry = forward(0, (zero,) * 4 + (zero_halo,) * 4, first=True)
    carry = lax.fori_loop(1, levels - 1, forward, carry, unroll=2)
    carry = forward(levels - 1, carry, last=True)

    def backward(i, carry):
        level = levels - 2 - i
        c, c_h = upper[level], halo_upper[level]
        x = base[level] - c * carry[0]
        y = impulse[level] - c * carry[1]
        x_h = halo_base[level] - c_h * carry[2]
        y_h = halo_impulse[level] - c_h * carry[3]
        base[level] = x
        impulse[level] = y
        halo_base[level] = x_h
        halo_impulse[level] = y_h
        return x, y, x_h, y_h

    lax.fori_loop(0, levels - 1, backward, (carry[2], carry[3], carry[6], carry[7]), unroll=2)


def last_kernel(
    cols, groups, mask, base, impulse, upper, gain, ratio, weights, halo_base, halo_impulse, halo_wet, *refs
):
    arrived = refs[: groups - 1]
    out, received, field, sem = refs[groups - 1 :]
    levels, height, width = base.shape
    total = arrived[0][...]
    for other in arrived[1:]:
        total = total + other[...]
    for f in range(F):
        for c in range(cols):
            at = (f * cols + c) * height
            received[f, :, c * 128 : (c + 1) * 128] = total[at : at + height, :]
    wet = wet_of(lax.axis_index("grp") == groups - 1, mask[...])
    force = FORCING_GAIN * wet * jnp.sum(received[...], 0)
    force_halo = FORCING_GAIN * halo_wet[...] * total[F * cols * height :, :]
    made = tuple(weights[i] for i in range(4))

    def forward(level, r, first=False):
        halo = halo_base[level] + halo_impulse[level] * force_halo
        x = stencil(base[level] + impulse[level] * force, halo, made)
        if first:
            x = x + force
        r = x * gain[level] + ratio[level] * r
        field[level] = r
        return r

    r = forward(0, jnp.zeros((height, width), jnp.float32), first=True)
    x = lax.fori_loop(1, levels, forward, r, unroll=2)

    def backward(i, x):
        level = levels - 2 - i
        x = field[level] - upper[level] * x
        field[level] = x
        return x

    chunks = 4
    size = levels // chunks
    copies = []
    for i in range(chunks):
        x = lax.fori_loop(max(0, i * size - 1), (i + 1) * size - 1, backward, x, unroll=3 if i == 0 else 2)
        at = pl.ds(levels - (i + 1) * size, size)
        copies.append(pltpu.make_async_copy(field.at[at], out.at[at], sem.at[i]))
        copies[-1].start()
    for copy in copies:
        copy.wait()


def f32(*shape):
    return jax.ShapeDtypeStruct(shape, jnp.float32)


def local(
    state, vert_coef, horiz_coef, wet_mask, coupling, surface_in, remap_w, dest_tile, dest_block, dest_group
):
    levels, height, width = state.shape
    groups, tiles = lax.axis_size("grp"), lax.axis_size("tile")
    cols = width // 128
    blocks = height * cols
    slots = max(8, 2 * blocks * K // tiles)
    rim = 2 * cols
    tags = -(-(tiles * slots // 128) // 8) * 8
    devices = groups * tiles
    start = (groups - 1) * tiles
    pairs = [(i, i + 1) for i in range(devices - 1) if i + 1 != start]
    back = [(j, i) for i, j in pairs]
    axes = ("grp", "tile")

    edges = levels + levels // 2 + 2
    down, up = pl.pallas_call(
        functools.partial(edge_kernel, groups),
        out_shape=(f32(edges, rim, 128),) * 2,
        in_specs=[HBM, HBM, VM, VM],
        scratch_shapes=[
            pltpu.VMEM((levels, height, width), jnp.float32),
            pltpu.VMEM((levels - 1, height, width), jnp.float32),
            pltpu.SemaphoreType.DMA((2,)),
        ],
        compiler_params=params(8),
    )(state, vert_coef, horiz_coef, wet_mask)
    above = lax.ppermute(down, axes, pairs)
    below = lax.ppermute(up, axes, back)

    packed = pl.pallas_call(
        functools.partial(pack_kernel, tiles, slots, groups),
        out_shape=(f32(F * slots + rim * (groups - 1) + tags, 128),) * tiles,
        in_specs=[HBM] * 3 + [VM] * 4 + [HBM],
        scratch_shapes=[
            pltpu.VMEM((cols, height, K, 128, 128), jnp.bfloat16),
            pltpu.VMEM((blocks * K, F * 128), jnp.float32),
            pltpu.VMEM((height, width), jnp.float32),
            pltpu.VMEM((F, height, width), jnp.float32),
            pltpu.VMEM((F, height, width), jnp.float32),
            pltpu.SemaphoreType.DMA((cols,)),
            pltpu.SemaphoreType.DMA((3,)),
        ],
        compiler_params=params(12),
    )(
        state,
        coupling,
        surface_in,
        wet_mask,
        dest_tile.T,
        dest_block.T,
        dest_group.T,
        remap_w.reshape(height, cols, K, 128, 128),
    )
    got = [packed[0]] + [
        lax.ppermute(packed[k], "tile", [(i, i ^ k) for i in range(tiles)])
        for k in range(tiles - 1, 0, -1)
    ][::-1]

    full, halo = f32(levels, height, width), f32(levels, rim, 128)
    solved = pl.pallas_call(
        functools.partial(base_kernel, tiles, groups),
        out_shape=(full,) * 5 + (f32(4, height, width), halo, halo, f32(rim, 128)),
        scratch_shapes=[pltpu.VMEM((levels, rim, 128), jnp.float32)] * 2,
        compiler_params=params(16),
        cost_estimate=pl.CostEstimate(flops=60 * state.size, bytes_accessed=28 * state.size, transcendentals=0),
    )(state, vert_coef, horiz_coef, wet_mask, down, up, above, below)
    upper, gain, ratio, base, impulse, weights, halo_base, halo_impulse, halo_wet = solved

    merged = pl.pallas_call(
        functools.partial(merge_kernel, tiles, slots, blocks, groups),
        out_shape=(f32(F * blocks + rim, 128),) * (groups - 1),
        compiler_params=params(8),
    )(halo_wet, *got)
    arrived = [
        lax.ppermute(merged[g], "grp", [(g, groups - 1), (groups - 1, g)])
        for g in range(groups - 1)
    ]
    return pl.pallas_call(
        functools.partial(last_kernel, cols, groups),
        out_shape=(full, f32(F, height, width)),
        out_specs=(HBM, VM),
        scratch_shapes=[
            pltpu.VMEM((levels, height, width), jnp.float32),
            pltpu.SemaphoreType.DMA((4,)),
        ],
        compiler_params=params(16),
    )(
        wet_mask, base, impulse, upper, gain, ratio, weights, halo_base, halo_impulse, halo_wet, *arrived
    )


def solution(mesh):
    in_specs = (
        P(None, ("grp", "tile"), None),
        P(None, ("grp", "tile"), None),
        P(("grp", "tile"), None),
        P("tile", None),
        P(None, ("grp", "tile"), None),
        P(None, ("grp", "tile"), None),
        P(("grp", "tile"), None, None, None),
        P(("grp", "tile"), None),
        P(("grp", "tile"), None),
        P(("grp", "tile"), None),
    )
    out_specs = (P(None, ("grp", "tile"), None), P(None, ("grp", "tile"), None))
    return jax.shard_map(local, mesh=mesh, in_specs=in_specs, out_specs=out_specs, check_vma=False)
```

```python
import functools

import jax
import jax.numpy as jnp
from jax import lax
from jax.experimental import pallas as pl
from jax.experimental.pallas import tpu as pltpu
from jax.sharding import PartitionSpec as P

F = 4
K = 4
FORCING_GAIN = 0.25
VM = pl.BlockSpec(memory_space=pltpu.VMEM)
HBM = pl.BlockSpec(memory_space=pltpu.HBM)
MIB = 1024 * 1024


def params(mib):
    return pltpu.CompilerParams(vmem_limit_bytes=mib * MIB)


def split(x):
    hi = x.astype(jnp.bfloat16)
    return hi, (x - hi.astype(jnp.float32)).astype(jnp.bfloat16)


def wet_of(ocean, mask):
    return jnp.where(ocean, mask.astype(jnp.float32), 1.0)


def iota(shape, dim):
    return lax.broadcasted_iota(jnp.int32, shape, dim)


def pack_kernel(
    tiles, slots, groups, state, coupling, surface, mask, dtile, dblock, dgroup, w_hbm, *rest
):
    outs = rest[:tiles]
    w, terms, first, gain, other, sem, sems = rest[tiles:]
    height, width = mask.shape
    cols = width // 128
    blocks = height * cols
    count = blocks * K
    copies = [pltpu.make_async_copy(w_hbm.at[:, c], w.at[c], sem.at[c]) for c in range(cols)]
    small = [
        pltpu.make_async_copy(state.at[0], first, sems.at[0]),
        pltpu.make_async_copy(coupling, gain, sems.at[1]),
        pltpu.make_async_copy(surface, other, sems.at[2]),
    ]
    for copy in small + copies:
        copy.start()
    ocean = lax.axis_index("grp") == groups - 1
    me = lax.axis_index("tile")

    block = dblock[...]
    line = block // cols
    col = block % cols
    group = jnp.where(ocean, dgroup[...], groups - 1)
    code = dtile[...] * 128 + col * height + line + jnp.where(ocean, dgroup[...] * blocks, 0)
    device = group * tiles + dtile[...]
    low = jnp.where(ocean, 0, (groups - 1) * tiles)
    high = jnp.where(ocean, (groups - 1) * tiles, groups * tiles)
    beside = jnp.where(line == height - 1, device + 1, device - 1)
    side = jnp.where(line == height - 1, 0, 1)
    reads = ((line == height - 1) | (line == 0)) & (beside >= low) & (beside < high)
    edge = (beside % tiles) * 32 + side * cols + col
    edge = edge + jnp.where(ocean, (beside // tiles) * (2 * cols), 0)
    edge = jnp.where(reads, edge, -1)

    item = iota((count, blocks), 0)
    item_k = (item // height) % K
    own = iota((count, blocks), 1) == (item % height) * cols + item // (height * K)
    up, down = iota((count, count), 0), iota((count, count), 1)

    def column(values):
        spread = jnp.broadcast_to(values[:1, :], (count, blocks))
        for k in range(1, K):
            spread = jnp.where(item_k == k, values[k : k + 1, :], spread)
        return jnp.sum(jnp.where(own, spread, 0), 1, keepdims=True)

    def turned(values):
        return jnp.sum(jnp.where(up == down, values, 0), 0, keepdims=True)

    code_col, edge_row = column(code), turned(column(edge))
    code_row = turned(code_col)
    tile_row, tile_col, tag_col = code_row // 128, code_col // 128, code_col % 128
    same = tile_row == tile_col
    place_row = jnp.sum(jnp.where(same & (up < down), 1, 0), 0, keepdims=True)
    place_col = jnp.sum(jnp.where(same & (down < up), 1, 0), 1, keepdims=True)
    slot_row = (tile_row ^ me) * slots + place_row
    chooser = jnp.where(iota((tiles * slots, count), 0) == slot_row, 1.0, 0.0).astype(jnp.bfloat16)
    to_tile = jnp.where((iota((tiles, count), 0) ^ me) == tile_row, 1.0, 0.0).astype(jnp.bfloat16)
    labels = jnp.where(
        iota((count, tiles * slots), 1) == (tile_col ^ me) * slots + place_col,
        (tag_col + 1).astype(jnp.float32),
        0.0,
    ).astype(jnp.bfloat16)
    tags = jnp.dot(to_tile, labels, preferred_element_type=jnp.float32)
    rim = 2 * cols * (groups - 1)
    rim_id = iota((tiles * rim, count), 0)
    rim_tile, rim_id = (rim_id // rim) ^ me, rim_id % rim
    rim_id = rim_tile * 32 + jnp.where(ocean, rim_id, rim_id % (2 * cols))
    rim_chooser = jnp.where(rim_id == edge_row, 1.0, 0.0).astype(jnp.bfloat16)
    base = F * slots + rim
    parts = tiles * slots // 128
    for t in range(tiles):
        outs[t][base:, :] = jnp.zeros((outs[t].shape[0] - base, 128), jnp.float32)
        for part in range(parts):
            outs[t][base + part : base + part + 1, :] = tags[
                t : t + 1, part * 128 : (part + 1) * 128
            ]

    for copy in small:
        copy.wait()
    send = gain[...] * (first[...][None] - other[...]) * wet_of(ocean, mask[...])[None]
    row_of = iota((F * height, 128), 0) % height
    for c in range(cols):
        piece = send[:, :, c * 128 : (c + 1) * 128].reshape(F * height, 128)
        left = jnp.concatenate(
            [jnp.where(row_of == r, piece, 0.0).astype(jnp.bfloat16) for r in range(height)], 1
        )
        copies[c].wait()
        for k in range(K):
            right = w[c, :, k].reshape(height * 128, 128)
            made = jnp.dot(left, right, preferred_element_type=jnp.float32)
            at = (c * K + k) * height
            for f in range(F):
                terms[at : at + height, f * 128 : (f + 1) * 128] = made[
                    f * height : (f + 1) * height, :
                ]
    total = terms[:, :128]
    for f in range(1, F):
        total = total + terms[:, f * 128 : (f + 1) * 128]
    hi, lo = split(terms[...])
    packed = jnp.dot(
        jnp.concatenate([chooser, chooser], 1),
        jnp.concatenate([hi, lo], 0),
        preferred_element_type=jnp.float32,
    )
    hi, lo = split(total)
    rims = jnp.dot(
        jnp.concatenate([rim_chooser, rim_chooser], 1),
        jnp.concatenate([hi, lo], 0),
        preferred_element_type=jnp.float32,
    )
    for t in range(tiles):
        for f in range(F):
            outs[t][f * slots : (f + 1) * slots, :] = packed[
                t * slots : (t + 1) * slots, f * 128 : (f + 1) * 128
            ]
        outs[t][F * slots : base, :] = rims[t * rim : (t + 1) * rim, :]


def merge_kernel(tiles, slots, blocks, groups, _, *refs):
    got, outs = refs[:tiles], refs[tiles:]
    ocean = lax.axis_index("grp") == groups - 1
    rim = outs[0].shape[0] - F * blocks
    base = F * slots + rim * (groups - 1)
    tail = got[0][F * slots :, :]
    for t in range(1, tiles):
        tail = tail + got[t][F * slots :, :]
    tags = tail[base - F * slots :, :]
    rows = (groups - 1) * blocks
    total = tiles * slots
    label = jnp.concatenate([tags[p : p + 1, :] for p in range(total // 128)], 1).astype(jnp.int32)
    ids = iota((rows, total), 0)
    ids = jnp.where(ocean, ids, ids % blocks) + 1
    chooser = jnp.where(ids == label, 1.0, 0.0).astype(jnp.bfloat16)
    for f in range(F):
        data = jnp.concatenate([got[t][f * slots : (f + 1) * slots, :] for t in range(tiles)], 0)
        hi, lo = split(data)
        merged = jnp.dot(chooser, hi, preferred_element_type=jnp.float32) + jnp.dot(
            chooser, lo, preferred_element_type=jnp.float32
        )
        for g in range(groups - 1):
            outs[g][f * blocks : (f + 1) * blocks, :] = merged[g * blocks : (g + 1) * blocks, :]
    for g in range(groups - 1):
        outs[g][F * blocks :, :] = tail[g * rim : (g + 1) * rim, :]


def edge_kernel(groups, state_hbm, vert_hbm, horiz, mask, down, up, state, vert, sem):
    levels, height, width = state.shape
    half = levels // 2
    copies = [
        pltpu.make_async_copy(state_hbm, state, sem.at[0]),
        pltpu.make_async_copy(vert_hbm, vert, sem.at[1]),
    ]
    for copy in copies:
        copy.start()
    wet = wet_of(lax.axis_index("grp") == groups - 1, mask[...])
    cols = width // 128
    last = height - 1
    for c in range(cols):
        at = slice(c * 128, (c + 1) * 128)
        down[levels + half, c : c + 1, :] = wet[last:, at]
        down[levels + half, cols + c : cols + c + 1, :] = wet[last - 1 : last, at]
        up[levels + half, c : c + 1, :] = wet[1:2, at]
        up[levels + half, cols + c : cols + c + 1, :] = wet[:1, at]
        for out, row in ((down, last), (up, 0)):
            out[levels + half + 1, c : c + 1, :] = horiz[row : row + 1, at]
            out[levels + half + 1, cols + c : cols + c + 1, :] = horiz[row : row + 1, at]
    copies[0].wait()
    for c in range(cols):
        at = slice(c * 128, (c + 1) * 128)
        down[:levels, c, :] = state[:, last, at]
        down[:levels, cols + c, :] = state[:, last - 1, at]
        up[:levels, c, :] = state[:, 1, at]
        up[:levels, cols + c, :] = state[:, 0, at]
    copies[1].wait()
    for c in range(cols):
        at = slice(c * 128, (c + 1) * 128)
        for out, row in ((down, last), (up, 0)):
            out[levels : levels + half, c, :] = vert[:half, row, at]
            out[levels : levels + half - 1, cols + c, :] = vert[half:, row, at]
            out[levels + half - 1, cols + c : cols + c + 1, :] = jnp.zeros((1, 128), jnp.float32)


def weights_of(tiles, groups, horiz, wet, wet_above, wet_below):
    height, width = wet.shape
    device = lax.axis_index("grp") * tiles + lax.axis_index("tile")
    rows = device * height + iota((height, width), 0)
    start = (groups - 1) * tiles * height
    last = groups * tiles * height - 1
    above = jnp.concatenate([wet_above, wet[:-1]], 0)
    below = jnp.concatenate([wet[1:], wet_below], 0)
    above = jnp.where((rows > 0) & (rows != start), above, 0.0)
    below = jnp.where((rows < last) & (rows + 1 != start), below, 0.0)
    column = iota((height, width), 1)
    left = jnp.where(column == 0, 0.0, pltpu.roll(wet, 1, 1))
    right = jnp.where(column == width - 1, 0.0, pltpu.roll(wet, width - 1, 1))
    scale = horiz * wet
    return scale * left, scale * right, scale * above, scale * below


def line_of(halo, first, cols):
    return jnp.concatenate([halo[first + c : first + c + 1, :] for c in range(cols)], 1)


def stencil(field, halo, weights):
    left, right, above, below = weights
    height, width = field.shape
    cols = width // 128
    top, bottom = line_of(halo, 0, cols), line_of(halo, cols, cols)
    return (
        field
        + left * (pltpu.roll(field, 1, 1) - field)
        + right * (pltpu.roll(field, width - 1, 1) - field)
        + above * (jnp.concatenate([top, field[:-1]], 0) - field)
        + below * (jnp.concatenate([field[1:], bottom], 0) - field)
    )


def shifted(halo, lane):
    rows = halo.shape[0]
    to_right, to_left = pltpu.roll(halo, 1, 1), pltpu.roll(halo, 127, 1)
    return (
        jnp.where(lane == 0, pltpu.roll(to_right, 1, 0), to_right),
        jnp.where(lane == 127, pltpu.roll(to_left, rows - 1, 0), to_left),
    )


def base_kernel(
    tiles, groups, state, vert, horiz, mask, down, up, above, below,
    upper, gain, ratio, base, impulse, weights, halo_base, halo_impulse, halo_wet, halo_vert, halo_upper,
):
    levels, height, width = state.shape
    cols = width // 128
    half = levels // 2
    shape = (2 * cols, 128)
    low_half = iota(shape, 0) < cols
    lane = iota(shape, 1)

    def turn(x):
        return pltpu.roll(x, cols, 0)

    def beside(i):
        return jnp.where(low_half, above[i], below[i])

    def behind(i):
        return turn(jnp.where(low_half, below[i], above[i]))

    def inside(i):
        return turn(jnp.where(low_half, down[i], up[i]))

    wet = wet_of(lax.axis_index("grp") == groups - 1, mask[...])
    wet_halo = beside(levels + half)
    halo_wet[...] = wet_halo
    made = weights_of(
        tiles, groups, horiz[...], wet, line_of(wet_halo, 0, cols), line_of(wet_halo, cols, cols)
    )
    for i in range(4):
        weights[i] = made[i]
    scale = beside(levels + half + 1) * wet_halo
    wet_left, wet_right = shifted(wet_halo, lane)
    place = iota(shape, 0) % cols
    weight_left = scale * jnp.where((place == 0) & (lane == 0), 0.0, wet_left)
    weight_right = scale * jnp.where((place == cols - 1) & (lane == 127), 0.0, wet_right)
    weight_behind = scale * behind(levels + half)
    weight_inside = scale * inside(levels + half)

    def spread(i, _):
        a, b = above[levels + i], below[levels + i]
        halo_vert[i] = jnp.where(low_half, a, turn(b)) * wet_halo
        halo_vert[half + i] = jnp.where(low_half, turn(a), b) * wet_halo
        return 0

    lax.fori_loop(0, half, spread, 0, unroll=4)
    zero = jnp.zeros((height, width), jnp.float32)
    zero_halo = jnp.zeros(shape, jnp.float32)

    def forward(level, carry, last=False, first=False):
        low, c, r, e, low_h, c_h, r_h, e_h = carry
        upp = zero if last else vert[level] * wet
        inverse = 1.0 / (1.0 + low + upp + low * c)
        c = -upp * inverse
        step = low * inverse
        halo = beside(level)
        r = stencil(state[level], halo, made) * inverse + step * r
        e = inverse if first else step * e
        upper[level] = c
        gain[level] = inverse
        ratio[level] = step
        base[level] = r
        impulse[level] = e
        upp_h = zero_halo if last else halo_vert[level]
        inverse = 1.0 / (1.0 + low_h + upp_h + low_h * c_h)
        c_h = -upp_h * inverse
        step = low_h * inverse
        left, right = shifted(halo, lane)
        field = (
            halo
            + weight_left * (left - halo)
            + weight_right * (right - halo)
            + weight_behind * (behind(level) - halo)
            + weight_inside * (inside(level) - halo)
        )
        r_h = field * inverse + step * r_h
        e_h = inverse if first else step * e_h
        halo_upper[level] = c_h
        halo_base[level] = r_h
        halo_impulse[level] = e_h
        return upp, c, r, e, upp_h, c_h, r_h, e_h

    carry = forward(0, (zero,) * 4 + (zero_halo,) * 4, first=True)
    carry = lax.fori_loop(1, levels - 1, forward, carry, unroll=2)
    carry = forward(levels - 1, carry, last=True)

    def backward(i, carry):
        level = levels - 2 - i
        c, c_h = upper[level], halo_upper[level]
        x = base[level] - c * carry[0]
        y = impulse[level] - c * carry[1]
        x_h = halo_base[level] - c_h * carry[2]
        y_h = halo_impulse[level] - c_h * carry[3]
        base[level] = x
        impulse[level] = y
        halo_base[level] = x_h
        halo_impulse[level] = y_h
        return x, y, x_h, y_h

    lax.fori_loop(0, levels - 1, backward, (carry[2], carry[3], carry[6], carry[7]), unroll=2)


def last_kernel(
    cols, groups, mask, base, impulse, upper, gain, ratio, weights, halo_base, halo_impulse, halo_wet, *refs
):
    arrived = refs[: groups - 1]
    out, received, field, sem = refs[groups - 1 :]
    levels, height, width = base.shape
    total = arrived[0][...]
    for other in arrived[1:]:
        total = total + other[...]
    for f in range(F):
        for c in range(cols):
            at = (f * cols + c) * height
            received[f, :, c * 128 : (c + 1) * 128] = total[at : at + height, :]
    wet = wet_of(lax.axis_index("grp") == groups - 1, mask[...])
    force = FORCING_GAIN * wet * jnp.sum(received[...], 0)
    force_halo = FORCING_GAIN * halo_wet[...] * total[F * cols * height :, :]
    made = tuple(weights[i] for i in range(4))

    def forward(level, r, first=False):
        halo = halo_base[level] + halo_impulse[level] * force_halo
        x = stencil(base[level] + impulse[level] * force, halo, made)
        if first:
            x = x + force
        r = x * gain[level] + ratio[level] * r
        field[level] = r
        return r

    r = forward(0, jnp.zeros((height, width), jnp.float32), first=True)
    x = lax.fori_loop(1, levels, forward, r, unroll=2)

    def backward(i, x):
        level = levels - 2 - i
        x = field[level] - upper[level] * x
        field[level] = x
        return x

    chunks = 4
    size = levels // chunks
    copies = []
    for i in range(chunks):
        x = lax.fori_loop(max(0, i * size - 1), (i + 1) * size - 1, backward, x, unroll=3 if i == 0 else 2)
        at = pl.ds(levels - (i + 1) * size, size)
        copies.append(pltpu.make_async_copy(field.at[at], out.at[at], sem.at[i]))
        copies[-1].start()
    for copy in copies:
        copy.wait()


def f32(*shape):
    return jax.ShapeDtypeStruct(shape, jnp.float32)


def local(
    state, vert_coef, horiz_coef, wet_mask, coupling, surface_in, remap_w, dest_tile, dest_block, dest_group
):
    levels, height, width = state.shape
    groups, tiles = lax.axis_size("grp"), lax.axis_size("tile")
    cols = width // 128
    blocks = height * cols
    slots = max(8, 2 * blocks * K // tiles)
    rim = 2 * cols
    tags = -(-(tiles * slots // 128) // 8) * 8
    devices = groups * tiles
    start = (groups - 1) * tiles
    pairs = [(i, i + 1) for i in range(devices - 1) if i + 1 != start]
    back = [(j, i) for i, j in pairs]
    axes = ("grp", "tile")

    edges = levels + levels // 2 + 2
    down, up = pl.pallas_call(
        functools.partial(edge_kernel, groups),
        out_shape=(f32(edges, rim, 128),) * 2,
        in_specs=[HBM, HBM, VM, VM],
        scratch_shapes=[
            pltpu.VMEM((levels, height, width), jnp.float32),
            pltpu.VMEM((levels - 1, height, width), jnp.float32),
            pltpu.SemaphoreType.DMA((2,)),
        ],
        compiler_params=params(60),
    )(state, vert_coef, horiz_coef, wet_mask)
    above = lax.ppermute(down, axes, pairs)
    below = lax.ppermute(up, axes, back)

    packed = pl.pallas_call(
        functools.partial(pack_kernel, tiles, slots, groups),
        out_shape=(f32(F * slots + rim * (groups - 1) + tags, 128),) * tiles,
        in_specs=[HBM] * 3 + [VM] * 4 + [HBM],
        scratch_shapes=[
            pltpu.VMEM((cols, height, K, 128, 128), jnp.bfloat16),
            pltpu.VMEM((blocks * K, F * 128), jnp.float32),
            pltpu.VMEM((height, width), jnp.float32),
            pltpu.VMEM((F, height, width), jnp.float32),
            pltpu.VMEM((F, height, width), jnp.float32),
            pltpu.SemaphoreType.DMA((cols,)),
            pltpu.SemaphoreType.DMA((3,)),
        ],
        compiler_params=params(60),
    )(
        state,
        coupling,
        surface_in,
        wet_mask,
        dest_tile.T,
        dest_block.T,
        dest_group.T,
        remap_w.reshape(height, cols, K, 128, 128),
    )
    got = [packed[0]] + [
        lax.ppermute(packed[k], "tile", [(i, i ^ k) for i in range(tiles)])
        for k in range(tiles - 1, 0, -1)
    ][::-1]

    full, halo = f32(levels, height, width), f32(levels, rim, 128)
    solved = pl.pallas_call(
        functools.partial(base_kernel, tiles, groups),
        out_shape=(full,) * 5 + (f32(4, height, width), halo, halo, f32(rim, 128)),
        scratch_shapes=[pltpu.VMEM((levels, rim, 128), jnp.float32)] * 2,
        compiler_params=params(16),
        cost_estimate=pl.CostEstimate(flops=60 * state.size, bytes_accessed=28 * state.size, transcendentals=0),
    )(state, vert_coef, horiz_coef, wet_mask, down, up, above, below)
    upper, gain, ratio, base, impulse, weights, halo_base, halo_impulse, halo_wet = solved

    merged = pl.pallas_call(
        functools.partial(merge_kernel, tiles, slots, blocks, groups),
        out_shape=(f32(F * blocks + rim, 128),) * (groups - 1),
        compiler_params=params(8),
    )(halo_wet, *got)
    arrived = [
        lax.ppermute(merged[g], "grp", [(g, groups - 1), (groups - 1, g)])
        for g in range(groups - 1)
    ]
    return pl.pallas_call(
        functools.partial(last_kernel, cols, groups),
        out_shape=(full, f32(F, height, width)),
        out_specs=(HBM, VM),
        scratch_shapes=[
            pltpu.VMEM((levels, height, width), jnp.float32),
            pltpu.SemaphoreType.DMA((4,)),
        ],
        compiler_params=params(16),
    )(
        wet_mask, base, impulse, upper, gain, ratio, weights, halo_base, halo_impulse, halo_wet, *arrived
    )


def solution(mesh):
    in_specs = (
        P(None, ("grp", "tile"), None),
        P(None, ("grp", "tile"), None),
        P(("grp", "tile"), None),
        P("tile", None),
        P(None, ("grp", "tile"), None),
        P(None, ("grp", "tile"), None),
        P(("grp", "tile"), None, None, None),
        P(("grp", "tile"), None),
        P(("grp", "tile"), None),
        P(("grp", "tile"), None),
    )
    out_specs = (P(None, ("grp", "tile"), None), P(None, ("grp", "tile"), None))
    return jax.shard_map(local, mesh=mesh, in_specs=in_specs, out_specs=out_specs, check_vma=False)
```

```python
import functools

import jax
import jax.numpy as jnp
from jax import lax
from jax.experimental import pallas as pl
from jax.experimental.pallas import tpu as pltpu
from jax.sharding import PartitionSpec as P

F = 4
K = 4
FORCING_GAIN = 0.25
VM = pl.BlockSpec(memory_space=pltpu.VMEM)
HBM = pl.BlockSpec(memory_space=pltpu.HBM)
MIB = 1024 * 1024


def params(mib):
    return pltpu.CompilerParams(vmem_limit_bytes=mib * MIB)


def split(x):
    hi = x.astype(jnp.bfloat16)
    return hi, (x - hi.astype(jnp.float32)).astype(jnp.bfloat16)


def wet_of(ocean, mask):
    return jnp.where(ocean, mask.astype(jnp.float32), 1.0)


def iota(shape, dim):
    return lax.broadcasted_iota(jnp.int32, shape, dim)


def pack_kernel(
    tiles, slots, groups, state, coupling, surface, mask, dtile, dblock, dgroup, w, *refs
):
    outs = refs[: tiles // 2]
    terms, w_here, *here, w_sem, sem = refs[tiles // 2 :]
    height, width = mask.shape
    cols = width // 128
    given = (dtile, dblock, dgroup, state.at[0], coupling, surface, mask)
    small = [pltpu.make_async_copy(a, b, sem.at[i]) for i, (a, b) in enumerate(zip(given, here))]
    large = [pltpu.make_async_copy(w.at[:, c], w_here.at[c], w_sem.at[c]) for c in range(cols)]
    for copy in small + large:
        copy.start()
    dtile, dblock, dgroup, state, coupling, surface, mask = here
    for copy in small[:3]:
        copy.wait()
    blocks = height * cols
    count = blocks * K
    ocean = lax.axis_index("grp") == groups - 1
    me = lax.axis_index("tile")

    block = dblock[...]
    line = block // cols
    col = block % cols
    group = jnp.where(ocean, dgroup[...], groups - 1)
    code = dtile[...] * 128 + col * height + line + jnp.where(ocean, dgroup[...] * blocks, 0)
    device = group * tiles + dtile[...]
    low = jnp.where(ocean, 0, (groups - 1) * tiles)
    high = jnp.where(ocean, (groups - 1) * tiles, groups * tiles)
    odd = device % 2 == 1
    beside = jnp.where(odd, device + 1, device - 1)
    reads = (line == jnp.where(odd, height - 1, 0)) & (beside >= low) & (beside < high)
    edge = (beside % tiles) * 16 + col + jnp.where(ocean, (beside // tiles) * cols, 0)
    edge = jnp.where(reads, edge, -1)

    item = iota((count, blocks), 0)
    item_k = (item // height) % K
    own = iota((count, blocks), 1) == (item % height) * cols + item // (height * K)
    up, down = iota((count, count), 0), iota((count, count), 1)

    def column(values):
        spread = jnp.broadcast_to(values[:1, :], (count, blocks))
        for k in range(1, K):
            spread = jnp.where(item_k == k, values[k : k + 1, :], spread)
        return jnp.sum(jnp.where(own, spread, 0), 1, keepdims=True)

    def turned(values):
        return jnp.sum(jnp.where(up == down, values, 0), 0, keepdims=True)

    def place_of(tile):
        return ((tile // 2) ^ (me // 2)) * 2 + tile % 2

    code_col, edge_row = column(code), turned(column(edge))
    code_row = turned(code_col)
    tile_row, tile_col, tag_col = code_row // 128, code_col // 128, code_col % 128
    same = tile_row == tile_col
    slot_row = jnp.sum(jnp.where(same & (up < down), 1, 0), 0, keepdims=True)
    slot_col = jnp.sum(jnp.where(same & (down < up), 1, 0), 1, keepdims=True)
    place_row, place_col = place_of(tile_row), place_of(tile_col)
    chooser = jnp.where(
        iota((tiles * slots, count), 0) == place_row * slots + slot_row, 1.0, 0.0
    ).astype(jnp.bfloat16)
    to_tile = jnp.where(iota((tiles, count), 0) == place_row, 1.0, 0.0).astype(jnp.bfloat16)
    labels = jnp.where(
        iota((count, 128), 1) == (place_col // 2) * slots + slot_col,
        (tag_col + 1).astype(jnp.float32),
        0.0,
    ).astype(jnp.bfloat16)
    tags = jnp.dot(to_tile, labels, preferred_element_type=jnp.float32)
    rim = cols * (groups - 1)
    rim_id = iota((tiles * 16, count), 0)
    rim_place, rim_id = rim_id // 16, rim_id % 16
    rim_tile = ((rim_place // 2) ^ (me // 2)) * 2 + rim_place % 2
    rim_id = jnp.where(
        rim_id < rim, rim_tile * 16 + jnp.where(ocean, rim_id, rim_id % cols), -2
    )
    rim_chooser = jnp.where(rim_id == edge_row, 1.0, 0.0).astype(jnp.bfloat16)

    for copy in small[3:]:
        copy.wait()
    send = coupling[...] * (state[...][None] - surface[...]) * wet_of(ocean, mask[...])[None]
    row_of = iota((F * height, 128), 0) % height
    for c in range(cols):
        piece = send[:, :, c * 128 : (c + 1) * 128].reshape(F * height, 128)
        left = jnp.concatenate(
            [jnp.where(row_of == r, piece, 0.0).astype(jnp.bfloat16) for r in range(height)], 1
        )
        large[c].wait()
        for k in range(K):
            right = w_here[c, :, k].reshape(height * 128, 128)
            made = jnp.dot(left, right, preferred_element_type=jnp.float32)
            at = (c * K + k) * height
            for f in range(F):
                terms[at : at + height, f * 128 : (f + 1) * 128] = made[
                    f * height : (f + 1) * height, :
                ]
    total = terms[:, :128]
    for f in range(1, F):
        total = total + terms[:, f * 128 : (f + 1) * 128]
    hi, lo = split(terms[...])
    packed = jnp.dot(
        jnp.concatenate([chooser, chooser], 1),
        jnp.concatenate([hi, lo], 0),
        preferred_element_type=jnp.float32,
    )
    hi, lo = split(total)
    rims = jnp.dot(
        jnp.concatenate([rim_chooser, rim_chooser], 1),
        jnp.concatenate([hi, lo], 0),
        preferred_element_type=jnp.float32,
    )
    size = F * slots + 16
    for t in range(tiles):
        out, at = outs[t // 2], (t % 2) * size
        for f in range(F):
            out[at + f * slots : at + (f + 1) * slots, :] = packed[
                t * slots : (t + 1) * slots, f * 128 : (f + 1) * 128
            ]
        at = at + F * slots
        out[at : at + 16, :] = rims[t * 16 : (t + 1) * 16, :]
        out[at + rim : at + rim + 1, :] = tags[t : t + 1, :]


def merge_kernel(slots, height, cols, groups, _, *refs):
    got, (mine, theirs) = refs[:-2], refs[-2:]
    blocks = height * cols
    size = F * slots + 16
    rim = cols * (groups - 1)
    rows = (groups - 1) * blocks
    ocean = lax.axis_index("grp") == groups - 1
    core = lax.axis_index("tile") % 2
    ids = iota((rows, 128), 0)
    ids = jnp.where(ocean, ids, ids % blocks) + 1

    def merged(which, out):
        first = which * size
        tail = got[0][pl.ds(first + F * slots, 16), :]
        for chunk in got[1:]:
            tail = tail + chunk[pl.ds(first + F * slots, 16), :]
        label = tail[rim : rim + 1, :].astype(jnp.int32)
        chooser = jnp.where(ids == label, 1.0, 0.0).astype(jnp.bfloat16)
        chooser = jnp.concatenate([chooser, chooser], 1)
        total = jnp.zeros((rows, 128), jnp.float32)
        for f in range(F):
            data = jnp.concatenate([chunk[pl.ds(first + f * slots, slots), :] for chunk in got], 0)
            hi, lo = split(data)
            part = jnp.dot(chooser, jnp.concatenate([hi, lo], 0), preferred_element_type=jnp.float32)
            total = total + part
            for g in range(groups - 1):
                at = (g * F + f) * blocks
                out[at : at + blocks, :] = part[g * blocks : (g + 1) * blocks, :]
        out[rows * F : rows * F + rim, :] = tail[:rim, :]
        return total.reshape(rim, height, 128)

    own = merged(core, mine)
    sibling = merged(1 - core, theirs)
    even = core == 0
    at = rows * F + rim
    theirs[at : at + rim, :] = jnp.where(even, own[:, height - 1, :], own[:, 0, :])
    mine[at : at + rim, :] = jnp.where(even, sibling[:, 0, :], sibling[:, height - 1, :])


def add_kernel(cols, mine, theirs, *outs):
    even = lax.axis_index("tile") % 2 == 0
    rows = outs[0].shape[0] - 2 * cols
    groups = len(outs)
    tail = groups * rows
    rims = mine[tail:, :] + theirs[tail:, :]
    for g, out in enumerate(outs):
        out[:rows, :] = mine[g * rows : (g + 1) * rows, :] + theirs[g * rows : (g + 1) * rows, :]
        far = rims[g * cols : (g + 1) * cols, :]
        near = rims[(groups + g) * cols : (groups + g + 1) * cols, :]
        out[rows : rows + cols, :] = jnp.where(even, far, near)
        out[rows + cols :, :] = jnp.where(even, near, far)


def edge_kernel(groups, state, vert, horiz, mask, down, up, wet, sem):
    levels, height, width = state.shape
    half = levels // 2
    cols = width // 128
    last = height - 1
    copies = [pltpu.make_async_copy(mask, wet, sem.at[0])]

    def move(src, dst):
        copies.append(pltpu.make_async_copy(src, dst, sem.at[len(copies)]))

    for c in range(cols):
        at, one, two = pl.ds(c * 128, 128), pl.ds(c, 1), pl.ds(cols + c, 1)
        all_levels = pl.ds(0, levels)
        move(state.at[:, pl.ds(last, 1), at], down.at[all_levels, one])
        move(state.at[:, pl.ds(last - 1, 1), at], down.at[all_levels, two])
        move(state.at[:, pl.ds(1, 1), at], up.at[all_levels, one])
        move(state.at[:, pl.ds(0, 1), at], up.at[all_levels, two])
        for out, row in ((down, pl.ds(last, 1)), (up, pl.ds(0, 1))):
            move(vert.at[pl.ds(0, half), row, at], out.at[pl.ds(levels, half), one])
            move(vert.at[pl.ds(half, half - 1), row, at], out.at[pl.ds(levels, half - 1), two])
            move(horiz.at[row, at], out.at[levels + half + 1, one])
            move(horiz.at[row, at], out.at[levels + half + 1, two])
    for copy in copies:
        copy.start()
    copies[0].wait()
    wet = wet_of(lax.axis_index("grp") == groups - 1, wet[...])
    for c in range(cols):
        at = slice(c * 128, (c + 1) * 128)
        one, two = slice(c, c + 1), slice(cols + c, cols + c + 1)
        down[levels + half, one, :] = wet[last:, at]
        down[levels + half, two, :] = wet[last - 1 : last, at]
        up[levels + half, one, :] = wet[1:2, at]
        up[levels + half, two, :] = wet[:1, at]
        for out in (down, up):
            out[levels + half - 1, two, :] = jnp.zeros((1, 128), jnp.float32)
    for copy in copies[1:]:
        copy.wait()


def weights_of(tiles, groups, horiz, wet, wet_above, wet_below):
    height, width = wet.shape
    device = lax.axis_index("grp") * tiles + lax.axis_index("tile")
    rows = device * height + iota((height, width), 0)
    start = (groups - 1) * tiles * height
    last = groups * tiles * height - 1
    above = jnp.concatenate([wet_above, wet[:-1]], 0)
    below = jnp.concatenate([wet[1:], wet_below], 0)
    above = jnp.where((rows > 0) & (rows != start), above, 0.0)
    below = jnp.where((rows < last) & (rows + 1 != start), below, 0.0)
    column = iota((height, width), 1)
    left = jnp.where(column == 0, 0.0, pltpu.roll(wet, 1, 1))
    right = jnp.where(column == width - 1, 0.0, pltpu.roll(wet, width - 1, 1))
    scale = horiz * wet
    return scale * left, scale * right, scale * above, scale * below


def line_of(halo, first, cols):
    return jnp.concatenate([halo[first + c : first + c + 1, :] for c in range(cols)], 1)


def around(field, halo):
    height, width = field.shape
    cols = width // 128
    return (
        pltpu.roll(field, 1, 1),
        pltpu.roll(field, width - 1, 1),
        jnp.concatenate([line_of(halo, 0, cols), field[:-1]], 0),
        jnp.concatenate([field[1:], line_of(halo, cols, cols)], 0),
    )


def stencil(field, halo, weights):
    total = field
    for other, weight in zip(around(field, halo), weights):
        total = total + weight * (other - field)
    return total


def shifted(halo, lane):
    rows = halo.shape[0]
    to_right, to_left = pltpu.roll(halo, 1, 1), pltpu.roll(halo, 127, 1)
    return (
        jnp.where(lane == 0, pltpu.roll(to_right, 1, 0), to_right),
        jnp.where(lane == 127, pltpu.roll(to_left, rows - 1, 0), to_left),
    )


def solve_kernel(
    tiles, groups, state, vert, horiz, mask, down, up, above, below, parts, halo_wet,
    upper, gain, ratio, base, impulse, halo_base, halo_impulse, halo_vert, halo_upper,
):
    levels, height, width = state.shape
    cols = width // 128
    half = levels // 2
    shape = (2 * cols, 128)
    low_half = iota(shape, 0) < cols
    lane = iota(shape, 1)

    def turn(x):
        return pltpu.roll(x, cols, 0)

    def beside(i):
        return jnp.where(low_half, above[i], below[i])

    def behind(i):
        return turn(jnp.where(low_half, below[i], above[i]))

    def inside(i):
        return turn(jnp.where(low_half, down[i], up[i]))

    wet = wet_of(lax.axis_index("grp") == groups - 1, mask[...])
    wet_halo = beside(levels + half)
    halo_wet[...] = wet_halo
    weights = weights_of(
        tiles, groups, horiz[...], wet, line_of(wet_halo, 0, cols), line_of(wet_halo, cols, cols)
    )
    scale = beside(levels + half + 1) * wet_halo
    wet_left, wet_right = shifted(wet_halo, lane)
    place = iota(shape, 0) % cols
    weight_left = scale * jnp.where((place == 0) & (lane == 0), 0.0, wet_left)
    weight_right = scale * jnp.where((place == cols - 1) & (lane == 127), 0.0, wet_right)
    weight_behind = scale * behind(levels + half)
    weight_inside = scale * inside(levels + half)

    def spread(i, _):
        a, b = above[levels + i], below[levels + i]
        halo_vert[i] = jnp.where(low_half, a, turn(b)) * wet_halo
        halo_vert[half + i] = jnp.where(low_half, turn(a), b) * wet_halo
        return 0

    lax.fori_loop(0, half, spread, 0, unroll=4)
    zero = jnp.zeros((height, width), jnp.float32)
    zero_halo = jnp.zeros(shape, jnp.float32)

    def forward(level, carry, last=False, first=False):
        low, c, r, e, low_h, c_h, r_h, e_h = carry
        upp = zero if last else vert[level] * wet
        inverse = 1.0 / (1.0 + low + upp + low * c)
        c = -upp * inverse
        step = low * inverse
        halo = beside(level)
        r = stencil(state[level], halo, weights) * inverse + step * r
        e = inverse if first else step * e
        upper[level] = c
        gain[level] = inverse
        ratio[level] = step
        base[level] = r
        impulse[level] = e
        upp_h = zero_halo if last else halo_vert[level]
        inverse = 1.0 / (1.0 + low_h + upp_h + low_h * c_h)
        c_h = -upp_h * inverse
        step = low_h * inverse
        left, right = shifted(halo, lane)
        field = (
            halo
            + weight_left * (left - halo)
            + weight_right * (right - halo)
            + weight_behind * (behind(level) - halo)
            + weight_inside * (inside(level) - halo)
        )
        r_h = field * inverse + step * r_h
        e_h = inverse if first else step * e_h
        halo_upper[level] = c_h
        halo_base[level] = r_h
        halo_impulse[level] = e_h
        return upp, c, r, e, upp_h, c_h, r_h, e_h

    carry = forward(0, (zero,) * 4 + (zero_halo,) * 4, first=True)
    carry = lax.fori_loop(1, levels - 1, forward, carry, unroll=2)
    carry = forward(levels - 1, carry, last=True)

    def backward(i, carry):
        level = levels - 2 - i
        c, c_h = upper[level], halo_upper[level]
        x = base[level] - c * carry[0]
        y = impulse[level] - c * carry[1]
        x_h = halo_base[level] - c_h * carry[2]
        y_h = halo_impulse[level] - c_h * carry[3]
        base[level] = x
        impulse[level] = y
        halo_base[level] = x_h
        halo_impulse[level] = y_h
        return x, y, x_h, y_h

    lax.fori_loop(0, levels - 1, backward, (carry[2], carry[3], carry[6], carry[7]), unroll=2)

    rest = 1.0 - weights[0] - weights[1] - weights[2] - weights[3]

    def forward_parts(level, carry, first=False):
        g = impulse[level]
        rhs = [stencil(base[level], halo_base[level], weights), rest * g + (1.0 if first else 0.0)]
        rhs += [w * x for w, x in zip(weights, around(g, halo_impulse[level]))]
        inverse, step = gain[level], ratio[level]
        made = tuple(x * inverse + step * r for x, r in zip(rhs, carry))
        for i in range(6):
            parts[i, level] = made[i]
        return made

    carry = forward_parts(0, (zero,) * 6, first=True)
    carry = lax.fori_loop(1, levels, forward_parts, carry)

    def backward_parts(i, carry):
        level = levels - 2 - i
        c = upper[level]
        made = tuple(parts[j, level] - c * carry[j] for j in range(6))
        for j in range(6):
            parts[j, level] = made[j]
        return made

    lax.fori_loop(0, levels - 1, backward_parts, carry, unroll=2)


def last_kernel(cols, groups, mask, parts, halo_wet, *refs):
    arrived = refs[: groups - 1]
    out, received, field, sem = refs[groups - 1 :]
    _, levels, height, width = parts.shape
    total = arrived[0][...]
    for other in arrived[1:]:
        total = total + other[...]
    for f in range(F):
        for c in range(cols):
            at = (f * cols + c) * height
            received[f, :, c * 128 : (c + 1) * 128] = total[at : at + height, :]
    wet = wet_of(lax.axis_index("grp") == groups - 1, mask[...])
    force = FORCING_GAIN * wet * jnp.sum(received[...], 0)
    force_halo = FORCING_GAIN * halo_wet[...] * total[F * cols * height :, :]
    factors = (force,) + around(force, force_halo)

    def level_of(level, _):
        x = parts[0, level]
        for i in range(5):
            x = x + parts[i + 1, level] * factors[i]
        field[level] = x
        return 0

    chunks = 4
    size = levels // chunks
    copies = []
    for i in range(chunks):
        lax.fori_loop(i * size, (i + 1) * size, level_of, 0, unroll=4)
        at = pl.ds(i * size, size)
        copies.append(pltpu.make_async_copy(field.at[at], out.at[at], sem.at[i]))
        copies[-1].start()
    for copy in copies:
        copy.wait()


def f32(*shape):
    return jax.ShapeDtypeStruct(shape, jnp.float32)


def cost(us):
    return pl.CostEstimate(flops=0, bytes_accessed=int(us * 3e6), transcendentals=0)


def local(
    state, vert_coef, horiz_coef, wet_mask, coupling, surface_in, remap_w, dest_tile, dest_block, dest_group
):
    levels, height, width = state.shape
    groups, tiles = lax.axis_size("grp"), lax.axis_size("tile")
    cols = width // 128
    blocks = height * cols
    slots = max(8, 2 * blocks * K // tiles)
    rim = 2 * cols
    devices = groups * tiles
    start = (groups - 1) * tiles
    pairs = [(i, i + 1) for i in range(devices - 1) if i + 1 != start]
    back = [(j, i) for i, j in pairs]
    axes = ("grp", "tile")

    edges = levels + levels // 2 + 2
    down, up = pl.pallas_call(
        functools.partial(edge_kernel, groups),
        out_shape=(f32(edges, rim, 128),) * 2,
        in_specs=[HBM] * 4,
        scratch_shapes=[
            pltpu.VMEM((height, width), jnp.int32),
            pltpu.SemaphoreType.DMA((1 + 12 * cols,)),
        ],
        compiler_params=params(60),
        cost_estimate=cost(10),
    )(state, vert_coef, horiz_coef, wet_mask)
    above = lax.ppermute(down, axes, pairs)
    below = lax.ppermute(up, axes, back)

    packed = pl.pallas_call(
        functools.partial(pack_kernel, tiles, slots, groups),
        out_shape=(f32(2 * (F * slots + 16), 128),) * (tiles // 2),
        in_specs=[HBM] * 8,
        scratch_shapes=[
            pltpu.VMEM((blocks * K, F * 128), jnp.float32),
            pltpu.VMEM((cols, height, K, 128, 128), jnp.bfloat16),
        ]
        + [pltpu.VMEM((K, blocks), jnp.int32)] * 3
        + [pltpu.VMEM((height, width), jnp.float32)]
        + [pltpu.VMEM((F, height, width), jnp.float32)] * 2
        + [
            pltpu.VMEM((height, width), jnp.int32),
            pltpu.SemaphoreType.DMA((cols,)),
            pltpu.SemaphoreType.DMA((7,)),
        ],
        compiler_params=params(60),
        cost_estimate=cost(3),
    )(
        state,
        coupling,
        surface_in,
        wet_mask,
        dest_tile.T,
        dest_block.T,
        dest_group.T,
        remap_w.reshape(height, cols, K, 128, 128),
    )
    got = [packed[0]] + [
        lax.ppermute(packed[k], "tile", [(i, ((i // 2) ^ k) * 2 + i % 2) for i in range(tiles)])
        for k in range(1, tiles // 2)
    ]

    full, halo = f32(levels, height, width), f32(levels, rim, 128)
    scratch = [pltpu.VMEM(s.shape, jnp.float32) for s in [full] * 5 + [halo] * 4]
    parts, halo_wet = pl.pallas_call(
        functools.partial(solve_kernel, tiles, groups),
        out_shape=(f32(6, levels, height, width), f32(rim, 128)),
        scratch_shapes=scratch,
        compiler_params=params(24),
        cost_estimate=cost(8),
    )(state, vert_coef, horiz_coef, wet_mask, down, up, above, below)

    rows = (groups - 1) * (F * blocks + rim)
    mine, theirs = pl.pallas_call(
        functools.partial(merge_kernel, slots, height, cols, groups),
        out_shape=(f32(rows, 128),) * 2,
        compiler_params=params(8),
        cost_estimate=cost(1),
    )(halo_wet, *got)
    theirs = lax.ppermute(theirs, "tile", [(i, i ^ 1) for i in range(tiles)])
    merged = pl.pallas_call(
        functools.partial(add_kernel, cols),
        out_shape=(f32(F * blocks + rim, 128),) * (groups - 1),
        compiler_params=params(8),
        cost_estimate=cost(1),
    )(mine, theirs)
    arrived = [
        lax.ppermute(merged[g], "grp", [(g, groups - 1), (groups - 1, g)])
        for g in range(groups - 1)
    ]
    return pl.pallas_call(
        functools.partial(last_kernel, cols, groups),
        out_shape=(full, f32(F, height, width)),
        out_specs=(HBM, VM),
        scratch_shapes=[
            pltpu.VMEM((levels, height, width), jnp.float32),
            pltpu.SemaphoreType.DMA((4,)),
        ],
        compiler_params=params(16),
    )(wet_mask, parts, halo_wet, *arrived)


def solution(mesh):
    in_specs = (
        P(None, ("grp", "tile"), None),
        P(None, ("grp", "tile"), None),
        P(("grp", "tile"), None),
        P("tile", None),
        P(None, ("grp", "tile"), None),
        P(None, ("grp", "tile"), None),
        P(("grp", "tile"), None, None, None),
        P(("grp", "tile"), None),
        P(("grp", "tile"), None),
        P(("grp", "tile"), None),
    )
    out_specs = (P(None, ("grp", "tile"), None), P(None, ("grp", "tile"), None))
    return jax.shard_map(local, mesh=mesh, in_specs=in_specs, out_specs=out_specs, check_vma=False)
```

```python
import functools

import jax
import jax.numpy as jnp
from jax import lax
from jax.experimental import pallas as pl
from jax.experimental.pallas import tpu as pltpu
from jax.sharding import PartitionSpec as P

F = 4
K = 4
FORCING_GAIN = 0.25
VM = pl.BlockSpec(memory_space=pltpu.VMEM)
HBM = pl.BlockSpec(memory_space=pltpu.HBM)
MIB = 1024 * 1024


def params(mib):
    return pltpu.CompilerParams(vmem_limit_bytes=mib * MIB)


def split(x):
    hi = x.astype(jnp.bfloat16)
    return hi, (x - hi.astype(jnp.float32)).astype(jnp.bfloat16)


def wet_of(ocean, mask):
    return jnp.where(ocean, mask.astype(jnp.float32), 1.0)


def iota(shape, dim):
    return lax.broadcasted_iota(jnp.int32, shape, dim)


def pack_kernel(
    tiles, slots, groups, state, coupling, surface, mask, dtile, dblock, dgroup, w, *refs
):
    outs = refs[: tiles // 2]
    terms, w_here, *here, w_sem, sem = refs[tiles // 2 :]
    height, width = mask.shape
    cols = width // 128
    given = (dtile, dblock, dgroup, state.at[0], coupling, surface, mask)
    small = [pltpu.make_async_copy(a, b, sem.at[i]) for i, (a, b) in enumerate(zip(given, here))]
    large = [pltpu.make_async_copy(w.at[:, c], w_here.at[c], w_sem.at[c]) for c in range(cols)]
    for copy in small + large:
        copy.start()
    dtile, dblock, dgroup, state, coupling, surface, mask = here
    for copy in small[:3]:
        copy.wait()
    blocks = height * cols
    count = blocks * K
    ocean = lax.axis_index("grp") == groups - 1
    me = lax.axis_index("tile")

    block = dblock[...]
    line = block // cols
    col = block % cols
    group = jnp.where(ocean, dgroup[...], groups - 1)
    code = dtile[...] * 128 + col * height + line + jnp.where(ocean, dgroup[...] * blocks, 0)
    device = group * tiles + dtile[...]
    low = jnp.where(ocean, 0, (groups - 1) * tiles)
    high = jnp.where(ocean, (groups - 1) * tiles, groups * tiles)
    odd = device % 2 == 1
    beside = jnp.where(odd, device + 1, device - 1)
    reads = (line == jnp.where(odd, height - 1, 0)) & (beside >= low) & (beside < high)
    edge = (beside % tiles) * 16 + col + jnp.where(ocean, (beside // tiles) * cols, 0)
    edge = jnp.where(reads, edge, -1)

    item = iota((count, blocks), 0)
    item_k = (item // height) % K
    own = iota((count, blocks), 1) == (item % height) * cols + item // (height * K)
    up, down = iota((count, count), 0), iota((count, count), 1)

    def column(values):
        spread = jnp.broadcast_to(values[:1, :], (count, blocks))
        for k in range(1, K):
            spread = jnp.where(item_k == k, values[k : k + 1, :], spread)
        return jnp.sum(jnp.where(own, spread, 0), 1, keepdims=True)

    def turned(values):
        return jnp.sum(jnp.where(up == down, values, 0), 0, keepdims=True)

    def place_of(tile):
        return ((tile // 2) ^ (me // 2)) * 2 + tile % 2

    code_col, edge_row = column(code), turned(column(edge))
    code_row = turned(code_col)
    tile_row, tile_col, tag_col = code_row // 128, code_col // 128, code_col % 128
    same = tile_row == tile_col
    slot_row = jnp.sum(jnp.where(same & (up < down), 1, 0), 0, keepdims=True)
    slot_col = jnp.sum(jnp.where(same & (down < up), 1, 0), 1, keepdims=True)
    place_row, place_col = place_of(tile_row), place_of(tile_col)
    chooser = jnp.where(
        iota((tiles * slots, count), 0) == place_row * slots + slot_row, 1.0, 0.0
    ).astype(jnp.bfloat16)
    to_tile = jnp.where(iota((tiles, count), 0) == place_row, 1.0, 0.0).astype(jnp.bfloat16)
    labels = jnp.where(
        iota((count, 128), 1) == (place_col // 2) * slots + slot_col,
        (tag_col + 1).astype(jnp.float32),
        0.0,
    ).astype(jnp.bfloat16)
    tags = jnp.dot(to_tile, labels, preferred_element_type=jnp.float32)
    rim = cols * (groups - 1)
    rim_id = iota((tiles * 16, count), 0)
    rim_place, rim_id = rim_id // 16, rim_id % 16
    rim_tile = ((rim_place // 2) ^ (me // 2)) * 2 + rim_place % 2
    rim_id = jnp.where(
        rim_id < rim, rim_tile * 16 + jnp.where(ocean, rim_id, rim_id % cols), -2
    )
    rim_chooser = jnp.where(rim_id == edge_row, 1.0, 0.0).astype(jnp.bfloat16)

    for copy in small[3:]:
        copy.wait()
    send = coupling[...] * (state[...][None] - surface[...]) * wet_of(ocean, mask[...])[None]
    row_of = iota((F * height, 128), 0) % height
    for c in range(cols):
        piece = send[:, :, c * 128 : (c + 1) * 128].reshape(F * height, 128)
        left = jnp.concatenate(
            [jnp.where(row_of == r, piece, 0.0).astype(jnp.bfloat16) for r in range(height)], 1
        )
        large[c].wait()
        for k in range(K):
            right = w_here[c, :, k].reshape(height * 128, 128)
            made = jnp.dot(left, right, preferred_element_type=jnp.float32)
            at = (c * K + k) * height
            for f in range(F):
                terms[at : at + height, f * 128 : (f + 1) * 128] = made[
                    f * height : (f + 1) * height, :
                ]
    total = terms[:, :128]
    for f in range(1, F):
        total = total + terms[:, f * 128 : (f + 1) * 128]
    hi, lo = split(terms[...])
    packed = jnp.dot(
        jnp.concatenate([chooser, chooser], 1),
        jnp.concatenate([hi, lo], 0),
        preferred_element_type=jnp.float32,
    )
    hi, lo = split(total)
    rims = jnp.dot(
        jnp.concatenate([rim_chooser, rim_chooser], 1),
        jnp.concatenate([hi, lo], 0),
        preferred_element_type=jnp.float32,
    )
    size = F * slots + 16
    for t in range(tiles):
        out, at = outs[t // 2], (t % 2) * size
        for f in range(F):
            out[at + f * slots : at + (f + 1) * slots, :] = packed[
                t * slots : (t + 1) * slots, f * 128 : (f + 1) * 128
            ]
        at = at + F * slots
        out[at : at + 16, :] = rims[t * 16 : (t + 1) * 16, :]
        out[at + rim : at + rim + 1, :] = tags[t : t + 1, :]


def merge_kernel(slots, height, cols, groups, *refs):
    got, (mine, theirs) = refs[:-2], refs[-2:]
    blocks = height * cols
    size = F * slots + 16
    rim = cols * (groups - 1)
    rows = (groups - 1) * blocks
    ocean = lax.axis_index("grp") == groups - 1
    core = lax.axis_index("tile") % 2
    ids = iota((rows, 128), 0)
    ids = jnp.where(ocean, ids, ids % blocks) + 1

    def merged(which, out):
        first = which * size
        tail = got[0][pl.ds(first + F * slots, 16), :]
        for chunk in got[1:]:
            tail = tail + chunk[pl.ds(first + F * slots, 16), :]
        label = tail[rim : rim + 1, :].astype(jnp.int32)
        chooser = jnp.where(ids == label, 1.0, 0.0).astype(jnp.bfloat16)
        chooser = jnp.concatenate([chooser, chooser], 1)
        total = jnp.zeros((rows, 128), jnp.float32)
        for f in range(F):
            data = jnp.concatenate([chunk[pl.ds(first + f * slots, slots), :] for chunk in got], 0)
            hi, lo = split(data)
            part = jnp.dot(chooser, jnp.concatenate([hi, lo], 0), preferred_element_type=jnp.float32)
            total = total + part
            for g in range(groups - 1):
                at = (g * F + f) * blocks
                out[at : at + blocks, :] = part[g * blocks : (g + 1) * blocks, :]
        out[rows * F : rows * F + rim, :] = tail[:rim, :]
        return total.reshape(rim, height, 128)

    own = merged(core, mine)
    sibling = merged(1 - core, theirs)
    even = core == 0
    at = rows * F + rim
    theirs[at : at + rim, :] = jnp.where(even, own[:, height - 1, :], own[:, 0, :])
    mine[at : at + rim, :] = jnp.where(even, sibling[:, 0, :], sibling[:, height - 1, :])


def add_kernel(cols, mine, theirs, *outs):
    even = lax.axis_index("tile") % 2 == 0
    rows = outs[0].shape[0] - 2 * cols
    groups = len(outs)
    tail = groups * rows
    rims = mine[tail:, :] + theirs[tail:, :]
    for g, out in enumerate(outs):
        out[:rows, :] = mine[g * rows : (g + 1) * rows, :] + theirs[g * rows : (g + 1) * rows, :]
        far = rims[g * cols : (g + 1) * cols, :]
        near = rims[(groups + g) * cols : (groups + g + 1) * cols, :]
        out[rows : rows + cols, :] = jnp.where(even, far, near)
        out[rows + cols :, :] = jnp.where(even, near, far)


def edge_kernel(groups, state, vert, horiz, mask, down, up, wet, sem):
    levels, height, width = state.shape
    half = levels // 2
    cols = width // 128
    last = height - 1
    copies = [pltpu.make_async_copy(mask, wet, sem.at[0])]

    def move(src, dst):
        copies.append(pltpu.make_async_copy(src, dst, sem.at[len(copies)]))

    for c in range(cols):
        at, one, two = pl.ds(c * 128, 128), pl.ds(c, 1), pl.ds(cols + c, 1)
        all_levels = pl.ds(0, levels)
        move(state.at[:, pl.ds(last, 1), at], down.at[all_levels, one])
        move(state.at[:, pl.ds(last - 1, 1), at], down.at[all_levels, two])
        move(state.at[:, pl.ds(1, 1), at], up.at[all_levels, one])
        move(state.at[:, pl.ds(0, 1), at], up.at[all_levels, two])
        for out, row in ((down, pl.ds(last, 1)), (up, pl.ds(0, 1))):
            move(vert.at[pl.ds(0, half), row, at], out.at[pl.ds(levels, half), one])
            move(vert.at[pl.ds(half, half - 1), row, at], out.at[pl.ds(levels, half - 1), two])
            move(horiz.at[row, at], out.at[levels + half + 1, one])
            move(horiz.at[row, at], out.at[levels + half + 1, two])
    for copy in copies:
        copy.start()
    copies[0].wait()
    wet = wet_of(lax.axis_index("grp") == groups - 1, wet[...])
    for c in range(cols):
        at = slice(c * 128, (c + 1) * 128)
        one, two = slice(c, c + 1), slice(cols + c, cols + c + 1)
        down[levels + half, one, :] = wet[last:, at]
        down[levels + half, two, :] = wet[last - 1 : last, at]
        up[levels + half, one, :] = wet[1:2, at]
        up[levels + half, two, :] = wet[:1, at]
        for out in (down, up):
            out[levels + half - 1, two, :] = jnp.zeros((1, 128), jnp.float32)
    for copy in copies[1:]:
        copy.wait()


def weights_of(tiles, groups, horiz, wet, wet_above, wet_below):
    height, width = wet.shape
    device = lax.axis_index("grp") * tiles + lax.axis_index("tile")
    rows = device * height + iota((height, width), 0)
    start = (groups - 1) * tiles * height
    last = groups * tiles * height - 1
    above = jnp.concatenate([wet_above, wet[:-1]], 0)
    below = jnp.concatenate([wet[1:], wet_below], 0)
    above = jnp.where((rows > 0) & (rows != start), above, 0.0)
    below = jnp.where((rows < last) & (rows + 1 != start), below, 0.0)
    column = iota((height, width), 1)
    left = jnp.where(column == 0, 0.0, pltpu.roll(wet, 1, 1))
    right = jnp.where(column == width - 1, 0.0, pltpu.roll(wet, width - 1, 1))
    scale = horiz * wet
    return scale * left, scale * right, scale * above, scale * below


def line_of(halo, first, cols):
    return jnp.concatenate([halo[first + c : first + c + 1, :] for c in range(cols)], 1)


def around(field, halo):
    height, width = field.shape
    cols = width // 128
    return (
        pltpu.roll(field, 1, 1),
        pltpu.roll(field, width - 1, 1),
        jnp.concatenate([line_of(halo, 0, cols), field[:-1]], 0),
        jnp.concatenate([field[1:], line_of(halo, cols, cols)], 0),
    )


def stencil(field, halo, weights):
    total = field
    for other, weight in zip(around(field, halo), weights):
        total = total + weight * (other - field)
    return total


def shifted(halo, lane):
    rows = halo.shape[0]
    to_right, to_left = pltpu.roll(halo, 1, 1), pltpu.roll(halo, 127, 1)
    return (
        jnp.where(lane == 0, pltpu.roll(to_right, 1, 0), to_right),
        jnp.where(lane == 127, pltpu.roll(to_left, rows - 1, 0), to_left),
    )


def inverse_of(x):
    y = pl.reciprocal(x, approx=True)
    return y * (2.0 - x * y)


def solve_kernel(
    tiles, groups, state, vert, horiz, mask, above, below, chunk, parts, halo_wet, chunk_out,
    upper, gain, ratio, base, impulse, halo_base, halo_impulse, halo_vert, halo_upper, rim, sem,
):
    levels, height, width = state.shape
    cols = width // 128
    half = levels // 2
    shape = (2 * cols, 128)
    low_half = iota(shape, 0) < cols
    lane = iota(shape, 1)

    def turn(x):
        return pltpu.roll(x, cols, 0)

    def beside(i):
        return jnp.where(low_half, above[i], below[i])

    def behind(i):
        return turn(jnp.where(low_half, below[i], above[i]))

    copy = pltpu.make_async_copy(chunk, chunk_out, sem)
    copy.start()
    for c in range(cols):
        rim[:, c, :] = state[:, 0, c * 128 : (c + 1) * 128]
        rim[:, cols + c, :] = state[:, height - 1, c * 128 : (c + 1) * 128]
    wet = wet_of(lax.axis_index("grp") == groups - 1, mask[...])
    wet_halo = beside(levels + half)
    halo_wet[...] = wet_halo
    weights = weights_of(
        tiles, groups, horiz[...], wet, line_of(wet_halo, 0, cols), line_of(wet_halo, cols, cols)
    )
    scale = beside(levels + half + 1) * wet_halo
    wet_left, wet_right = shifted(wet_halo, lane)
    place = iota(shape, 0) % cols
    weight_left = scale * jnp.where((place == 0) & (lane == 0), 0.0, wet_left)
    weight_right = scale * jnp.where((place == cols - 1) & (lane == 127), 0.0, wet_right)
    weight_behind = scale * behind(levels + half)
    wet_inside = [wet[r : r + 1, c * 128 : (c + 1) * 128] for r in (0, height - 1) for c in range(cols)]
    weight_inside = scale * jnp.concatenate(wet_inside, 0)

    def spread(i, _):
        a, b = above[levels + i], below[levels + i]
        halo_vert[i] = jnp.where(low_half, a, turn(b)) * wet_halo
        halo_vert[half + i] = jnp.where(low_half, turn(a), b) * wet_halo
        return 0

    lax.fori_loop(0, half, spread, 0, unroll=4)
    zero = jnp.zeros((height, width), jnp.float32)
    zero_halo = jnp.zeros(shape, jnp.float32)

    def forward(level, carry, last=False, first=False):
        low, c, r, e, low_h, c_h, r_h, e_h = carry
        upp = zero if last else vert[level] * wet
        inverse = inverse_of(1.0 + low + upp + low * c)
        c = -upp * inverse
        step = low * inverse
        halo = beside(level)
        r = stencil(state[level], halo, weights) * inverse + step * r
        e = inverse if first else step * e
        upper[level] = c
        gain[level] = inverse
        ratio[level] = step
        base[level] = r
        impulse[level] = e
        upp_h = zero_halo if last else halo_vert[level]
        inverse = inverse_of(1.0 + low_h + upp_h + low_h * c_h)
        c_h = -upp_h * inverse
        step = low_h * inverse
        left, right = shifted(halo, lane)
        field = (
            halo
            + weight_left * (left - halo)
            + weight_right * (right - halo)
            + weight_behind * (behind(level) - halo)
            + weight_inside * (rim[level] - halo)
        )
        r_h = field * inverse + step * r_h
        e_h = inverse if first else step * e_h
        halo_upper[level] = c_h
        halo_base[level] = r_h
        halo_impulse[level] = e_h
        return upp, c, r, e, upp_h, c_h, r_h, e_h

    carry = forward(0, (zero,) * 4 + (zero_halo,) * 4, first=True)
    carry = lax.fori_loop(1, levels - 1, forward, carry, unroll=31)
    carry = forward(levels - 1, carry, last=True)

    def backward(i, carry):
        level = levels - 2 - i
        c, c_h = upper[level], halo_upper[level]
        x = base[level] - c * carry[0]
        y = impulse[level] - c * carry[1]
        x_h = halo_base[level] - c_h * carry[2]
        y_h = halo_impulse[level] - c_h * carry[3]
        base[level] = x
        impulse[level] = y
        halo_base[level] = x_h
        halo_impulse[level] = y_h
        return x, y, x_h, y_h

    lax.fori_loop(0, levels - 1, backward, (carry[2], carry[3], carry[6], carry[7]), unroll=9)

    rest = 1.0 - weights[0] - weights[1] - weights[2] - weights[3]

    def forward_parts(level, carry, first=False):
        g = impulse[level]
        rhs = [stencil(base[level], halo_base[level], weights), rest * g + (1.0 if first else 0.0)]
        rhs += [w * x for w, x in zip(weights, around(g, halo_impulse[level]))]
        inverse, step = gain[level], ratio[level]
        made = tuple(x * inverse + step * r for x, r in zip(rhs, carry))
        for i in range(6):
            parts[i, level] = made[i]
        return made

    carry = forward_parts(0, (zero,) * 6, first=True)
    carry = lax.fori_loop(1, levels, forward_parts, carry, unroll=7)

    def backward_parts(i, carry):
        level = levels - 2 - i
        c = upper[level]
        made = tuple(parts[j, level] - c * carry[j] for j in range(6))
        for j in range(6):
            parts[j, level] = made[j]
        return made

    lax.fori_loop(0, levels - 1, backward_parts, carry, unroll=9)
    copy.wait()


def last_kernel(cols, groups, mask, parts, halo_wet, *refs):
    arrived = refs[: groups - 1]
    out, received, field, sem = refs[groups - 1 :]
    _, levels, height, width = parts.shape
    total = arrived[0][...]
    for other in arrived[1:]:
        total = total + other[...]
    for f in range(F):
        for c in range(cols):
            at = (f * cols + c) * height
            received[f, :, c * 128 : (c + 1) * 128] = total[at : at + height, :]
    wet = wet_of(lax.axis_index("grp") == groups - 1, mask[...])
    force = FORCING_GAIN * wet * jnp.sum(received[...], 0)
    force_halo = FORCING_GAIN * halo_wet[...] * total[F * cols * height :, :]
    factors = (force,) + around(force, force_halo)

    def level_of(level, _):
        x = parts[0, level]
        for i in range(5):
            x = x + parts[i + 1, level] * factors[i]
        field[level] = x
        return 0

    chunks = 4
    size = levels // chunks
    copies = []
    for i in range(chunks):
        lax.fori_loop(i * size, (i + 1) * size, level_of, 0, unroll=4)
        at = pl.ds(i * size, size)
        copies.append(pltpu.make_async_copy(field.at[at], out.at[at], sem.at[i]))
        copies[-1].start()
    for copy in copies:
        copy.wait()


def f32(*shape):
    return jax.ShapeDtypeStruct(shape, jnp.float32)


def cost(us):
    return pl.CostEstimate(flops=0, bytes_accessed=int(us * 3e6), transcendentals=0)


def edges_of(groups, state, vert_coef, horiz_coef, wet_mask):
    levels, height, width = state.shape
    cols = width // 128
    return pl.pallas_call(
        functools.partial(edge_kernel, groups),
        out_shape=(f32(levels + levels // 2 + 2, 2 * cols, 128),) * 2,
        in_specs=[HBM] * 4,
        scratch_shapes=[
            pltpu.VMEM((height, width), jnp.int32),
            pltpu.SemaphoreType.DMA((1 + 12 * cols,)),
        ],
        compiler_params=params(60),
        cost_estimate=cost(10),
    )(state, vert_coef, horiz_coef, wet_mask)


def pack(groups, tiles, slots, state, coupling, surface, mask, dtile, dblock, dgroup, w):
    height, width = mask.shape
    cols = width // 128
    blocks = height * cols
    return pl.pallas_call(
        functools.partial(pack_kernel, tiles, slots, groups),
        out_shape=(f32(2 * (F * slots + 16), 128),) * (tiles // 2),
        in_specs=[HBM] * 8,
        scratch_shapes=[
            pltpu.VMEM((blocks * K, F * 128), jnp.float32),
            pltpu.VMEM((cols, height, K, 128, 128), jnp.bfloat16),
        ]
        + [pltpu.VMEM((K, blocks), jnp.int32)] * 3
        + [pltpu.VMEM((height, width), jnp.float32)]
        + [pltpu.VMEM((F, height, width), jnp.float32)] * 2
        + [
            pltpu.VMEM((height, width), jnp.int32),
            pltpu.SemaphoreType.DMA((cols,)),
            pltpu.SemaphoreType.DMA((7,)),
        ],
        compiler_params=params(60),
        cost_estimate=cost(3),
    )(state, coupling, surface, mask, dtile.T, dblock.T, dgroup.T, w.reshape(height, cols, K, 128, 128))


def solve(groups, tiles, state, vert_coef, horiz_coef, wet_mask, above, below, chunk):
    levels, height, width = state.shape
    full, halo = f32(levels, height, width), f32(levels, width // 64, 128)
    scratch = [pltpu.VMEM(s.shape, jnp.float32) for s in [full] * 5 + [halo] * 5]
    return pl.pallas_call(
        functools.partial(solve_kernel, tiles, groups),
        out_shape=(f32(6, levels, height, width), f32(width // 64, 128), f32(*chunk.shape)),
        in_specs=[VM] * 6 + [HBM],
        scratch_shapes=scratch + [pltpu.SemaphoreType.DMA],
        compiler_params=params(24),
        cost_estimate=cost(8),
    )(state, vert_coef, horiz_coef, wet_mask, above, below, chunk)


def finish(groups, wet_mask, parts, halo_wet, arrived):
    _, levels, height, width = parts.shape
    return pl.pallas_call(
        functools.partial(last_kernel, width // 128, groups),
        out_shape=(f32(levels, height, width), f32(F, height, width)),
        out_specs=(HBM, VM),
        scratch_shapes=[
            pltpu.VMEM((levels, height, width), jnp.float32),
            pltpu.SemaphoreType.DMA((4,)),
        ],
        compiler_params=params(16),
    )(wet_mask, parts, halo_wet, *arrived)


def local(
    state, vert_coef, horiz_coef, wet_mask, coupling, surface_in, remap_w, dest_tile, dest_block, dest_group
):
    levels, height, width = state.shape
    groups, tiles = lax.axis_size("grp"), lax.axis_size("tile")
    cols = width // 128
    blocks = height * cols
    slots = max(8, 2 * blocks * K // tiles)
    rim = 2 * cols
    devices = groups * tiles
    start = (groups - 1) * tiles
    pairs = [(i, i + 1) for i in range(devices - 1) if i + 1 != start]
    back = [(j, i) for i, j in pairs]
    axes = ("grp", "tile")

    down, up = edges_of(groups, state, vert_coef, horiz_coef, wet_mask)
    above = lax.ppermute(down, axes, pairs)
    below = lax.ppermute(up, axes, back)
    packed = pack(
        groups, tiles, slots, state, coupling, surface_in, wet_mask, dest_tile, dest_block, dest_group, remap_w
    )
    got = [
        lax.ppermute(packed[k], "tile", [(i, ((i // 2) ^ k) * 2 + i % 2) for i in range(tiles)])
        for k in range(1, tiles // 2)
    ]
    parts, halo_wet, chunk = solve(
        groups, tiles, state, vert_coef, horiz_coef, wet_mask, above, below, packed[0]
    )
    rows = (groups - 1) * (F * blocks + rim)
    mine, theirs = pl.pallas_call(
        functools.partial(merge_kernel, slots, height, cols, groups),
        out_shape=(f32(rows, 128),) * 2,
        compiler_params=params(8),
        cost_estimate=cost(1),
    )(chunk, *got)
    theirs = lax.ppermute(theirs, "tile", [(i, i ^ 1) for i in range(tiles)])
    merged = pl.pallas_call(
        functools.partial(add_kernel, cols),
        out_shape=(f32(F * blocks + rim, 128),) * (groups - 1),
        compiler_params=params(8),
        cost_estimate=cost(1),
    )(mine, theirs)
    arrived = [
        lax.ppermute(merged[g], "grp", [(g, groups - 1), (groups - 1, g)])
        for g in range(groups - 1)
    ]
    return finish(groups, wet_mask, parts, halo_wet, arrived)


def solution(mesh):
    in_specs = (
        P(None, ("grp", "tile"), None),
        P(None, ("grp", "tile"), None),
        P(("grp", "tile"), None),
        P("tile", None),
        P(None, ("grp", "tile"), None),
        P(None, ("grp", "tile"), None),
        P(("grp", "tile"), None, None, None),
        P(("grp", "tile"), None),
        P(("grp", "tile"), None),
        P(("grp", "tile"), None),
    )
    out_specs = (P(None, ("grp", "tile"), None), P(None, ("grp", "tile"), None))
    return jax.shard_map(local, mesh=mesh, in_specs=in_specs, out_specs=out_specs, check_vma=False)
```

```python
import functools

import jax
import jax.numpy as jnp
from jax import lax
from jax.experimental import pallas as pl
from jax.experimental.pallas import tpu as pltpu
from jax.sharding import PartitionSpec as P

F = 4
K = 4
FORCING_GAIN = 0.25
VM = pl.BlockSpec(memory_space=pltpu.VMEM)
HBM = pl.BlockSpec(memory_space=pltpu.HBM)
MIB = 1024 * 1024


def params(mib):
    return pltpu.CompilerParams(vmem_limit_bytes=mib * MIB)


def split(x):
    hi = x.astype(jnp.bfloat16)
    return hi, (x - hi.astype(jnp.float32)).astype(jnp.bfloat16)


def wet_of(ocean, mask):
    return jnp.where(ocean, mask.astype(jnp.float32), 1.0)


def iota(shape, dim):
    return lax.broadcasted_iota(jnp.int32, shape, dim)


def pack_kernel(
    tiles, slots, groups, state, coupling, surface, mask, dtile, dblock, dgroup, w, *refs
):
    outs = refs[: tiles // 2]
    terms, w_here, *here, w_sem, sem = refs[tiles // 2 :]
    height, width = mask.shape
    cols = width // 128
    given = (dtile, dblock, dgroup, state.at[0], coupling, surface, mask)
    small = [pltpu.make_async_copy(a, b, sem.at[i]) for i, (a, b) in enumerate(zip(given, here))]
    large = [pltpu.make_async_copy(w.at[:, c], w_here.at[c], w_sem.at[c]) for c in range(cols)]
    for copy in small + large:
        copy.start()
    dtile, dblock, dgroup, state, coupling, surface, mask = here
    for copy in small[:3]:
        copy.wait()
    blocks = height * cols
    count = blocks * K
    ocean = lax.axis_index("grp") == groups - 1
    me = lax.axis_index("tile")

    block = dblock[...]
    line = block // cols
    col = block % cols
    group = jnp.where(ocean, dgroup[...], groups - 1)
    code = dtile[...] * 128 + col * height + line + jnp.where(ocean, dgroup[...] * blocks, 0)
    device = group * tiles + dtile[...]
    low = jnp.where(ocean, 0, (groups - 1) * tiles)
    high = jnp.where(ocean, (groups - 1) * tiles, groups * tiles)
    odd = device % 2 == 1
    beside = jnp.where(odd, device + 1, device - 1)
    reads = (line == jnp.where(odd, height - 1, 0)) & (beside >= low) & (beside < high)
    edge = (beside % tiles) * 16 + col + jnp.where(ocean, (beside // tiles) * cols, 0)
    edge = jnp.where(reads, edge, -1)

    item = iota((count, blocks), 0)
    item_k = (item // height) % K
    own = iota((count, blocks), 1) == (item % height) * cols + item // (height * K)
    up, down = iota((count, count), 0), iota((count, count), 1)

    def column(values):
        spread = jnp.broadcast_to(values[:1, :], (count, blocks))
        for k in range(1, K):
            spread = jnp.where(item_k == k, values[k : k + 1, :], spread)
        return jnp.sum(jnp.where(own, spread, 0), 1, keepdims=True)

    def turned(values):
        return jnp.sum(jnp.where(up == down, values, 0), 0, keepdims=True)

    def place_of(tile):
        return ((tile // 2) ^ (me // 2)) * 2 + tile % 2

    code_col, edge_row = column(code), turned(column(edge))
    code_row = turned(code_col)
    tile_row, tile_col, tag_col = code_row // 128, code_col // 128, code_col % 128
    same = tile_row == tile_col
    slot_row = jnp.sum(jnp.where(same & (up < down), 1, 0), 0, keepdims=True)
    slot_col = jnp.sum(jnp.where(same & (down < up), 1, 0), 1, keepdims=True)
    place_row, place_col = place_of(tile_row), place_of(tile_col)
    chooser = jnp.where(
        iota((tiles * slots, count), 0) == place_row * slots + slot_row, 1.0, 0.0
    ).astype(jnp.bfloat16)
    to_tile = jnp.where(iota((tiles, count), 0) == place_row, 1.0, 0.0).astype(jnp.bfloat16)
    labels = jnp.where(
        iota((count, 128), 1) == (place_col // 2) * slots + slot_col,
        (tag_col + 1).astype(jnp.float32),
        0.0,
    ).astype(jnp.bfloat16)
    tags = jnp.dot(to_tile, labels, preferred_element_type=jnp.float32)
    rim = cols * (groups - 1)
    rim_id = iota((tiles * 16, count), 0)
    rim_place, rim_id = rim_id // 16, rim_id % 16
    rim_tile = ((rim_place // 2) ^ (me // 2)) * 2 + rim_place % 2
    rim_id = jnp.where(
        rim_id < rim, rim_tile * 16 + jnp.where(ocean, rim_id, rim_id % cols), -2
    )
    rim_chooser = jnp.where(rim_id == edge_row, 1.0, 0.0).astype(jnp.bfloat16)

    for copy in small[3:]:
        copy.wait()
    send = coupling[...] * (state[...][None] - surface[...]) * wet_of(ocean, mask[...])[None]
    row_of = iota((F * height, 128), 0) % height
    for c in range(cols):
        piece = send[:, :, c * 128 : (c + 1) * 128].reshape(F * height, 128)
        left = jnp.concatenate(
            [jnp.where(row_of == r, piece, 0.0).astype(jnp.bfloat16) for r in range(height)], 1
        )
        large[c].wait()
        for k in range(K):
            right = w_here[c, :, k].reshape(height * 128, 128)
            made = jnp.dot(left, right, preferred_element_type=jnp.float32)
            at = (c * K + k) * height
            for f in range(F):
                terms[at : at + height, f * 128 : (f + 1) * 128] = made[
                    f * height : (f + 1) * height, :
                ]
    total = terms[:, :128]
    for f in range(1, F):
        total = total + terms[:, f * 128 : (f + 1) * 128]
    hi, lo = split(terms[...])
    packed = jnp.dot(
        jnp.concatenate([chooser, chooser], 1),
        jnp.concatenate([hi, lo], 0),
        preferred_element_type=jnp.float32,
    )
    hi, lo = split(total)
    rims = jnp.dot(
        jnp.concatenate([rim_chooser, rim_chooser], 1),
        jnp.concatenate([hi, lo], 0),
        preferred_element_type=jnp.float32,
    )
    size = F * slots + 16
    for t in range(tiles):
        out, at = outs[t // 2], (t % 2) * size
        for f in range(F):
            out[at + f * slots : at + (f + 1) * slots, :] = packed[
                t * slots : (t + 1) * slots, f * 128 : (f + 1) * 128
            ]
        at = at + F * slots
        out[at : at + 16, :] = rims[t * 16 : (t + 1) * 16, :]
        out[at + rim : at + rim + 1, :] = tags[t : t + 1, :]


def merge_kernel(slots, height, cols, groups, *refs):
    got, (mine, theirs) = refs[:-2], refs[-2:]
    blocks = height * cols
    size = F * slots + 16
    rim = cols * (groups - 1)
    rows = (groups - 1) * blocks
    ocean = lax.axis_index("grp") == groups - 1
    core = lax.axis_index("tile") % 2
    ids = iota((rows, 128), 0)
    ids = jnp.where(ocean, ids, ids % blocks) + 1

    def merged(which, out):
        first = which * size
        tail = got[0][pl.ds(first + F * slots, 16), :]
        for chunk in got[1:]:
            tail = tail + chunk[pl.ds(first + F * slots, 16), :]
        label = tail[rim : rim + 1, :].astype(jnp.int32)
        chooser = jnp.where(ids == label, 1.0, 0.0).astype(jnp.bfloat16)
        chooser = jnp.concatenate([chooser, chooser], 1)
        total = jnp.zeros((rows, 128), jnp.float32)
        for f in range(F):
            data = jnp.concatenate([chunk[pl.ds(first + f * slots, slots), :] for chunk in got], 0)
            hi, lo = split(data)
            part = jnp.dot(chooser, jnp.concatenate([hi, lo], 0), preferred_element_type=jnp.float32)
            total = total + part
            for g in range(groups - 1):
                at = (g * F + f) * blocks
                out[at : at + blocks, :] = part[g * blocks : (g + 1) * blocks, :]
        out[rows * F : rows * F + rim, :] = tail[:rim, :]
        return total.reshape(rim, height, 128)

    own = merged(core, mine)
    sibling = merged(1 - core, theirs)
    even = core == 0
    at = rows * F + rim
    theirs[at : at + rim, :] = jnp.where(even, own[:, height - 1, :], own[:, 0, :])
    mine[at : at + rim, :] = jnp.where(even, sibling[:, 0, :], sibling[:, height - 1, :])


def add_kernel(cols, mine, theirs, *outs):
    even = lax.axis_index("tile") % 2 == 0
    rows = outs[0].shape[0] - 2 * cols
    groups = len(outs)
    tail = groups * rows
    rims = mine[tail:, :] + theirs[tail:, :]
    for g, out in enumerate(outs):
        out[:rows, :] = mine[g * rows : (g + 1) * rows, :] + theirs[g * rows : (g + 1) * rows, :]
        far = rims[g * cols : (g + 1) * cols, :]
        near = rims[(groups + g) * cols : (groups + g + 1) * cols, :]
        out[rows : rows + cols, :] = jnp.where(even, far, near)
        out[rows + cols :, :] = jnp.where(even, near, far)


def edge_kernel(groups, state, vert, horiz, mask, chip, core, wet, sem):
    levels, height, width = state.shape
    half = levels // 2
    cols = width // 128
    last = height - 1

    def fill(down, up):
        copies = [pltpu.make_async_copy(mask, wet, sem.at[0])]

        def move(src, dst):
            copies.append(pltpu.make_async_copy(src, dst, sem.at[len(copies)]))

        for c in range(cols):
            at, one, two = pl.ds(c * 128, 128), pl.ds(c, 1), pl.ds(cols + c, 1)
            all_levels = pl.ds(0, levels)
            move(state.at[:, pl.ds(last, 1), at], down.at[all_levels, one])
            move(state.at[:, pl.ds(last - 1, 1), at], down.at[all_levels, two])
            move(state.at[:, pl.ds(1, 1), at], up.at[all_levels, one])
            move(state.at[:, pl.ds(0, 1), at], up.at[all_levels, two])
            for out, row in ((down, pl.ds(last, 1)), (up, pl.ds(0, 1))):
                move(vert.at[pl.ds(0, half), row, at], out.at[pl.ds(levels, half), one])
                move(vert.at[pl.ds(half, half - 1), row, at], out.at[pl.ds(levels, half - 1), two])
                move(horiz.at[row, at], out.at[levels + half + 1, one])
                move(horiz.at[row, at], out.at[levels + half + 1, two])
        for copy in copies:
            copy.start()
        copies[0].wait()
        wet_here = wet_of(lax.axis_index("grp") == groups - 1, wet[...])
        for c in range(cols):
            at = slice(c * 128, (c + 1) * 128)
            one, two = slice(c, c + 1), slice(cols + c, cols + c + 1)
            down[levels + half, one, :] = wet_here[last:, at]
            down[levels + half, two, :] = wet_here[last - 1 : last, at]
            up[levels + half, one, :] = wet_here[1:2, at]
            up[levels + half, two, :] = wet_here[:1, at]
            for out in (down, up):
                out[levels + half - 1, two, :] = jnp.zeros((1, 128), jnp.float32)
        for copy in copies[1:]:
            copy.wait()

    even = lax.axis_index("tile") % 2 == 0
    pl.when(even)(lambda: fill(core, chip))
    pl.when(jnp.logical_not(even))(lambda: fill(chip, core))


def weights_of(tiles, groups, horiz, wet, wet_above, wet_below):
    height, width = wet.shape
    device = lax.axis_index("grp") * tiles + lax.axis_index("tile")
    rows = device * height + iota((height, width), 0)
    start = (groups - 1) * tiles * height
    last = groups * tiles * height - 1
    above = jnp.concatenate([wet_above, wet[:-1]], 0)
    below = jnp.concatenate([wet[1:], wet_below], 0)
    above = jnp.where((rows > 0) & (rows != start), above, 0.0)
    below = jnp.where((rows < last) & (rows + 1 != start), below, 0.0)
    column = iota((height, width), 1)
    left = jnp.where(column == 0, 0.0, pltpu.roll(wet, 1, 1))
    right = jnp.where(column == width - 1, 0.0, pltpu.roll(wet, width - 1, 1))
    scale = horiz * wet
    return scale * left, scale * right, scale * above, scale * below


def line_of(halo, first, cols):
    return jnp.concatenate([halo[first + c : first + c + 1, :] for c in range(cols)], 1)


def around(field, halo):
    height, width = field.shape
    cols = width // 128
    return (
        pltpu.roll(field, 1, 1),
        pltpu.roll(field, width - 1, 1),
        jnp.concatenate([line_of(halo, 0, cols), field[:-1]], 0),
        jnp.concatenate([field[1:], line_of(halo, cols, cols)], 0),
    )


def stencil(field, halo, weights):
    total = field
    for other, weight in zip(around(field, halo), weights):
        total = total + weight * (other - field)
    return total


def shifted(halo, lane):
    rows = halo.shape[0]
    to_right, to_left = pltpu.roll(halo, 1, 1), pltpu.roll(halo, 127, 1)
    return (
        jnp.where(lane == 0, pltpu.roll(to_right, 1, 0), to_right),
        jnp.where(lane == 127, pltpu.roll(to_left, rows - 1, 0), to_left),
    )


def inverse_of(x):
    y = pl.reciprocal(x, approx=True)
    return y * (2.0 - x * y)


def solve_kernel(
    tiles, groups, state, vert, horiz, mask, chip, core, chunk, parts, halo_wet, chunk_out,
    upper, gain, ratio, base, impulse, halo_base, halo_impulse, halo_vert, halo_upper, rim, sem,
):
    levels, height, width = state.shape
    cols = width // 128
    half = levels // 2
    shape = (2 * cols, 128)
    low_half = iota(shape, 0) < cols
    lane = iota(shape, 1)
    parity = lax.axis_index("tile") % 2
    from_chip = iota(shape, 0) // cols == parity

    def turn(x):
        return pltpu.roll(x, cols, 0)

    def beside(i):
        return jnp.where(from_chip, chip[i], core[i])

    def behind(i):
        return turn(jnp.where(from_chip, core[i], chip[i]))

    copy = pltpu.make_async_copy(chunk, chunk_out, sem)
    copy.start()
    for c in range(cols):
        rim[:, c, :] = state[:, 0, c * 128 : (c + 1) * 128]
        rim[:, cols + c, :] = state[:, height - 1, c * 128 : (c + 1) * 128]
    wet = wet_of(lax.axis_index("grp") == groups - 1, mask[...])
    wet_halo = beside(levels + half)
    halo_wet[...] = wet_halo
    weights = weights_of(
        tiles, groups, horiz[...], wet, line_of(wet_halo, 0, cols), line_of(wet_halo, cols, cols)
    )
    scale = beside(levels + half + 1) * wet_halo
    wet_left, wet_right = shifted(wet_halo, lane)
    place = iota(shape, 0) % cols
    weight_left = scale * jnp.where((place == 0) & (lane == 0), 0.0, wet_left)
    weight_right = scale * jnp.where((place == cols - 1) & (lane == 127), 0.0, wet_right)
    weight_behind = scale * behind(levels + half)
    wet_inside = [wet[r : r + 1, c * 128 : (c + 1) * 128] for r in (0, height - 1) for c in range(cols)]
    weight_inside = scale * jnp.concatenate(wet_inside, 0)

    def spread(i, _):
        x, y = chip[levels + i], core[levels + i]
        a, b = jnp.where(parity == 0, x, y), jnp.where(parity == 0, y, x)
        halo_vert[i] = jnp.where(low_half, a, turn(b)) * wet_halo
        halo_vert[half + i] = jnp.where(low_half, turn(a), b) * wet_halo
        return 0

    lax.fori_loop(0, half, spread, 0, unroll=4)
    zero = jnp.zeros((height, width), jnp.float32)
    zero_halo = jnp.zeros(shape, jnp.float32)

    def forward(level, carry, last=False, first=False):
        low, c, r, e, low_h, c_h, r_h, e_h = carry
        upp = zero if last else vert[level] * wet
        inverse = inverse_of(1.0 + low + upp + low * c)
        c = -upp * inverse
        step = low * inverse
        halo = beside(level)
        r = stencil(state[level], halo, weights) * inverse + step * r
        e = inverse if first else step * e
        upper[level] = c
        gain[level] = inverse
        ratio[level] = step
        base[level] = r
        impulse[level] = e
        upp_h = zero_halo if last else halo_vert[level]
        inverse = inverse_of(1.0 + low_h + upp_h + low_h * c_h)
        c_h = -upp_h * inverse
        step = low_h * inverse
        left, right = shifted(halo, lane)
        field = (
            halo
            + weight_left * (left - halo)
            + weight_right * (right - halo)
            + weight_behind * (behind(level) - halo)
            + weight_inside * (rim[level] - halo)
        )
        r_h = field * inverse + step * r_h
        e_h = inverse if first else step * e_h
        halo_upper[level] = c_h
        halo_base[level] = r_h
        halo_impulse[level] = e_h
        return upp, c, r, e, upp_h, c_h, r_h, e_h

    carry = forward(0, (zero,) * 4 + (zero_halo,) * 4, first=True)
    carry = lax.fori_loop(1, levels - 1, forward, carry, unroll=31)
    carry = forward(levels - 1, carry, last=True)

    def backward(i, carry):
        level = levels - 2 - i
        c, c_h = upper[level], halo_upper[level]
        x = base[level] - c * carry[0]
        y = impulse[level] - c * carry[1]
        x_h = halo_base[level] - c_h * carry[2]
        y_h = halo_impulse[level] - c_h * carry[3]
        base[level] = x
        impulse[level] = y
        halo_base[level] = x_h
        halo_impulse[level] = y_h
        return x, y, x_h, y_h

    lax.fori_loop(0, levels - 1, backward, (carry[2], carry[3], carry[6], carry[7]), unroll=9)

    rest = 1.0 - weights[0] - weights[1] - weights[2] - weights[3]

    def forward_parts(level, carry, first=False):
        g = impulse[level]
        rhs = [stencil(base[level], halo_base[level], weights), rest * g + (1.0 if first else 0.0)]
        rhs += [w * x for w, x in zip(weights, around(g, halo_impulse[level]))]
        inverse, step = gain[level], ratio[level]
        made = tuple(x * inverse + step * r for x, r in zip(rhs, carry))
        for i in range(6):
            parts[i, level] = made[i]
        return made

    carry = forward_parts(0, (zero,) * 6, first=True)
    carry = lax.fori_loop(1, levels, forward_parts, carry, unroll=7)

    def backward_parts(i, carry):
        level = levels - 2 - i
        c = upper[level]
        made = tuple(parts[j, level] - c * carry[j] for j in range(6))
        for j in range(6):
            parts[j, level] = made[j]
        return made

    lax.fori_loop(0, levels - 1, backward_parts, carry, unroll=9)
    copy.wait()


def last_kernel(cols, groups, mask, parts, halo_wet, *refs):
    arrived = refs[: groups - 1]
    out, received, field, sem = refs[groups - 1 :]
    _, levels, height, width = parts.shape
    group = lax.axis_index("grp")
    total = jnp.zeros(arrived[0].shape, jnp.float32)
    for g, other in enumerate(arrived):
        total = total + jnp.where((group == groups - 1) | (group == g), other[...], 0.0)
    for f in range(F):
        for c in range(cols):
            at = (f * cols + c) * height
            received[f, :, c * 128 : (c + 1) * 128] = total[at : at + height, :]
    wet = wet_of(lax.axis_index("grp") == groups - 1, mask[...])
    force = FORCING_GAIN * wet * jnp.sum(received[...], 0)
    force_halo = FORCING_GAIN * halo_wet[...] * total[F * cols * height :, :]
    factors = (force,) + around(force, force_halo)

    def level_of(level, _):
        x = parts[0, level]
        for i in range(5):
            x = x + parts[i + 1, level] * factors[i]
        field[level] = x
        return 0

    chunks = 4
    size = levels // chunks
    copies = []
    for i in range(chunks):
        lax.fori_loop(i * size, (i + 1) * size, level_of, 0, unroll=4)
        at = pl.ds(i * size, size)
        copies.append(pltpu.make_async_copy(field.at[at], out.at[at], sem.at[i]))
        copies[-1].start()
    for copy in copies:
        copy.wait()


def f32(*shape):
    return jax.ShapeDtypeStruct(shape, jnp.float32)


def cost(us):
    return pl.CostEstimate(flops=0, bytes_accessed=int(us * 3e6), transcendentals=0)


def edges_of(groups, state, vert_coef, horiz_coef, wet_mask):
    levels, height, width = state.shape
    cols = width // 128
    return pl.pallas_call(
        functools.partial(edge_kernel, groups),
        out_shape=(f32(levels + levels // 2 + 2, 2 * cols, 128),) * 2,
        in_specs=[HBM] * 4,
        scratch_shapes=[
            pltpu.VMEM((height, width), jnp.int32),
            pltpu.SemaphoreType.DMA((1 + 12 * cols,)),
        ],
        compiler_params=params(60),
        cost_estimate=cost(10),
    )(state, vert_coef, horiz_coef, wet_mask)


def pack(groups, tiles, slots, state, coupling, surface, mask, dtile, dblock, dgroup, w):
    height, width = mask.shape
    cols = width // 128
    blocks = height * cols
    return pl.pallas_call(
        functools.partial(pack_kernel, tiles, slots, groups),
        out_shape=(f32(2 * (F * slots + 16), 128),) * (tiles // 2),
        in_specs=[HBM] * 8,
        scratch_shapes=[
            pltpu.VMEM((blocks * K, F * 128), jnp.float32),
            pltpu.VMEM((cols, height, K, 128, 128), jnp.bfloat16),
        ]
        + [pltpu.VMEM((K, blocks), jnp.int32)] * 3
        + [pltpu.VMEM((height, width), jnp.float32)]
        + [pltpu.VMEM((F, height, width), jnp.float32)] * 2
        + [
            pltpu.VMEM((height, width), jnp.int32),
            pltpu.SemaphoreType.DMA((cols,)),
            pltpu.SemaphoreType.DMA((7,)),
        ],
        compiler_params=params(60),
        cost_estimate=cost(3),
    )(state, coupling, surface, mask, dtile.T, dblock.T, dgroup.T, w.reshape(height, cols, K, 128, 128))


def solve(groups, tiles, state, vert_coef, horiz_coef, wet_mask, chip, core, chunk):
    levels, height, width = state.shape
    full, halo = f32(levels, height, width), f32(levels, width // 64, 128)
    scratch = [pltpu.VMEM(s.shape, jnp.float32) for s in [full] * 5 + [halo] * 5]
    return pl.pallas_call(
        functools.partial(solve_kernel, tiles, groups),
        out_shape=(f32(6, levels, height, width), f32(width // 64, 128), f32(*chunk.shape)),
        in_specs=[VM] * 6 + [HBM],
        scratch_shapes=scratch + [pltpu.SemaphoreType.DMA],
        compiler_params=params(24),
        cost_estimate=cost(8),
    )(state, vert_coef, horiz_coef, wet_mask, chip, core, chunk)


def finish(groups, wet_mask, parts, halo_wet, arrived):
    _, levels, height, width = parts.shape
    return pl.pallas_call(
        functools.partial(last_kernel, width // 128, groups),
        out_shape=(f32(levels, height, width), f32(F, height, width)),
        out_specs=(HBM, VM),
        scratch_shapes=[
            pltpu.VMEM((levels, height, width), jnp.float32),
            pltpu.SemaphoreType.DMA((4,)),
        ],
        compiler_params=params(16),
    )(wet_mask, parts, halo_wet, *arrived)


def local(
    state, vert_coef, horiz_coef, wet_mask, coupling, surface_in, remap_w, dest_tile, dest_block, dest_group
):
    levels, height, width = state.shape
    groups, tiles = lax.axis_size("grp"), lax.axis_size("tile")
    cols = width // 128
    blocks = height * cols
    slots = max(8, 2 * blocks * K // tiles)
    rim = 2 * cols
    devices = groups * tiles
    start = (groups - 1) * tiles
    axes = ("grp", "tile")
    across = [(i, i + 1) for i in range(1, devices - 1, 2) if i + 1 != start]
    across = across + [(j, i) for i, j in across]
    chip, core = edges_of(groups, state, vert_coef, horiz_coef, wet_mask)
    chip = lax.ppermute(chip, axes, across)
    core = lax.ppermute(core, axes, [(i, i ^ 1) for i in range(devices)])
    packed = pack(
        groups, tiles, slots, state, coupling, surface_in, wet_mask, dest_tile, dest_block, dest_group, remap_w
    )
    chips = tiles // 2
    got = [
        lax.ppermute(packed[k], "tile", [(i, ((i // 2) ^ k) * 2 + i % 2) for i in range(tiles)])
        for k in list(range(chips // 2, chips)) + list(range(1, chips // 2))
    ]
    got = got[chips - chips // 2 :] + got[: chips - chips // 2]
    parts, halo_wet, chunk = solve(
        groups, tiles, state, vert_coef, horiz_coef, wet_mask, chip, core, packed[0]
    )
    rows = (groups - 1) * (F * blocks + rim)
    mine, theirs = pl.pallas_call(
        functools.partial(merge_kernel, slots, height, cols, groups),
        out_shape=(f32(rows, 128),) * 2,
        compiler_params=params(8),
        cost_estimate=cost(1),
    )(chunk, *got)
    theirs = lax.ppermute(theirs, "tile", [(i, i ^ 1) for i in range(tiles)])
    merged = pl.pallas_call(
        functools.partial(add_kernel, cols),
        out_shape=(f32(F * blocks + rim, 128),) * (groups - 1),
        compiler_params=params(8),
        cost_estimate=cost(1),
    )(mine, theirs)
    arrived = [
        lax.ppermute(merged[g], "grp", [(j, (j + g + 1) % groups) for j in range(groups)])
        for g in range(groups - 1)
    ]
    return finish(groups, wet_mask, parts, halo_wet, arrived)


def solution(mesh):
    in_specs = (
        P(None, ("grp", "tile"), None),
        P(None, ("grp", "tile"), None),
        P(("grp", "tile"), None),
        P("tile", None),
        P(None, ("grp", "tile"), None),
        P(None, ("grp", "tile"), None),
        P(("grp", "tile"), None, None, None),
        P(("grp", "tile"), None),
        P(("grp", "tile"), None),
        P(("grp", "tile"), None),
    )
    out_specs = (P(None, ("grp", "tile"), None), P(None, ("grp", "tile"), None))
    return jax.shard_map(local, mesh=mesh, in_specs=in_specs, out_specs=out_specs, check_vma=False)
```

```python
import functools

import jax
import jax.numpy as jnp
from jax import lax
from jax.experimental import pallas as pl
from jax.experimental.pallas import tpu as pltpu
from jax.sharding import PartitionSpec as P

F = 4
K = 4
FORCING_GAIN = 0.25
VM = pl.BlockSpec(memory_space=pltpu.VMEM)
HBM = pl.BlockSpec(memory_space=pltpu.HBM)
MIB = 1024 * 1024


def params(mib):
    return pltpu.CompilerParams(vmem_limit_bytes=mib * MIB)


def split(x):
    hi = x.astype(jnp.bfloat16)
    return hi, (x - hi.astype(jnp.float32)).astype(jnp.bfloat16)


def wet_of(ocean, mask):
    return jnp.where(ocean, mask.astype(jnp.float32), 1.0)


def iota(shape, dim):
    return lax.broadcasted_iota(jnp.int32, shape, dim)


def pack_kernel(
    tiles, slots, groups, state, coupling, surface, mask, dtile, dblock, dgroup, w, *refs
):
    outs = refs[: tiles // 2]
    terms, w_here, *here, w_sem, sem = refs[tiles // 2 :]
    height, width = mask.shape
    cols = width // 128
    given = (dtile, dblock, dgroup, state.at[0], coupling, surface, mask)
    small = [pltpu.make_async_copy(a, b, sem.at[i]) for i, (a, b) in enumerate(zip(given, here))]
    large = [pltpu.make_async_copy(w.at[:, c], w_here.at[c], w_sem.at[c]) for c in range(cols)]
    for copy in small + large:
        copy.start()
    dtile, dblock, dgroup, state, coupling, surface, mask = here
    for copy in small[:3]:
        copy.wait()
    blocks = height * cols
    count = blocks * K
    ocean = lax.axis_index("grp") == groups - 1
    me = lax.axis_index("tile")

    block = dblock[...]
    line = block // cols
    col = block % cols
    group = jnp.where(ocean, dgroup[...], groups - 1)
    code = dtile[...] * 128 + col * height + line + jnp.where(ocean, dgroup[...] * blocks, 0)
    device = group * tiles + dtile[...]
    low = jnp.where(ocean, 0, (groups - 1) * tiles)
    high = jnp.where(ocean, (groups - 1) * tiles, groups * tiles)
    odd = device % 2 == 1
    beside = jnp.where(odd, device + 1, device - 1)
    reads = (line == jnp.where(odd, height - 1, 0)) & (beside >= low) & (beside < high)
    edge = (beside % tiles) * 16 + col + jnp.where(ocean, (beside // tiles) * cols, 0)
    edge = jnp.where(reads, edge, -1)

    item = iota((count, blocks), 0)
    item_k = (item // height) % K
    own = iota((count, blocks), 1) == (item % height) * cols + item // (height * K)
    up, down = iota((count, count), 0), iota((count, count), 1)

    def column(values):
        spread = jnp.broadcast_to(values[:1, :], (count, blocks))
        for k in range(1, K):
            spread = jnp.where(item_k == k, values[k : k + 1, :], spread)
        return jnp.sum(jnp.where(own, spread, 0), 1, keepdims=True)

    def turned(values):
        return jnp.sum(jnp.where(up == down, values, 0), 0, keepdims=True)

    def place_of(tile):
        return ((tile // 2) ^ (me // 2)) * 2 + tile % 2

    code_col, edge_row = column(code), turned(column(edge))
    code_row = turned(code_col)
    tile_row, tile_col, tag_col = code_row // 128, code_col // 128, code_col % 128
    same = tile_row == tile_col
    slot_row = jnp.sum(jnp.where(same & (up < down), 1, 0), 0, keepdims=True)
    slot_col = jnp.sum(jnp.where(same & (down < up), 1, 0), 1, keepdims=True)
    place_row, place_col = place_of(tile_row), place_of(tile_col)
    chooser = jnp.where(
        iota((tiles * slots, count), 0) == place_row * slots + slot_row, 1.0, 0.0
    ).astype(jnp.bfloat16)
    to_tile = jnp.where(iota((tiles, count), 0) == place_row, 1.0, 0.0).astype(jnp.bfloat16)
    labels = jnp.where(
        iota((count, 128), 1) == (place_col // 2) * slots + slot_col,
        (tag_col + 1).astype(jnp.float32),
        0.0,
    ).astype(jnp.bfloat16)
    tags = jnp.dot(to_tile, labels, preferred_element_type=jnp.float32)
    rim = cols * (groups - 1)
    rim_id = iota((tiles * 16, count), 0)
    rim_place, rim_id = rim_id // 16, rim_id % 16
    rim_tile = ((rim_place // 2) ^ (me // 2)) * 2 + rim_place % 2
    rim_id = jnp.where(
        rim_id < rim, rim_tile * 16 + jnp.where(ocean, rim_id, rim_id % cols), -2
    )
    rim_chooser = jnp.where(rim_id == edge_row, 1.0, 0.0).astype(jnp.bfloat16)

    for copy in small[3:]:
        copy.wait()
    send = coupling[...] * (state[...][None] - surface[...]) * wet_of(ocean, mask[...])[None]
    row_of = iota((F * height, 128), 0) % height
    for c in range(cols):
        piece = send[:, :, c * 128 : (c + 1) * 128].reshape(F * height, 128)
        left = jnp.concatenate(
            [jnp.where(row_of == r, piece, 0.0).astype(jnp.bfloat16) for r in range(height)], 1
        )
        large[c].wait()
        for k in range(K):
            right = w_here[c, :, k].reshape(height * 128, 128)
            made = jnp.dot(left, right, preferred_element_type=jnp.float32)
            at = (c * K + k) * height
            for f in range(F):
                terms[at : at + height, f * 128 : (f + 1) * 128] = made[
                    f * height : (f + 1) * height, :
                ]
    total = terms[:, :128]
    for f in range(1, F):
        total = total + terms[:, f * 128 : (f + 1) * 128]
    hi, lo = split(terms[...])
    packed = jnp.dot(
        jnp.concatenate([chooser, chooser], 1),
        jnp.concatenate([hi, lo], 0),
        preferred_element_type=jnp.float32,
    )
    hi, lo = split(total)
    rims = jnp.dot(
        jnp.concatenate([rim_chooser, rim_chooser], 1),
        jnp.concatenate([hi, lo], 0),
        preferred_element_type=jnp.float32,
    )
    size = F * slots + 16
    for t in range(tiles):
        out, at = outs[t // 2], (t % 2) * size
        for f in range(F):
            out[at + f * slots : at + (f + 1) * slots, :] = packed[
                t * slots : (t + 1) * slots, f * 128 : (f + 1) * 128
            ]
        at = at + F * slots
        out[at : at + 16, :] = rims[t * 16 : (t + 1) * 16, :]
        out[at + rim : at + rim + 1, :] = tags[t : t + 1, :]


def merge_kernel(slots, height, cols, groups, *refs):
    got, (mine, theirs) = refs[:-2], refs[-2:]
    blocks = height * cols
    size = F * slots + 16
    rim = cols * (groups - 1)
    rows = (groups - 1) * blocks
    ocean = lax.axis_index("grp") == groups - 1
    core = lax.axis_index("tile") % 2
    ids = iota((rows, 128), 0)
    ids = jnp.where(ocean, ids, ids % blocks) + 1

    def merged(which, out):
        first = which * size
        tail = got[0][pl.ds(first + F * slots, 16), :]
        for chunk in got[1:]:
            tail = tail + chunk[pl.ds(first + F * slots, 16), :]
        label = tail[rim : rim + 1, :].astype(jnp.int32)
        chooser = jnp.where(ids == label, 1.0, 0.0).astype(jnp.bfloat16)
        chooser = jnp.concatenate([chooser, chooser], 1)
        total = jnp.zeros((rows, 128), jnp.float32)
        for f in range(F):
            data = jnp.concatenate([chunk[pl.ds(first + f * slots, slots), :] for chunk in got], 0)
            hi, lo = split(data)
            part = jnp.dot(chooser, jnp.concatenate([hi, lo], 0), preferred_element_type=jnp.float32)
            total = total + part
            for g in range(groups - 1):
                at = (g * F + f) * blocks
                out[at : at + blocks, :] = part[g * blocks : (g + 1) * blocks, :]
        out[rows * F : rows * F + rim, :] = tail[:rim, :]
        return total.reshape(rim, height, 128)

    own = merged(core, mine)
    sibling = merged(1 - core, theirs)
    even = core == 0
    at = rows * F + rim
    theirs[at : at + rim, :] = jnp.where(even, own[:, height - 1, :], own[:, 0, :])
    mine[at : at + rim, :] = jnp.where(even, sibling[:, 0, :], sibling[:, height - 1, :])


def add_kernel(cols, mine, theirs, *outs):
    even = lax.axis_index("tile") % 2 == 0
    rows = outs[0].shape[0] - 2 * cols
    groups = len(outs)
    tail = groups * rows
    rims = mine[tail:, :] + theirs[tail:, :]
    for g, out in enumerate(outs):
        out[:rows, :] = mine[g * rows : (g + 1) * rows, :] + theirs[g * rows : (g + 1) * rows, :]
        far = rims[g * cols : (g + 1) * cols, :]
        near = rims[(groups + g) * cols : (groups + g + 1) * cols, :]
        out[rows : rows + cols, :] = jnp.where(even, far, near)
        out[rows + cols :, :] = jnp.where(even, near, far)


def edge_kernel(groups, state, vert, horiz, mask, _, chip, core):
    levels, height, width = state.shape
    half = levels // 2
    cols = width // 128
    last = height - 1
    wet = wet_of(lax.axis_index("grp") == groups - 1, mask[...])

    def fill(down, up):
        for c in range(cols):
            at = slice(c * 128, (c + 1) * 128)
            for out, beside, behind, one, two in (
                (down, last, last - 1, c, cols + c),
                (up, 0, 1, cols + c, c),
            ):
                out[:levels, one, :] = state[:, beside, at]
                out[:levels, two, :] = state[:, behind, at]
                out[levels + half, one : one + 1, :] = wet[beside : beside + 1, at]
                out[levels + half, two : two + 1, :] = wet[behind : behind + 1, at]
                out[levels : levels + half, c, :] = vert[:half, beside, at]
                out[levels : levels + half - 1, cols + c, :] = vert[half:, beside, at]
                out[levels + half - 1, cols + c : cols + c + 1, :] = jnp.zeros((1, 128), jnp.float32)
                for row in (c, cols + c):
                    out[levels + half + 1, row : row + 1, :] = horiz[beside : beside + 1, at]

    even = lax.axis_index("tile") % 2 == 0
    pl.when(even)(lambda: fill(core, chip))
    pl.when(jnp.logical_not(even))(lambda: fill(chip, core))


def side_weights(horiz, wet):
    height, width = wet.shape
    column = iota((height, width), 1)
    left = jnp.where(column == 0, 0.0, pltpu.roll(wet, 1, 1))
    right = jnp.where(column == width - 1, 0.0, pltpu.roll(wet, width - 1, 1))
    return horiz * wet * left, horiz * wet * right


def weights_of(tiles, groups, horiz, wet, wet_above, wet_below):
    height, width = wet.shape
    device = lax.axis_index("grp") * tiles + lax.axis_index("tile")
    rows = device * height + iota((height, width), 0)
    start = (groups - 1) * tiles * height
    last = groups * tiles * height - 1
    above = jnp.concatenate([wet_above, wet[:-1]], 0)
    below = jnp.concatenate([wet[1:], wet_below], 0)
    above = jnp.where((rows > 0) & (rows != start), above, 0.0)
    below = jnp.where((rows < last) & (rows + 1 != start), below, 0.0)
    scale = horiz * wet
    return side_weights(horiz, wet) + (scale * above, scale * below)


def line_of(halo, first, cols):
    return jnp.concatenate([halo[first + c : first + c + 1, :] for c in range(cols)], 1)


def row_above(field, halo):
    return jnp.concatenate([line_of(halo, 0, field.shape[1] // 128), field[:-1]], 0)


def row_below(field, halo):
    cols = field.shape[1] // 128
    return jnp.concatenate([field[1:], line_of(halo, cols, cols)], 0)


def around(field, halo):
    width = field.shape[1]
    return (
        pltpu.roll(field, 1, 1),
        pltpu.roll(field, width - 1, 1),
        row_above(field, halo),
        row_below(field, halo),
    )


def stencil(field, halo, weights):
    total = field
    for other, weight in zip(around(field, halo), weights):
        total = total + weight * (other - field)
    return total


def shifted(halo, lane):
    rows = halo.shape[0]
    to_right, to_left = pltpu.roll(halo, 1, 1), pltpu.roll(halo, 127, 1)
    return (
        jnp.where(lane == 0, pltpu.roll(to_right, 1, 0), to_right),
        jnp.where(lane == 127, pltpu.roll(to_left, rows - 1, 0), to_left),
    )


def inverse_of(x):
    y = pl.reciprocal(x, approx=True)
    return y * (2.0 - x * y)


def early_kernel(
    groups, vert, horiz, mask, chunk, upper, gain, ratio, impulse, sides, chunk_out, sem
):
    levels, height, width = upper.shape
    copy = pltpu.make_async_copy(chunk, chunk_out, sem)
    copy.start()
    wet = wet_of(lax.axis_index("grp") == groups - 1, mask[...])
    weights = side_weights(horiz[...], wet)
    zero = jnp.zeros((height, width), jnp.float32)

    def forward(level, carry, last=False, first=False):
        low, c, e = carry
        upp = zero if last else vert[level] * wet
        inverse = inverse_of(1.0 + low + upp + low * c)
        c = -upp * inverse
        step = low * inverse
        e = inverse if first else step * e
        upper[level] = c
        gain[level] = inverse
        ratio[level] = step
        impulse[level] = e
        return upp, c, e

    carry = forward(0, (zero,) * 3, first=True)
    carry = lax.fori_loop(1, levels - 1, forward, carry, unroll=31)
    _, _, e = forward(levels - 1, carry, last=True)

    def backward(i, x):
        level = levels - 2 - i
        x = impulse[level] - upper[level] * x
        impulse[level] = x
        return x

    lax.fori_loop(0, levels - 1, backward, e, unroll=9)

    def forward_parts(level, carry):
        g = impulse[level]
        rhs = (weights[0] * pltpu.roll(g, 1, 1), weights[1] * pltpu.roll(g, width - 1, 1))
        inverse, step = gain[level], ratio[level]
        made = tuple(x * inverse + step * r for x, r in zip(rhs, carry))
        for i in range(2):
            sides[i, level] = made[i]
        return made

    carry = lax.fori_loop(0, levels, forward_parts, (zero,) * 2, unroll=8)
    back_parts(sides, upper, carry)
    copy.wait()


def back_parts(parts, upper, carry):
    count, levels = parts.shape[:2]

    def backward(i, carry):
        level = levels - 2 - i
        c = upper[level]
        made = tuple(parts[j, level] - c * carry[j] for j in range(count))
        for j in range(count):
            parts[j, level] = made[j]
        return made

    lax.fori_loop(0, levels - 1, backward, carry, unroll=9)


def late_kernel(
    tiles, groups, state, horiz, mask, chip, core, upper, gain, ratio, impulse, _, parts, halo_wet,
    base, halo_base, halo_impulse, halo_vert, halo_upper, rim,
):
    levels, height, width = state.shape
    cols = width // 128
    half = levels // 2
    shape = (2 * cols, 128)
    low_half = iota(shape, 0) < cols
    lane = iota(shape, 1)
    parity = lax.axis_index("tile") % 2
    from_chip = iota(shape, 0) // cols == parity

    def turn(x):
        return pltpu.roll(x, cols, 0)

    def beside(i):
        return jnp.where(from_chip, chip[i], core[i])

    def behind(i):
        return turn(jnp.where(from_chip, core[i], chip[i]))

    for c in range(cols):
        rim[:, c, :] = state[:, 0, c * 128 : (c + 1) * 128]
        rim[:, cols + c, :] = state[:, height - 1, c * 128 : (c + 1) * 128]
    wet = wet_of(lax.axis_index("grp") == groups - 1, mask[...])
    wet_halo = beside(levels + half)
    halo_wet[...] = wet_halo
    weights = weights_of(
        tiles, groups, horiz[...], wet, line_of(wet_halo, 0, cols), line_of(wet_halo, cols, cols)
    )
    scale = beside(levels + half + 1) * wet_halo
    wet_left, wet_right = shifted(wet_halo, lane)
    place = iota(shape, 0) % cols
    weight_left = scale * jnp.where((place == 0) & (lane == 0), 0.0, wet_left)
    weight_right = scale * jnp.where((place == cols - 1) & (lane == 127), 0.0, wet_right)
    weight_behind = scale * behind(levels + half)
    wet_inside = [wet[r : r + 1, c * 128 : (c + 1) * 128] for r in (0, height - 1) for c in range(cols)]
    weight_inside = scale * jnp.concatenate(wet_inside, 0)

    def spread(i, _):
        x, y = chip[levels + i], core[levels + i]
        a, b = jnp.where(parity == 0, x, y), jnp.where(parity == 0, y, x)
        halo_vert[i] = jnp.where(low_half, a, turn(b)) * wet_halo
        halo_vert[half + i] = jnp.where(low_half, turn(a), b) * wet_halo
        return 0

    lax.fori_loop(0, half, spread, 0, unroll=4)
    zero = jnp.zeros((height, width), jnp.float32)
    zero_halo = jnp.zeros(shape, jnp.float32)

    def forward(level, carry, last=False, first=False):
        r, low, c, x, e = carry
        halo = beside(level)
        r = stencil(state[level], halo, weights) * gain[level] + ratio[level] * r
        base[level] = r
        upp = zero_halo if last else halo_vert[level]
        inverse = inverse_of(1.0 + low + upp + low * c)
        c = -upp * inverse
        step = low * inverse
        left, right = shifted(halo, lane)
        field = (
            halo
            + weight_left * (left - halo)
            + weight_right * (right - halo)
            + weight_behind * (behind(level) - halo)
            + weight_inside * (rim[level] - halo)
        )
        x = field * inverse + step * x
        e = inverse if first else step * e
        halo_upper[level] = c
        halo_base[level] = x
        halo_impulse[level] = e
        return r, upp, c, x, e

    carry = forward(0, (zero,) + (zero_halo,) * 4, first=True)
    carry = lax.fori_loop(1, levels - 1, forward, carry, unroll=31)
    r, _, _, x, e = forward(levels - 1, carry, last=True)

    def backward(i, carry):
        level = levels - 2 - i
        c = halo_upper[level]
        r = base[level] - upper[level] * carry[0]
        x = halo_base[level] - c * carry[1]
        e = halo_impulse[level] - c * carry[2]
        base[level] = r
        halo_base[level] = x
        halo_impulse[level] = e
        return r, x, e

    lax.fori_loop(0, levels - 1, backward, (r, x, e), unroll=9)
    rest = 1.0 - weights[0] - weights[1] - weights[2] - weights[3]

    def forward_parts(level, carry, first=False):
        g, halo = impulse[level], halo_impulse[level]
        rhs = (
            stencil(base[level], halo_base[level], weights),
            rest * g + (1.0 if first else 0.0),
            weights[2] * row_above(g, halo),
            weights[3] * row_below(g, halo),
        )
        inverse, step = gain[level], ratio[level]
        made = tuple(x * inverse + step * r for x, r in zip(rhs, carry))
        for i in range(4):
            parts[i, level] = made[i]
        return made

    carry = forward_parts(0, (zero,) * 4, first=True)
    carry = lax.fori_loop(1, levels, forward_parts, carry, unroll=7)
    back_parts(parts, upper, carry)


def last_kernel(cols, groups, mask, sides, parts, halo_wet, *refs):
    arrived = refs[: groups - 1]
    out, received, field, sem = refs[groups - 1 :]
    _, levels, height, width = parts.shape
    group = lax.axis_index("grp")
    total = jnp.zeros(arrived[0].shape, jnp.float32)
    for g, other in enumerate(arrived):
        total = total + jnp.where((group == groups - 1) | (group == g), other[...], 0.0)
    for f in range(F):
        for c in range(cols):
            at = (f * cols + c) * height
            received[f, :, c * 128 : (c + 1) * 128] = total[at : at + height, :]
    wet = wet_of(lax.axis_index("grp") == groups - 1, mask[...])
    force = FORCING_GAIN * wet * jnp.sum(received[...], 0)
    force_halo = FORCING_GAIN * halo_wet[...] * total[F * cols * height :, :]
    left, right, above, below = around(force, force_halo)

    def level_of(level, _):
        x = parts[0, level] + parts[1, level] * force
        x = x + parts[2, level] * above + parts[3, level] * below
        field[level] = x + sides[0, level] * left + sides[1, level] * right
        return 0

    chunks = 4
    size = levels // chunks
    copies = []
    for i in range(chunks):
        lax.fori_loop(i * size, (i + 1) * size, level_of, 0, unroll=4)
        at = pl.ds(i * size, size)
        copies.append(pltpu.make_async_copy(field.at[at], out.at[at], sem.at[i]))
        copies[-1].start()
    for copy in copies:
        copy.wait()


def f32(*shape):
    return jax.ShapeDtypeStruct(shape, jnp.float32)


def cost(us):
    return pl.CostEstimate(flops=0, bytes_accessed=int(us * 3e6), transcendentals=0)


def edges_of(groups, state, vert_coef, horiz_coef, wet_mask, after):
    levels, height, width = state.shape
    return pl.pallas_call(
        functools.partial(edge_kernel, groups),
        out_shape=(f32(levels + levels // 2 + 2, width // 64, 128),) * 2,
        in_specs=[VM] * 4 + [HBM],
        compiler_params=params(8),
        cost_estimate=cost(1),
    )(state, vert_coef, horiz_coef, wet_mask, after)


def pack(groups, tiles, slots, state, coupling, surface, mask, dtile, dblock, dgroup, w):
    height, width = mask.shape
    cols = width // 128
    blocks = height * cols
    return pl.pallas_call(
        functools.partial(pack_kernel, tiles, slots, groups),
        out_shape=(f32(2 * (F * slots + 16), 128),) * (tiles // 2),
        in_specs=[HBM] * 8,
        scratch_shapes=[
            pltpu.VMEM((blocks * K, F * 128), jnp.float32),
            pltpu.VMEM((cols, height, K, 128, 128), jnp.bfloat16),
        ]
        + [pltpu.VMEM((K, blocks), jnp.int32)] * 3
        + [pltpu.VMEM((height, width), jnp.float32)]
        + [pltpu.VMEM((F, height, width), jnp.float32)] * 2
        + [
            pltpu.VMEM((height, width), jnp.int32),
            pltpu.SemaphoreType.DMA((cols,)),
            pltpu.SemaphoreType.DMA((7,)),
        ],
        compiler_params=params(60),
        cost_estimate=cost(3),
    )(state, coupling, surface, mask, dtile.T, dblock.T, dgroup.T, w.reshape(height, cols, K, 128, 128))


def early(groups, vert_coef, horiz_coef, wet_mask, chunk):
    levels, height, width = vert_coef.shape
    full = f32(levels + 1, height, width)
    return pl.pallas_call(
        functools.partial(early_kernel, groups),
        out_shape=(full,) * 4 + (f32(2, levels + 1, height, width), f32(*chunk.shape)),
        in_specs=[VM] * 3 + [HBM],
        scratch_shapes=[pltpu.SemaphoreType.DMA],
        compiler_params=params(16),
        cost_estimate=cost(3),
    )(vert_coef, horiz_coef, wet_mask, chunk)


def late(groups, tiles, state, horiz_coef, wet_mask, chip, core, solved, after):
    levels, height, width = state.shape
    full, halo = f32(levels, height, width), f32(levels, width // 64, 128)
    return pl.pallas_call(
        functools.partial(late_kernel, tiles, groups),
        out_shape=(f32(4, levels, height, width), f32(width // 64, 128)),
        in_specs=[VM] * 10,
        scratch_shapes=[pltpu.VMEM(s.shape, jnp.float32) for s in [full] + [halo] * 5],
        compiler_params=params(16),
        cost_estimate=cost(4),
    )(state, horiz_coef, wet_mask, chip, core, *solved, after)


def finish(groups, wet_mask, sides, parts, halo_wet, arrived):
    _, levels, height, width = parts.shape
    return pl.pallas_call(
        functools.partial(last_kernel, width // 128, groups),
        out_shape=(f32(levels, height, width), f32(F, height, width)),
        out_specs=(HBM, VM),
        scratch_shapes=[
            pltpu.VMEM((levels, height, width), jnp.float32),
            pltpu.SemaphoreType.DMA((4,)),
        ],
        compiler_params=params(16),
    )(wet_mask, sides, parts, halo_wet, *arrived)


def local(
    state, vert_coef, horiz_coef, wet_mask, coupling, surface_in, remap_w, dest_tile, dest_block, dest_group
):
    levels, height, width = state.shape
    groups, tiles = lax.axis_size("grp"), lax.axis_size("tile")
    cols = width // 128
    blocks = height * cols
    slots = max(8, 2 * blocks * K // tiles)
    rim = 2 * cols
    devices = groups * tiles
    start = (groups - 1) * tiles
    axes = ("grp", "tile")
    across = [(i, i + 1) for i in range(1, devices - 1, 2) if i + 1 != start]
    across = across + [(j, i) for i, j in across]
    packed = pack(
        groups, tiles, slots, state, coupling, surface_in, wet_mask, dest_tile, dest_block, dest_group, remap_w
    )
    chips = tiles // 2
    moved = {
        k: lax.ppermute(packed[k], "tile", [(i, ((i // 2) ^ k) * 2 + i % 2) for i in range(tiles)])
        for k in sorted(range(1, chips), key=lambda k: (k != chips // 2, k))
    }
    got = [moved[k] for k in range(1, chips)]
    *solved, sides, chunk = early(groups, vert_coef, horiz_coef, wet_mask, packed[0])
    chip, core = edges_of(groups, state, vert_coef, horiz_coef, wet_mask, chunk)
    chip = lax.ppermute(chip, axes, across)
    core = lax.ppermute(core, axes, [(i, i ^ 1) for i in range(devices)])
    rows = (groups - 1) * (F * blocks + rim)
    mine, theirs = pl.pallas_call(
        functools.partial(merge_kernel, slots, height, cols, groups),
        out_shape=(f32(rows, 128),) * 2,
        compiler_params=params(8),
        cost_estimate=cost(1),
    )(chunk, *got)
    theirs = lax.ppermute(theirs, "tile", [(i, i ^ 1) for i in range(tiles)])
    merged = pl.pallas_call(
        functools.partial(add_kernel, cols),
        out_shape=(f32(F * blocks + rim, 128),) * (groups - 1),
        compiler_params=params(8),
        cost_estimate=cost(1),
    )(mine, theirs)
    arrived = [
        lax.ppermute(merged[g], "grp", [(j, (j + g + 1) % groups) for j in range(groups)])
        for g in range(groups - 1)
    ]
    parts, halo_wet = late(groups, tiles, state, horiz_coef, wet_mask, chip, core, solved, merged[0])
    return finish(groups, wet_mask, sides, parts, halo_wet, arrived)


def solution(mesh):
    in_specs = (
        P(None, ("grp", "tile"), None),
        P(None, ("grp", "tile"), None),
        P(("grp", "tile"), None),
        P("tile", None),
        P(None, ("grp", "tile"), None),
        P(None, ("grp", "tile"), None),
        P(("grp", "tile"), None, None, None),
        P(("grp", "tile"), None),
        P(("grp", "tile"), None),
        P(("grp", "tile"), None),
    )
    out_specs = (P(None, ("grp", "tile"), None), P(None, ("grp", "tile"), None))
    return jax.shard_map(local, mesh=mesh, in_specs=in_specs, out_specs=out_specs, check_vma=False)
```

```python
import functools

import jax
import jax.numpy as jnp
from jax import lax
from jax.experimental import pallas as pl
from jax.experimental.pallas import tpu as pltpu
from jax.sharding import PartitionSpec as P

F = 4
K = 4
FORCING_GAIN = 0.25
VM = pl.BlockSpec(memory_space=pltpu.VMEM)
HBM = pl.BlockSpec(memory_space=pltpu.HBM)
MIB = 1024 * 1024


def params(mib):
    return pltpu.CompilerParams(vmem_limit_bytes=mib * MIB)


def split(x):
    hi = x.astype(jnp.bfloat16)
    return hi, (x - hi.astype(jnp.float32)).astype(jnp.bfloat16)


def wet_of(ocean, mask):
    return jnp.where(ocean, mask.astype(jnp.float32), 1.0)


def iota(shape, dim):
    return lax.broadcasted_iota(jnp.int32, shape, dim)


def pack_kernel(
    tiles, slots, groups, state, coupling, surface, mask, dtile, dblock, dgroup, w, *refs
):
    outs = refs[: tiles // 2]
    terms, w_here, *here, w_sem, sem = refs[tiles // 2 :]
    height, width = mask.shape
    cols = width // 128
    given = (dtile, dblock, dgroup, state.at[0], coupling, surface, mask)
    small = [pltpu.make_async_copy(a, b, sem.at[i]) for i, (a, b) in enumerate(zip(given, here))]
    large = [pltpu.make_async_copy(w.at[:, c], w_here.at[c], w_sem.at[c]) for c in range(cols)]
    for copy in small + large:
        copy.start()
    dtile, dblock, dgroup, state, coupling, surface, mask = here
    for copy in small[:3]:
        copy.wait()
    blocks = height * cols
    count = blocks * K
    ocean = lax.axis_index("grp") == groups - 1
    me = lax.axis_index("tile")

    block = dblock[...]
    line = block // cols
    col = block % cols
    group = jnp.where(ocean, dgroup[...], groups - 1)
    code = dtile[...] * 128 + col * height + line + jnp.where(ocean, dgroup[...] * blocks, 0)
    device = group * tiles + dtile[...]
    low = jnp.where(ocean, 0, (groups - 1) * tiles)
    high = jnp.where(ocean, (groups - 1) * tiles, groups * tiles)
    odd = device % 2 == 1
    beside = jnp.where(odd, device + 1, device - 1)
    reads = (line == jnp.where(odd, height - 1, 0)) & (beside >= low) & (beside < high)
    edge = (beside % tiles) * 16 + col + jnp.where(ocean, (beside // tiles) * cols, 0)
    edge = jnp.where(reads, edge, -1)

    item = iota((count, blocks), 0)
    item_k = (item // height) % K
    own = iota((count, blocks), 1) == (item % height) * cols + item // (height * K)
    up, down = iota((count, count), 0), iota((count, count), 1)

    def column(values):
        spread = jnp.broadcast_to(values[:1, :], (count, blocks))
        for k in range(1, K):
            spread = jnp.where(item_k == k, values[k : k + 1, :], spread)
        return jnp.sum(jnp.where(own, spread, 0), 1, keepdims=True)

    def turned(values):
        return jnp.sum(jnp.where(up == down, values, 0), 0, keepdims=True)

    def place_of(tile):
        return ((tile // 2) ^ (me // 2)) * 2 + tile % 2

    code_col, edge_row = column(code), turned(column(edge))
    code_row = turned(code_col)
    tile_row, tile_col, tag_col = code_row // 128, code_col // 128, code_col % 128
    same = tile_row == tile_col
    slot_row = jnp.sum(jnp.where(same & (up < down), 1, 0), 0, keepdims=True)
    slot_col = jnp.sum(jnp.where(same & (down < up), 1, 0), 1, keepdims=True)
    place_row, place_col = place_of(tile_row), place_of(tile_col)
    chooser = jnp.where(
        iota((tiles * slots, count), 0) == place_row * slots + slot_row, 1.0, 0.0
    ).astype(jnp.bfloat16)
    to_tile = jnp.where(iota((tiles, count), 0) == place_row, 1.0, 0.0).astype(jnp.bfloat16)
    labels = jnp.where(
        iota((count, 128), 1) == (place_col // 2) * slots + slot_col,
        (tag_col + 1).astype(jnp.float32),
        0.0,
    ).astype(jnp.bfloat16)
    tags = jnp.dot(to_tile, labels, preferred_element_type=jnp.float32)
    rim = cols * (groups - 1)
    rim_id = iota((tiles * 16, count), 0)
    rim_place, rim_id = rim_id // 16, rim_id % 16
    rim_tile = ((rim_place // 2) ^ (me // 2)) * 2 + rim_place % 2
    rim_id = jnp.where(
        rim_id < rim, rim_tile * 16 + jnp.where(ocean, rim_id, rim_id % cols), -2
    )
    rim_chooser = jnp.where(rim_id == edge_row, 1.0, 0.0).astype(jnp.bfloat16)

    for copy in small[3:]:
        copy.wait()
    send = coupling[...] * (state[...][None] - surface[...]) * wet_of(ocean, mask[...])[None]
    row_of = iota((F * height, 128), 0) % height
    for c in range(cols):
        piece = send[:, :, c * 128 : (c + 1) * 128].reshape(F * height, 128)
        left = jnp.concatenate(
            [jnp.where(row_of == r, piece, 0.0).astype(jnp.bfloat16) for r in range(height)], 1
        )
        large[c].wait()
        for k in range(K):
            right = w_here[c, :, k].reshape(height * 128, 128)
            made = jnp.dot(left, right, preferred_element_type=jnp.float32)
            at = (c * K + k) * height
            for f in range(F):
                terms[at : at + height, f * 128 : (f + 1) * 128] = made[
                    f * height : (f + 1) * height, :
                ]
    total = terms[:, :128]
    for f in range(1, F):
        total = total + terms[:, f * 128 : (f + 1) * 128]
    hi, lo = split(terms[...])
    packed = jnp.dot(
        jnp.concatenate([chooser, chooser], 1),
        jnp.concatenate([hi, lo], 0),
        preferred_element_type=jnp.float32,
    )
    hi, lo = split(total)
    rims = jnp.dot(
        jnp.concatenate([rim_chooser, rim_chooser], 1),
        jnp.concatenate([hi, lo], 0),
        preferred_element_type=jnp.float32,
    )
    size = F * slots + 16
    for t in range(tiles):
        out, at = outs[t // 2], (t % 2) * size
        for f in range(F):
            out[at + f * slots : at + (f + 1) * slots, :] = packed[
                t * slots : (t + 1) * slots, f * 128 : (f + 1) * 128
            ]
        at = at + F * slots
        out[at : at + 16, :] = rims[t * 16 : (t + 1) * 16, :]
        out[at + rim : at + rim + 1, :] = tags[t : t + 1, :]


def merge_kernel(slots, height, cols, groups, *refs):
    got, (mine, theirs) = refs[:-2], refs[-2:]
    blocks = height * cols
    size = F * slots + 16
    rim = cols * (groups - 1)
    rows = (groups - 1) * blocks
    ocean = lax.axis_index("grp") == groups - 1
    core = lax.axis_index("tile") % 2
    ids = iota((rows, 128), 0)
    ids = jnp.where(ocean, ids, ids % blocks) + 1

    def merged(which, out):
        first = which * size
        tail = got[0][pl.ds(first + F * slots, 16), :]
        for chunk in got[1:]:
            tail = tail + chunk[pl.ds(first + F * slots, 16), :]
        label = tail[rim : rim + 1, :].astype(jnp.int32)
        chooser = jnp.where(ids == label, 1.0, 0.0).astype(jnp.bfloat16)
        chooser = jnp.concatenate([chooser, chooser], 1)
        total = jnp.zeros((rows, 128), jnp.float32)
        for f in range(F):
            data = jnp.concatenate([chunk[pl.ds(first + f * slots, slots), :] for chunk in got], 0)
            hi, lo = split(data)
            part = jnp.dot(chooser, jnp.concatenate([hi, lo], 0), preferred_element_type=jnp.float32)
            total = total + part
            for g in range(groups - 1):
                at = (g * F + f) * blocks
                out[at : at + blocks, :] = part[g * blocks : (g + 1) * blocks, :]
        out[rows * F : rows * F + rim, :] = tail[:rim, :]
        return total.reshape(rim, height, 128)

    own = merged(core, mine)
    sibling = merged(1 - core, theirs)
    even = core == 0
    at = rows * F + rim
    theirs[at : at + rim, :] = jnp.where(even, own[:, height - 1, :], own[:, 0, :])
    mine[at : at + rim, :] = jnp.where(even, sibling[:, 0, :], sibling[:, height - 1, :])


def add_kernel(cols, mine, theirs, *outs):
    even = lax.axis_index("tile") % 2 == 0
    rows = outs[0].shape[0] - 2 * cols
    groups = len(outs)
    tail = groups * rows
    rims = mine[tail:, :] + theirs[tail:, :]
    for g, out in enumerate(outs):
        out[:rows, :] = mine[g * rows : (g + 1) * rows, :] + theirs[g * rows : (g + 1) * rows, :]
        far = rims[g * cols : (g + 1) * cols, :]
        near = rims[(groups + g) * cols : (groups + g + 1) * cols, :]
        out[rows : rows + cols, :] = jnp.where(even, far, near)
        out[rows + cols :, :] = jnp.where(even, near, far)


def edge_kernel(groups, state, vert, horiz, mask, *refs):
    chip, core = refs[-2:]
    levels, height, width = state.shape
    half = levels // 2
    cols = width // 128
    last = height - 1
    wet = wet_of(lax.axis_index("grp") == groups - 1, mask[...])

    def fill(down, up):
        for c in range(cols):
            at = slice(c * 128, (c + 1) * 128)
            for out, beside, behind, one, two in (
                (down, last, last - 1, c, cols + c),
                (up, 0, 1, cols + c, c),
            ):
                out[:levels, one, :] = state[:, beside, at]
                out[:levels, two, :] = state[:, behind, at]
                out[levels + half, one : one + 1, :] = wet[beside : beside + 1, at]
                out[levels + half, two : two + 1, :] = wet[behind : behind + 1, at]
                out[levels : levels + half, c, :] = vert[:half, beside, at]
                out[levels : levels + half - 1, cols + c, :] = vert[half:, beside, at]
                out[levels + half - 1, cols + c : cols + c + 1, :] = jnp.zeros((1, 128), jnp.float32)
                for row in (c, cols + c):
                    out[levels + half + 1, row : row + 1, :] = horiz[beside : beside + 1, at]

    even = lax.axis_index("tile") % 2 == 0
    pl.when(even)(lambda: fill(core, chip))
    pl.when(jnp.logical_not(even))(lambda: fill(chip, core))


def side_weights(horiz, wet):
    height, width = wet.shape
    column = iota((height, width), 1)
    left = jnp.where(column == 0, 0.0, pltpu.roll(wet, 1, 1))
    right = jnp.where(column == width - 1, 0.0, pltpu.roll(wet, width - 1, 1))
    return horiz * wet * left, horiz * wet * right


def weights_of(tiles, groups, horiz, wet, wet_above, wet_below):
    height, width = wet.shape
    device = lax.axis_index("grp") * tiles + lax.axis_index("tile")
    rows = device * height + iota((height, width), 0)
    start = (groups - 1) * tiles * height
    last = groups * tiles * height - 1
    above = jnp.concatenate([wet_above, wet[:-1]], 0)
    below = jnp.concatenate([wet[1:], wet_below], 0)
    above = jnp.where((rows > 0) & (rows != start), above, 0.0)
    below = jnp.where((rows < last) & (rows + 1 != start), below, 0.0)
    scale = horiz * wet
    return side_weights(horiz, wet) + (scale * above, scale * below)


def line_of(halo, first, cols):
    return jnp.concatenate([halo[first + c : first + c + 1, :] for c in range(cols)], 1)


def row_above(field, halo):
    return jnp.concatenate([line_of(halo, 0, field.shape[1] // 128), field[:-1]], 0)


def row_below(field, halo):
    cols = field.shape[1] // 128
    return jnp.concatenate([field[1:], line_of(halo, cols, cols)], 0)


def around(field, halo):
    width = field.shape[1]
    return (
        pltpu.roll(field, 1, 1),
        pltpu.roll(field, width - 1, 1),
        row_above(field, halo),
        row_below(field, halo),
    )


def stencil(field, halo, weights):
    total = field
    for other, weight in zip(around(field, halo), weights):
        total = total + weight * (other - field)
    return total


def shifted(halo, lane):
    rows = halo.shape[0]
    to_right, to_left = pltpu.roll(halo, 1, 1), pltpu.roll(halo, 127, 1)
    return (
        jnp.where(lane == 0, pltpu.roll(to_right, 1, 0), to_right),
        jnp.where(lane == 127, pltpu.roll(to_left, rows - 1, 0), to_left),
    )


def inverse_of(x):
    y = pl.reciprocal(x, approx=True)
    return y * (2.0 - x * y)


def early_kernel(
    groups, vert, horiz, mask, chunk, upper, gain, ratio, impulse, sides, chunk_out, sem
):
    levels, height, width = upper.shape
    copy = pltpu.make_async_copy(chunk, chunk_out, sem)
    copy.start()
    wet = wet_of(lax.axis_index("grp") == groups - 1, mask[...])
    weights = side_weights(horiz[...], wet)
    zero = jnp.zeros((height, width), jnp.float32)

    def forward(level, carry, last=False, first=False):
        low, c, e = carry
        upp = zero if last else vert[level] * wet
        inverse = inverse_of(1.0 + low + upp + low * c)
        c = -upp * inverse
        step = low * inverse
        e = inverse if first else step * e
        upper[level] = c
        gain[level] = inverse
        ratio[level] = step
        impulse[level] = e
        return upp, c, e

    carry = forward(0, (zero,) * 3, first=True)
    carry = lax.fori_loop(1, levels - 1, forward, carry, unroll=31)
    _, _, e = forward(levels - 1, carry, last=True)

    def backward(i, x):
        level = levels - 2 - i
        x = impulse[level] - upper[level] * x
        impulse[level] = x
        return x

    lax.fori_loop(0, levels - 1, backward, e, unroll=9)

    def forward_parts(level, carry):
        g = impulse[level]
        rhs = (weights[0] * pltpu.roll(g, 1, 1), weights[1] * pltpu.roll(g, width - 1, 1))
        inverse, step = gain[level], ratio[level]
        made = tuple(x * inverse + step * r for x, r in zip(rhs, carry))
        for i in range(2):
            sides[i, level] = made[i]
        return made

    carry = lax.fori_loop(0, levels, forward_parts, (zero,) * 2, unroll=8)
    back_parts(sides, upper, carry)
    copy.wait()


def back_parts(parts, upper, carry):
    count, levels = parts.shape[:2]

    def backward(i, carry):
        level = levels - 2 - i
        c = upper[level]
        made = tuple(parts[j, level] - c * carry[j] for j in range(count))
        for j in range(count):
            parts[j, level] = made[j]
        return made

    lax.fori_loop(0, levels - 1, backward, carry, unroll=9)


def late_kernel(
    tiles, groups, state, horiz, mask, chip, core, upper, gain, ratio, impulse, _, parts, halo_wet,
    base, halo_base, halo_impulse, halo_vert, halo_upper, rim,
):
    levels, height, width = state.shape
    cols = width // 128
    half = levels // 2
    shape = (2 * cols, 128)
    low_half = iota(shape, 0) < cols
    lane = iota(shape, 1)
    parity = lax.axis_index("tile") % 2
    from_chip = iota(shape, 0) // cols == parity

    def turn(x):
        return pltpu.roll(x, cols, 0)

    def beside(i):
        return jnp.where(from_chip, chip[i], core[i])

    def behind(i):
        return turn(jnp.where(from_chip, core[i], chip[i]))

    for c in range(cols):
        rim[:, c, :] = state[:, 0, c * 128 : (c + 1) * 128]
        rim[:, cols + c, :] = state[:, height - 1, c * 128 : (c + 1) * 128]
    wet = wet_of(lax.axis_index("grp") == groups - 1, mask[...])
    wet_halo = beside(levels + half)
    halo_wet[...] = wet_halo
    weights = weights_of(
        tiles, groups, horiz[...], wet, line_of(wet_halo, 0, cols), line_of(wet_halo, cols, cols)
    )
    scale = beside(levels + half + 1) * wet_halo
    wet_left, wet_right = shifted(wet_halo, lane)
    place = iota(shape, 0) % cols
    weight_left = scale * jnp.where((place == 0) & (lane == 0), 0.0, wet_left)
    weight_right = scale * jnp.where((place == cols - 1) & (lane == 127), 0.0, wet_right)
    weight_behind = scale * behind(levels + half)
    wet_inside = [wet[r : r + 1, c * 128 : (c + 1) * 128] for r in (0, height - 1) for c in range(cols)]
    weight_inside = scale * jnp.concatenate(wet_inside, 0)

    def spread(i, _):
        x, y = chip[levels + i], core[levels + i]
        a, b = jnp.where(parity == 0, x, y), jnp.where(parity == 0, y, x)
        halo_vert[i] = jnp.where(low_half, a, turn(b)) * wet_halo
        halo_vert[half + i] = jnp.where(low_half, turn(a), b) * wet_halo
        return 0

    lax.fori_loop(0, half, spread, 0, unroll=4)
    zero = jnp.zeros((height, width), jnp.float32)
    zero_halo = jnp.zeros(shape, jnp.float32)

    def forward(level, carry, last=False, first=False):
        r, low, c, x, e = carry
        halo = beside(level)
        r = stencil(state[level], halo, weights) * gain[level] + ratio[level] * r
        base[level] = r
        upp = zero_halo if last else halo_vert[level]
        inverse = inverse_of(1.0 + low + upp + low * c)
        c = -upp * inverse
        step = low * inverse
        left, right = shifted(halo, lane)
        field = (
            halo
            + weight_left * (left - halo)
            + weight_right * (right - halo)
            + weight_behind * (behind(level) - halo)
            + weight_inside * (rim[level] - halo)
        )
        x = field * inverse + step * x
        e = inverse if first else step * e
        halo_upper[level] = c
        halo_base[level] = x
        halo_impulse[level] = e
        return r, upp, c, x, e

    carry = forward(0, (zero,) + (zero_halo,) * 4, first=True)
    carry = lax.fori_loop(1, levels - 1, forward, carry, unroll=31)
    r, _, _, x, e = forward(levels - 1, carry, last=True)

    def backward(i, carry):
        level = levels - 2 - i
        c = halo_upper[level]
        r = base[level] - upper[level] * carry[0]
        x = halo_base[level] - c * carry[1]
        e = halo_impulse[level] - c * carry[2]
        base[level] = r
        halo_base[level] = x
        halo_impulse[level] = e
        return r, x, e

    lax.fori_loop(0, levels - 1, backward, (r, x, e), unroll=9)
    rest = 1.0 - weights[0] - weights[1] - weights[2] - weights[3]

    def forward_parts(level, carry, first=False):
        g, halo = impulse[level], halo_impulse[level]
        rhs = (
            stencil(base[level], halo_base[level], weights),
            rest * g + (1.0 if first else 0.0),
            weights[2] * row_above(g, halo),
            weights[3] * row_below(g, halo),
        )
        inverse, step = gain[level], ratio[level]
        made = tuple(x * inverse + step * r for x, r in zip(rhs, carry))
        for i in range(4):
            parts[i, level] = made[i]
        return made

    carry = forward_parts(0, (zero,) * 4, first=True)
    carry = lax.fori_loop(1, levels, forward_parts, carry, unroll=7)
    back_parts(parts, upper, carry)


def last_kernel(cols, groups, mask, sides, parts, halo_wet, *refs):
    arrived = refs[: groups - 1]
    out, received, field, sem = refs[groups - 1 :]
    _, levels, height, width = parts.shape
    group = lax.axis_index("grp")
    total = jnp.zeros(arrived[0].shape, jnp.float32)
    for g, other in enumerate(arrived):
        total = total + jnp.where((group == groups - 1) | (group == g), other[...], 0.0)
    for f in range(F):
        for c in range(cols):
            at = (f * cols + c) * height
            received[f, :, c * 128 : (c + 1) * 128] = total[at : at + height, :]
    wet = wet_of(lax.axis_index("grp") == groups - 1, mask[...])
    force = FORCING_GAIN * wet * jnp.sum(received[...], 0)
    force_halo = FORCING_GAIN * halo_wet[...] * total[F * cols * height :, :]
    left, right, above, below = around(force, force_halo)

    def level_of(level, _):
        x = parts[0, level] + parts[1, level] * force
        x = x + parts[2, level] * above + parts[3, level] * below
        field[level] = x + sides[0, level] * left + sides[1, level] * right
        return 0

    chunks = 4
    size = levels // chunks
    copies = []
    for i in range(chunks):
        lax.fori_loop(i * size, (i + 1) * size, level_of, 0, unroll=4)
        at = pl.ds(i * size, size)
        copies.append(pltpu.make_async_copy(field.at[at], out.at[at], sem.at[i]))
        copies[-1].start()
    for copy in copies:
        copy.wait()


def f32(*shape):
    return jax.ShapeDtypeStruct(shape, jnp.float32)


def cost(us):
    return pl.CostEstimate(flops=0, bytes_accessed=int(us * 3e6), transcendentals=0)


def edges_of(groups, state, vert_coef, horiz_coef, wet_mask, *after):
    levels, height, width = state.shape
    return pl.pallas_call(
        functools.partial(edge_kernel, groups),
        out_shape=(f32(levels + levels // 2 + 2, width // 64, 128),) * 2,
        in_specs=[VM] * 4 + [HBM] * len(after),
        compiler_params=params(8),
        cost_estimate=cost(1),
    )(state, vert_coef, horiz_coef, wet_mask, *after)


def pack(groups, tiles, slots, state, coupling, surface, mask, dtile, dblock, dgroup, w):
    height, width = mask.shape
    cols = width // 128
    blocks = height * cols
    return pl.pallas_call(
        functools.partial(pack_kernel, tiles, slots, groups),
        out_shape=(f32(2 * (F * slots + 16), 128),) * (tiles // 2),
        in_specs=[HBM] * 8,
        scratch_shapes=[
            pltpu.VMEM((blocks * K, F * 128), jnp.float32),
            pltpu.VMEM((cols, height, K, 128, 128), jnp.bfloat16),
        ]
        + [pltpu.VMEM((K, blocks), jnp.int32)] * 3
        + [pltpu.VMEM((height, width), jnp.float32)]
        + [pltpu.VMEM((F, height, width), jnp.float32)] * 2
        + [
            pltpu.VMEM((height, width), jnp.int32),
            pltpu.SemaphoreType.DMA((cols,)),
            pltpu.SemaphoreType.DMA((7,)),
        ],
        compiler_params=params(60),
        cost_estimate=cost(3),
    )(state, coupling, surface, mask, dtile.T, dblock.T, dgroup.T, w.reshape(height, cols, K, 128, 128))


def early(groups, vert_coef, horiz_coef, wet_mask, chunk):
    levels, height, width = vert_coef.shape
    full = f32(levels + 1, height, width)
    return pl.pallas_call(
        functools.partial(early_kernel, groups),
        out_shape=(full,) * 4 + (f32(2, levels + 1, height, width), f32(*chunk.shape)),
        in_specs=[VM] * 3 + [HBM],
        scratch_shapes=[pltpu.SemaphoreType.DMA],
        compiler_params=params(16),
        cost_estimate=cost(3),
    )(vert_coef, horiz_coef, wet_mask, chunk)


def late(groups, tiles, state, horiz_coef, wet_mask, chip, core, solved, after):
    levels, height, width = state.shape
    full, halo = f32(levels, height, width), f32(levels, width // 64, 128)
    return pl.pallas_call(
        functools.partial(late_kernel, tiles, groups),
        out_shape=(f32(4, levels, height, width), f32(width // 64, 128)),
        in_specs=[VM] * 10,
        scratch_shapes=[pltpu.VMEM(s.shape, jnp.float32) for s in [full] + [halo] * 5],
        compiler_params=params(16),
        cost_estimate=cost(4),
    )(state, horiz_coef, wet_mask, chip, core, *solved, after)


def finish(groups, wet_mask, sides, parts, halo_wet, arrived):
    _, levels, height, width = parts.shape
    return pl.pallas_call(
        functools.partial(last_kernel, width // 128, groups),
        out_shape=(f32(levels, height, width), f32(F, height, width)),
        out_specs=(HBM, VM),
        scratch_shapes=[
            pltpu.VMEM((levels, height, width), jnp.float32),
            pltpu.SemaphoreType.DMA((4,)),
        ],
        compiler_params=params(16),
    )(wet_mask, sides, parts, halo_wet, *arrived)


def local(
    state, vert_coef, horiz_coef, wet_mask, coupling, surface_in, remap_w, dest_tile, dest_block, dest_group
):
    levels, height, width = state.shape
    groups, tiles = lax.axis_size("grp"), lax.axis_size("tile")
    cols = width // 128
    blocks = height * cols
    slots = max(8, 2 * blocks * K // tiles)
    rim = 2 * cols
    devices = groups * tiles
    start = (groups - 1) * tiles
    axes = ("grp", "tile")
    across = [(i, i + 1) for i in range(1, devices - 1, 2) if i + 1 != start]
    across = across + [(j, i) for i, j in across]
    packed = pack(
        groups, tiles, slots, state, coupling, surface_in, wet_mask, dest_tile, dest_block, dest_group, remap_w
    )
    chips = tiles // 2
    moved = {
        k: lax.ppermute(packed[k], "tile", [(i, ((i // 2) ^ k) * 2 + i % 2) for i in range(tiles)])
        for k in sorted(range(1, chips), key=lambda k: (k != chips // 2, k))
    }
    got = [moved[k] for k in range(1, chips)]
    *solved, sides, chunk = early(groups, vert_coef, horiz_coef, wet_mask, packed[0])
    chip, core = edges_of(groups, state, vert_coef, horiz_coef, wet_mask, chunk, got[2])
    chip = lax.ppermute(chip, axes, across)
    core = lax.ppermute(core, axes, [(i, i ^ 1) for i in range(devices)])
    rows = (groups - 1) * (F * blocks + rim)
    mine, theirs = pl.pallas_call(
        functools.partial(merge_kernel, slots, height, cols, groups),
        out_shape=(f32(rows, 128),) * 2,
        compiler_params=params(8),
        cost_estimate=cost(1),
    )(chunk, *got)
    theirs = lax.ppermute(theirs, "tile", [(i, i ^ 1) for i in range(tiles)])
    merged = pl.pallas_call(
        functools.partial(add_kernel, cols),
        out_shape=(f32(F * blocks + rim, 128),) * (groups - 1),
        compiler_params=params(8),
        cost_estimate=cost(1),
    )(mine, theirs)
    arrived = [
        lax.ppermute(merged[g], "grp", [(j, (j + g + 1) % groups) for j in range(groups)])
        for g in range(groups - 1)
    ]
    parts, halo_wet = late(groups, tiles, state, horiz_coef, wet_mask, chip, core, solved, merged[0])
    return finish(groups, wet_mask, sides, parts, halo_wet, arrived)


def solution(mesh):
    in_specs = (
        P(None, ("grp", "tile"), None),
        P(None, ("grp", "tile"), None),
        P(("grp", "tile"), None),
        P("tile", None),
        P(None, ("grp", "tile"), None),
        P(None, ("grp", "tile"), None),
        P(("grp", "tile"), None, None, None),
        P(("grp", "tile"), None),
        P(("grp", "tile"), None),
        P(("grp", "tile"), None),
    )
    out_specs = (P(None, ("grp", "tile"), None), P(None, ("grp", "tile"), None))
    return jax.shard_map(local, mesh=mesh, in_specs=in_specs, out_specs=out_specs, check_vma=False)
```

```python
import functools

import jax
import jax.numpy as jnp
from jax import lax
from jax.experimental import pallas as pl
from jax.experimental.pallas import tpu as pltpu
from jax.sharding import PartitionSpec as P

F = 4
K = 4
FORCING_GAIN = 0.25
VM = pl.BlockSpec(memory_space=pltpu.VMEM)
HBM = pl.BlockSpec(memory_space=pltpu.HBM)
MIB = 1024 * 1024


def params(mib):
    return pltpu.CompilerParams(vmem_limit_bytes=mib * MIB)


def split(x):
    hi = x.astype(jnp.bfloat16)
    return hi, (x - hi.astype(jnp.float32)).astype(jnp.bfloat16)


def wet_of(ocean, mask):
    return jnp.where(ocean, mask.astype(jnp.float32), 1.0)


def iota(shape, dim):
    return lax.broadcasted_iota(jnp.int32, shape, dim)


def pack_kernel(
    tiles, slots, groups, state, coupling, surface, mask, dtile, dblock, dgroup, w, *refs
):
    outs = refs[: tiles // 2]
    terms, w_here, *here, w_sem, sem = refs[tiles // 2 :]
    height, width = mask.shape
    cols = width // 128
    given = (dtile, dblock, dgroup, state.at[0], coupling, surface, mask)
    small = [pltpu.make_async_copy(a, b, sem.at[i]) for i, (a, b) in enumerate(zip(given, here))]
    large = [pltpu.make_async_copy(w.at[:, c], w_here.at[c], w_sem.at[c]) for c in range(cols)]
    for copy in small + large:
        copy.start()
    dtile, dblock, dgroup, state, coupling, surface, mask = here
    for copy in small[:3]:
        copy.wait()
    blocks = height * cols
    count = blocks * K
    ocean = lax.axis_index("grp") == groups - 1
    me = lax.axis_index("tile")

    block = dblock[...]
    line = block // cols
    col = block % cols
    group = jnp.where(ocean, dgroup[...], groups - 1)
    code = dtile[...] * 128 + col * height + line + jnp.where(ocean, dgroup[...] * blocks, 0)
    device = group * tiles + dtile[...]
    low = jnp.where(ocean, 0, (groups - 1) * tiles)
    high = jnp.where(ocean, (groups - 1) * tiles, groups * tiles)
    odd = device % 2 == 1
    beside = jnp.where(odd, device + 1, device - 1)
    reads = (line == jnp.where(odd, height - 1, 0)) & (beside >= low) & (beside < high)
    edge = (beside % tiles) * 16 + col + jnp.where(ocean, (beside // tiles) * cols, 0)
    edge = jnp.where(reads, edge, -1)

    item = iota((count, blocks), 0)
    item_k = (item // height) % K
    own = iota((count, blocks), 1) == (item % height) * cols + item // (height * K)
    up, down = iota((count, count), 0), iota((count, count), 1)

    def column(values):
        spread = jnp.broadcast_to(values[:1, :], (count, blocks))
        for k in range(1, K):
            spread = jnp.where(item_k == k, values[k : k + 1, :], spread)
        return jnp.sum(jnp.where(own, spread, 0), 1, keepdims=True)

    def turned(values):
        return jnp.sum(jnp.where(up == down, values, 0), 0, keepdims=True)

    def place_of(tile):
        return ((tile // 2) ^ (me // 2)) * 2 + tile % 2

    code_col, edge_row = column(code), turned(column(edge))
    code_row = turned(code_col)
    tile_row, tile_col, tag_col = code_row // 128, code_col // 128, code_col % 128
    same = tile_row == tile_col
    slot_row = jnp.sum(jnp.where(same & (up < down), 1, 0), 0, keepdims=True)
    slot_col = jnp.sum(jnp.where(same & (down < up), 1, 0), 1, keepdims=True)
    place_row, place_col = place_of(tile_row), place_of(tile_col)
    chooser = jnp.where(
        iota((tiles * slots, count), 0) == place_row * slots + slot_row, 1.0, 0.0
    ).astype(jnp.bfloat16)
    to_tile = jnp.where(iota((tiles, count), 0) == place_row, 1.0, 0.0).astype(jnp.bfloat16)
    labels = jnp.where(
        iota((count, 128), 1) == (place_col // 2) * slots + slot_col,
        (tag_col + 1).astype(jnp.float32),
        0.0,
    ).astype(jnp.bfloat16)
    tags = jnp.dot(to_tile, labels, preferred_element_type=jnp.float32)
    rim = cols * (groups - 1)
    rim_id = iota((tiles * 16, count), 0)
    rim_place, rim_id = rim_id // 16, rim_id % 16
    rim_tile = ((rim_place // 2) ^ (me // 2)) * 2 + rim_place % 2
    rim_id = jnp.where(
        rim_id < rim, rim_tile * 16 + jnp.where(ocean, rim_id, rim_id % cols), -2
    )
    rim_chooser = jnp.where(rim_id == edge_row, 1.0, 0.0).astype(jnp.bfloat16)

    for copy in small[3:]:
        copy.wait()
    send = coupling[...] * (state[...][None] - surface[...]) * wet_of(ocean, mask[...])[None]
    row_of = iota((F * height, 128), 0) % height
    for c in range(cols):
        piece = send[:, :, c * 128 : (c + 1) * 128].reshape(F * height, 128)
        left = jnp.concatenate(
            [jnp.where(row_of == r, piece, 0.0).astype(jnp.bfloat16) for r in range(height)], 1
        )
        large[c].wait()
        for k in range(K):
            right = w_here[c, :, k].reshape(height * 128, 128)
            made = jnp.dot(left, right, preferred_element_type=jnp.float32)
            at = (c * K + k) * height
            for f in range(F):
                terms[at : at + height, f * 128 : (f + 1) * 128] = made[
                    f * height : (f + 1) * height, :
                ]
    total = terms[:, :128]
    for f in range(1, F):
        total = total + terms[:, f * 128 : (f + 1) * 128]
    hi, lo = split(terms[...])
    packed = jnp.dot(
        jnp.concatenate([chooser, chooser], 1),
        jnp.concatenate([hi, lo], 0),
        preferred_element_type=jnp.float32,
    )
    hi, lo = split(total)
    rims = jnp.dot(
        jnp.concatenate([rim_chooser, rim_chooser], 1),
        jnp.concatenate([hi, lo], 0),
        preferred_element_type=jnp.float32,
    )
    size = F * slots + 16
    for t in range(tiles):
        out, at = outs[t // 2], (t % 2) * size
        for f in range(F):
            out[at + f * slots : at + (f + 1) * slots, :] = packed[
                t * slots : (t + 1) * slots, f * 128 : (f + 1) * 128
            ]
        at = at + F * slots
        out[at : at + 16, :] = rims[t * 16 : (t + 1) * 16, :]
        out[at + rim : at + rim + 1, :] = tags[t : t + 1, :]


def merge_kernel(slots, height, cols, groups, *refs):
    got, (mine, theirs) = refs[:-2], refs[-2:]
    blocks = height * cols
    size = F * slots + 16
    rim = cols * (groups - 1)
    rows = (groups - 1) * blocks
    ocean = lax.axis_index("grp") == groups - 1
    core = lax.axis_index("tile") % 2
    ids = iota((rows, 128), 0)
    ids = jnp.where(ocean, ids, ids % blocks) + 1

    def merged(which, out):
        first = which * size
        tail = got[0][pl.ds(first + F * slots, 16), :]
        for chunk in got[1:]:
            tail = tail + chunk[pl.ds(first + F * slots, 16), :]
        label = tail[rim : rim + 1, :].astype(jnp.int32)
        chooser = jnp.where(ids == label, 1.0, 0.0).astype(jnp.bfloat16)
        chooser = jnp.concatenate([chooser, chooser], 1)
        total = jnp.zeros((rows, 128), jnp.float32)
        for f in range(F):
            data = jnp.concatenate([chunk[pl.ds(first + f * slots, slots), :] for chunk in got], 0)
            hi, lo = split(data)
            part = jnp.dot(chooser, jnp.concatenate([hi, lo], 0), preferred_element_type=jnp.float32)
            total = total + part
            for g in range(groups - 1):
                at = (g * F + f) * blocks
                out[at : at + blocks, :] = part[g * blocks : (g + 1) * blocks, :]
        out[rows * F : rows * F + rim, :] = tail[:rim, :]
        return total.reshape(rim, height, 128)

    own = merged(core, mine)
    sibling = merged(1 - core, theirs)
    even = core == 0
    at = rows * F + rim
    theirs[at : at + rim, :] = jnp.where(even, own[:, height - 1, :], own[:, 0, :])
    mine[at : at + rim, :] = jnp.where(even, sibling[:, 0, :], sibling[:, height - 1, :])


def add_kernel(cols, mine, theirs, *outs):
    even = lax.axis_index("tile") % 2 == 0
    rows = outs[0].shape[0] - 2 * cols
    groups = len(outs)
    tail = groups * rows
    rims = mine[tail:, :] + theirs[tail:, :]
    for g, out in enumerate(outs):
        out[:rows, :] = mine[g * rows : (g + 1) * rows, :] + theirs[g * rows : (g + 1) * rows, :]
        far = rims[g * cols : (g + 1) * cols, :]
        near = rims[(groups + g) * cols : (groups + g + 1) * cols, :]
        out[rows : rows + cols, :] = jnp.where(even, far, near)
        out[rows + cols :, :] = jnp.where(even, near, far)


def edge_kernel(groups, state, vert, horiz, mask, *refs):
    chip, core = refs[-2:]
    levels, height, width = state.shape
    half = levels // 2
    cols = width // 128
    last = height - 1
    wet = wet_of(lax.axis_index("grp") == groups - 1, mask[...])

    def fill(down, up):
        for c in range(cols):
            at = slice(c * 128, (c + 1) * 128)
            for out, beside, behind, one, two in (
                (down, last, last - 1, c, cols + c),
                (up, 0, 1, cols + c, c),
            ):
                out[:levels, one, :] = state[:, beside, at]
                out[:levels, two, :] = state[:, behind, at]
                out[levels + half, one : one + 1, :] = wet[beside : beside + 1, at]
                out[levels + half, two : two + 1, :] = wet[behind : behind + 1, at]
                out[levels : levels + half, c, :] = vert[:half, beside, at]
                out[levels : levels + half - 1, cols + c, :] = vert[half:, beside, at]
                out[levels + half - 1, cols + c : cols + c + 1, :] = jnp.zeros((1, 128), jnp.float32)
                for row in (c, cols + c):
                    out[levels + half + 1, row : row + 1, :] = horiz[beside : beside + 1, at]

    even = lax.axis_index("tile") % 2 == 0
    pl.when(even)(lambda: fill(core, chip))
    pl.when(jnp.logical_not(even))(lambda: fill(chip, core))


def weights_of(horiz, wet):
    height, width = wet.shape
    row, column = iota((height, width), 0), iota((height, width), 1)
    left, right, above, below = around(wet)
    scale = horiz * wet
    return (
        scale * jnp.where(column == 0, 0.0, left),
        scale * jnp.where(column == width - 1, 0.0, right),
        scale * jnp.where(row == 0, 0.0, above),
        scale * jnp.where(row == height - 1, 0.0, below),
    )


def around(field):
    height, width = field.shape
    return (
        pltpu.roll(field, 1, 1),
        pltpu.roll(field, width - 1, 1),
        pltpu.roll(field, 1, 0),
        pltpu.roll(field, height - 1, 0),
    )


def stencil(field, weights):
    total = field
    for other, weight in zip(around(field), weights):
        total = total + weight * (other - field)
    return total


def inverse_of(x):
    y = pl.reciprocal(x, approx=True)
    return y * (2.0 - x * y)


def early_kernel(
    groups, state, vert, horiz, mask, chunk, packs, chunk_out, upper, gain, ratio, base, impulse, sem,
):
    levels, height, width = state.shape
    cols = width // 128
    copy = pltpu.make_async_copy(chunk, chunk_out, sem)
    copy.start()
    wet = wet_of(lax.axis_index("grp") == groups - 1, mask[...])
    zero = jnp.zeros((height, width), jnp.float32)
    weights = weights_of(horiz[...], wet)

    def forward(level, carry, last=False, first=False):
        low, c, r, e = carry
        upp = zero if last else vert[level] * wet
        inverse = inverse_of(1.0 + low + upp + low * c)
        c = -upp * inverse
        step = low * inverse
        r = stencil(state[level], weights) * inverse + step * r
        e = inverse if first else step * e
        upper[level] = c
        gain[level] = inverse
        ratio[level] = step
        base[level] = r
        impulse[level] = e
        return upp, c, r, e

    carry = forward(0, (zero,) * 4, first=True)
    carry = lax.fori_loop(1, levels - 1, forward, carry, unroll=31)
    _, _, r, e = forward(levels - 1, carry, last=True)

    def backward(i, carry):
        level = levels - 2 - i
        c = upper[level]
        r = base[level] - c * carry[0]
        e = impulse[level] - c * carry[1]
        base[level] = r
        impulse[level] = e
        return r, e

    lax.fori_loop(0, levels - 1, backward, (r, e), unroll=9)
    for i, (source, low, high) in enumerate(
        [(x, 0, height - 1) for x in (upper, gain, ratio)]
        + [(x, 1, height - 2) for x in (upper, gain, ratio)]
        + [(x, 0, height - 1) for x in (impulse, base, state)]
    ):
        for c in range(cols):
            at = slice(c * 128, (c + 1) * 128)
            packs[i, :, c, :] = source[:, low, at]
            packs[i, :, cols + c, :] = source[:, high, at]
    copy.wait()


def parts_kernel(groups, horiz, mask, upper, gain, ratio, base, impulse, _, parts):
    levels = base.shape[0]
    weights = weights_of(horiz[...], wet_of(lax.axis_index("grp") == groups - 1, mask[...]))
    rest = 1.0 - weights[0] - weights[1] - weights[2] - weights[3]

    def forward_parts(level, carry, first=False):
        g = impulse[level]
        rhs = [stencil(base[level], weights), rest * g + (1.0 if first else 0.0)]
        rhs += [w * x for w, x in zip(weights, around(g))]
        inverse, step = gain[level], ratio[level]
        made = tuple(x * inverse + step * r for x, r in zip(rhs, carry))
        for i in range(6):
            parts[i, level] = made[i]
        return made

    carry = forward_parts(0, (jnp.zeros(mask.shape, jnp.float32),) * 6, first=True)
    carry = lax.fori_loop(1, levels, forward_parts, carry, unroll=7)
    back_parts(parts, upper, carry)


def back_parts(parts, upper, carry):
    count, levels = parts.shape[:2]

    def backward(i, carry):
        level = levels - 2 - i
        c = upper[level]
        made = tuple(parts[j, level] - c * carry[j] for j in range(count))
        for j in range(count):
            parts[j, level] = made[j]
        return made

    lax.fori_loop(0, levels - 1, backward, carry, unroll=9)


def late_kernel(
    groups, horiz, mask, chip, core, packs, _, fixes, halo_wet,
    delta, halo_base, halo_impulse, halo_vert, halo_upper,
):
    levels = packs.shape[1]
    height, width = mask.shape
    cols = width // 128
    half = levels // 2
    shape = (2 * cols, 128)
    low_half = iota(shape, 0) < cols
    lane = iota(shape, 1)
    place = iota(shape, 0) % cols
    parity = lax.axis_index("tile") % 2
    from_chip = iota(shape, 0) // cols == parity

    def turn(x):
        return pltpu.roll(x, cols, 0)

    def beside(i):
        return jnp.where(from_chip, chip[i], core[i])

    def behind(i):
        return turn(jnp.where(from_chip, core[i], chip[i]))

    def packed(x, low, high):
        return jnp.concatenate(
            [x[r : r + 1, c * 128 : (c + 1) * 128] for r in (low, high) for c in range(cols)], 0
        )

    def shifted(x):
        rows = x.shape[0]
        to_right, to_left = pltpu.roll(x, 1, 1), pltpu.roll(x, 127, 1)
        return (
            jnp.where(lane == 0, pltpu.roll(to_right, 1, 0), to_right),
            jnp.where(lane == 127, pltpu.roll(to_left, rows - 1, 0), to_left),
        )

    def along(scale, wet):
        left, right = shifted(wet)
        return (
            scale * jnp.where((place == 0) & (lane == 0), 0.0, left),
            scale * jnp.where((place == cols - 1) & (lane == 127), 0.0, right),
        )

    wet = wet_of(lax.axis_index("grp") == groups - 1, mask[...])
    nu = horiz[...]
    rim_wet, next_wet = packed(wet, 0, height - 1), packed(wet, 1, height - 2)
    wet_halo = beside(levels + half)
    halo_wet[...] = wet_halo
    scale = beside(levels + half + 1) * wet_halo
    halo_left, halo_right = along(scale, wet_halo)
    halo_behind = scale * behind(levels + half)
    halo_inside = scale * rim_wet
    scale = packed(nu, 0, height - 1) * rim_wet
    rim_left, rim_right = along(scale, rim_wet)
    rim_inside = scale * next_wet
    outside = scale * wet_halo
    next_outside = packed(nu, 1, height - 2) * next_wet * rim_wet

    def spread(i, _):
        x, y = chip[levels + i], core[levels + i]
        a, b = jnp.where(parity == 0, x, y), jnp.where(parity == 0, y, x)
        halo_vert[i] = jnp.where(low_half, a, turn(b)) * wet_halo
        halo_vert[half + i] = jnp.where(low_half, turn(a), b) * wet_halo
        return 0

    lax.fori_loop(0, half, spread, 0, unroll=4)
    zero = jnp.zeros(shape, jnp.float32)

    def forward(level, carry, last=False, first=False):
        low, c, x, e, d = carry
        halo, rim = beside(level), packs[8, level]
        upp = zero if last else halo_vert[level]
        inverse = inverse_of(1.0 + low + upp + low * c)
        c = -upp * inverse
        step = low * inverse
        left, right = shifted(halo)
        field = (
            halo
            + halo_left * (left - halo)
            + halo_right * (right - halo)
            + halo_behind * (behind(level) - halo)
            + halo_inside * (rim - halo)
        )
        x = field * inverse + step * x
        e = inverse if first else step * e
        d = outside * (halo - rim) * packs[1, level] + packs[2, level] * d
        halo_upper[level] = c
        halo_base[level] = x
        halo_impulse[level] = e
        delta[level] = d
        return upp, c, x, e, d

    carry = forward(0, (zero,) * 5, first=True)
    carry = lax.fori_loop(1, levels - 1, forward, carry, unroll=31)
    _, _, x, e, d = forward(levels - 1, carry, last=True)

    def backward(i, carry):
        level = levels - 2 - i
        c = halo_upper[level]
        x = halo_base[level] - c * carry[0]
        e = halo_impulse[level] - c * carry[1]
        d = delta[level] - packs[0, level] * carry[2]
        halo_base[level] = x
        halo_impulse[level] = e
        delta[level] = d
        return x, e, d

    lax.fori_loop(0, levels - 1, backward, (x, e, d), unroll=9)

    def forward_fixes(level, carry):
        d = delta[level]
        left, right = shifted(d)
        rhs = (
            d
            + rim_left * (left - d)
            + rim_right * (right - d)
            - rim_inside * d
            + outside * (halo_base[level] - (packs[7, level] + d)),
            outside * halo_impulse[level],
            outside * packs[6, level],
            next_outside * d,
        )
        made = tuple(
            x * packs[1 if i < 3 else 4, level] + packs[2 if i < 3 else 5, level] * r
            for i, (x, r) in enumerate(zip(rhs, carry))
        )
        for i in range(4):
            fixes[i, level] = made[i]
        return made

    carry = lax.fori_loop(0, levels, forward_fixes, (zero,) * 4, unroll=8)

    def backward_fixes(i, carry):
        level = levels - 2 - i
        made = tuple(
            fixes[j, level] - packs[0 if j < 3 else 3, level] * carry[j] for j in range(4)
        )
        for j in range(4):
            fixes[j, level] = made[j]
        return made

    lax.fori_loop(0, levels - 1, backward_fixes, carry, unroll=9)


def last_kernel(cols, groups, mask, parts, fixes, halo_wet, *refs):
    arrived = refs[: groups - 1]
    out, received_out, field, received, sem = refs[groups - 1 :]
    _, levels, height, width = parts.shape
    group = lax.axis_index("grp")
    total = jnp.zeros(arrived[0].shape, jnp.float32)
    for g, other in enumerate(arrived):
        total = total + jnp.where((group == groups - 1) | (group == g), other[...], 0.0)
    for f in range(F):
        for c in range(cols):
            at = (f * cols + c) * height
            received[f, :, c * 128 : (c + 1) * 128] = total[at : at + height, :]
    copies = [pltpu.make_async_copy(received, received_out, sem.at[0])]
    copies[0].start()
    wet = wet_of(lax.axis_index("grp") == groups - 1, mask[...])
    force = FORCING_GAIN * wet * jnp.sum(received[...], 0)
    force_halo = FORCING_GAIN * halo_wet[...] * total[F * cols * height :, :]
    factors = (force,) + around(force)
    force_rim = jnp.concatenate(
        [force[r : r + 1, c * 128 : (c + 1) * 128] for r in (0, height - 1) for c in range(cols)], 0
    )

    def level_of(level, _):
        x = parts[0, level]
        for i in range(5):
            x = x + parts[i + 1, level] * factors[i]
        field[level] = x
        return 0

    chunks = 8
    size = levels // chunks
    for i in range(chunks):
        lax.fori_loop(i * size, (i + 1) * size, level_of, 0, unroll=8)
        at = pl.ds(i * size, size)
        rims = fixes[0, at] + fixes[1, at] * force_halo[None] - fixes[2, at] * force_rim[None]
        for c in range(cols):
            block = pl.ds(c * 128, 128)
            for row, fix in ((0, rims[:, c]), (height - 1, rims[:, cols + c])):
                field[at, row, block] = field[at, row, block] + fix
            for row, fix in ((1, c), (height - 2, cols + c)):
                field[at, row, block] = field[at, row, block] + fixes[3, at, fix, :]
        copies.append(pltpu.make_async_copy(field.at[at], out.at[at], sem.at[i + 1]))
        copies[-1].start()
    for copy in copies:
        copy.wait()


def f32(*shape):
    return jax.ShapeDtypeStruct(shape, jnp.float32)


def cost(us):
    return pl.CostEstimate(flops=0, bytes_accessed=int(us * 3e6), transcendentals=0)


def edges_of(groups, state, vert_coef, horiz_coef, wet_mask, *after):
    levels, height, width = state.shape
    return pl.pallas_call(
        functools.partial(edge_kernel, groups),
        out_shape=(f32(levels + levels // 2 + 2, width // 64, 128),) * 2,
        in_specs=[VM] * 4 + [HBM] * len(after),
        compiler_params=params(8),
        cost_estimate=cost(1),
    )(state, vert_coef, horiz_coef, wet_mask, *after)


def pack(groups, tiles, slots, state, coupling, surface, mask, dtile, dblock, dgroup, w):
    height, width = mask.shape
    cols = width // 128
    blocks = height * cols
    return pl.pallas_call(
        functools.partial(pack_kernel, tiles, slots, groups),
        out_shape=(f32(2 * (F * slots + 16), 128),) * (tiles // 2),
        in_specs=[HBM] * 8,
        scratch_shapes=[
            pltpu.VMEM((blocks * K, F * 128), jnp.float32),
            pltpu.VMEM((cols, height, K, 128, 128), jnp.bfloat16),
        ]
        + [pltpu.VMEM((K, blocks), jnp.int32)] * 3
        + [pltpu.VMEM((height, width), jnp.float32)]
        + [pltpu.VMEM((F, height, width), jnp.float32)] * 2
        + [
            pltpu.VMEM((height, width), jnp.int32),
            pltpu.SemaphoreType.DMA((cols,)),
            pltpu.SemaphoreType.DMA((7,)),
        ],
        compiler_params=params(60),
        cost_estimate=cost(3),
    )(state, coupling, surface, mask, dtile.T, dblock.T, dgroup.T, w.reshape(height, cols, K, 128, 128))


def early(groups, state, vert_coef, horiz_coef, wet_mask, chunk):
    levels, height, width = state.shape
    return pl.pallas_call(
        functools.partial(early_kernel, groups),
        out_shape=(f32(9, levels, width // 64, 128), f32(*chunk.shape))
        + (f32(levels, height, width),) * 5,
        in_specs=[VM] * 4 + [HBM],
        scratch_shapes=[pltpu.SemaphoreType.DMA],
        compiler_params=params(16),
        cost_estimate=cost(3),
    )(state, vert_coef, horiz_coef, wet_mask, chunk)


def parts_of(groups, horiz_coef, wet_mask, solved, after):
    return pl.pallas_call(
        functools.partial(parts_kernel, groups),
        out_shape=f32(6, *solved[0].shape),
        in_specs=[VM] * 8,
        compiler_params=params(16),
        cost_estimate=cost(3),
    )(horiz_coef, wet_mask, *solved, after)


def late(groups, horiz_coef, wet_mask, chip, core, packs, after):
    _, levels, rows, lanes = packs.shape
    return pl.pallas_call(
        functools.partial(late_kernel, groups),
        out_shape=(f32(4, levels, rows, lanes), f32(rows, lanes)),
        in_specs=[VM] * 6,
        scratch_shapes=[pltpu.VMEM((levels, rows, lanes), jnp.float32)] * 5,
        compiler_params=params(12),
        cost_estimate=cost(2),
    )(horiz_coef, wet_mask, chip, core, packs, after)


def finish(groups, wet_mask, parts, fixes, halo_wet, arrived):
    _, levels, height, width = parts.shape
    return pl.pallas_call(
        functools.partial(last_kernel, width // 128, groups),
        out_shape=(f32(levels, height, width), f32(F, height, width)),
        out_specs=(HBM, HBM),
        scratch_shapes=[
            pltpu.VMEM((levels, height, width), jnp.float32),
            pltpu.VMEM((F, height, width), jnp.float32),
            pltpu.SemaphoreType.DMA((8 + 1,)),
        ],
        compiler_params=params(16),
    )(wet_mask, parts, fixes, halo_wet, *arrived)


def local(
    state, vert_coef, horiz_coef, wet_mask, coupling, surface_in, remap_w, dest_tile, dest_block, dest_group
):
    levels, height, width = state.shape
    groups, tiles = lax.axis_size("grp"), lax.axis_size("tile")
    cols = width // 128
    blocks = height * cols
    slots = max(8, 2 * blocks * K // tiles)
    rim = 2 * cols
    devices = groups * tiles
    start = (groups - 1) * tiles
    axes = ("grp", "tile")
    across = [(i, i + 1) for i in range(1, devices - 1, 2) if i + 1 != start]
    across = across + [(j, i) for i, j in across]
    packed = pack(
        groups, tiles, slots, state, coupling, surface_in, wet_mask, dest_tile, dest_block, dest_group, remap_w
    )
    chips = tiles // 2
    moved = {
        k: lax.ppermute(packed[k], "tile", [(i, ((i // 2) ^ k) * 2 + i % 2) for i in range(tiles)])
        for k in sorted(range(1, chips), key=lambda k: (k != chips // 2, k))
    }
    got = [moved[k] for k in range(1, chips)]
    packs, chunk, *solved = early(groups, state, vert_coef, horiz_coef, wet_mask, packed[0])
    chip, core = edges_of(groups, state, vert_coef, horiz_coef, wet_mask, chunk, got[2])
    chip = lax.ppermute(chip, axes, across)
    core = lax.ppermute(core, axes, [(i, i ^ 1) for i in range(devices)])
    rows = (groups - 1) * (F * blocks + rim)
    mine, theirs = pl.pallas_call(
        functools.partial(merge_kernel, slots, height, cols, groups),
        out_shape=(f32(rows, 128),) * 2,
        compiler_params=params(8),
        cost_estimate=cost(1),
    )(chunk, *got)
    parts = parts_of(groups, horiz_coef, wet_mask, solved, mine)
    theirs = lax.ppermute(theirs, "tile", [(i, i ^ 1) for i in range(tiles)])
    merged = pl.pallas_call(
        functools.partial(add_kernel, cols),
        out_shape=(f32(F * blocks + rim, 128),) * (groups - 1),
        compiler_params=params(8),
        cost_estimate=cost(1),
    )(mine, theirs)
    arrived = [
        lax.ppermute(merged[g], "grp", [(j, (j + g + 1) % groups) for j in range(groups)])
        for g in range(groups - 1)
    ]
    fixes, halo_wet = late(groups, horiz_coef, wet_mask, chip, core, packs, merged[0])
    return finish(groups, wet_mask, parts, fixes, halo_wet, arrived)


def solution(mesh):
    in_specs = (
        P(None, ("grp", "tile"), None),
        P(None, ("grp", "tile"), None),
        P(("grp", "tile"), None),
        P("tile", None),
        P(None, ("grp", "tile"), None),
        P(None, ("grp", "tile"), None),
        P(("grp", "tile"), None, None, None),
        P(("grp", "tile"), None),
        P(("grp", "tile"), None),
        P(("grp", "tile"), None),
    )
    out_specs = (P(None, ("grp", "tile"), None), P(None, ("grp", "tile"), None))
    return jax.shard_map(local, mesh=mesh, in_specs=in_specs, out_specs=out_specs, check_vma=False)
```

```python
import functools

import jax
import jax.numpy as jnp
from jax import lax
from jax.experimental import pallas as pl
from jax.experimental.pallas import tpu as pltpu
from jax.sharding import PartitionSpec as P

F = 4
K = 4
FORCING_GAIN = 0.25
VM = pl.BlockSpec(memory_space=pltpu.VMEM)
HBM = pl.BlockSpec(memory_space=pltpu.HBM)
MIB = 1024 * 1024


def params(mib):
    return pltpu.CompilerParams(vmem_limit_bytes=mib * MIB)


def split(x):
    hi = x.astype(jnp.bfloat16)
    return hi, (x - hi.astype(jnp.float32)).astype(jnp.bfloat16)


def wet_of(ocean, mask):
    return jnp.where(ocean, mask.astype(jnp.float32), 1.0)


def iota(shape, dim):
    return lax.broadcasted_iota(jnp.int32, shape, dim)


def pack_kernel(
    tiles, slots, groups, state, coupling, surface, mask, dtile, dblock, dgroup, w, *refs
):
    outs = refs[: tiles // 2]
    terms, w_here, *here, w_sem, sem = refs[tiles // 2 :]
    height, width = mask.shape
    cols = width // 128
    given = (dtile, dblock, dgroup, state.at[0], coupling, surface, mask)
    small = [pltpu.make_async_copy(a, b, sem.at[i]) for i, (a, b) in enumerate(zip(given, here))]
    large = [pltpu.make_async_copy(w.at[:, c], w_here.at[c], w_sem.at[c]) for c in range(cols)]
    for copy in small + large:
        copy.start()
    dtile, dblock, dgroup, state, coupling, surface, mask = here
    for copy in small[:3]:
        copy.wait()
    blocks = height * cols
    count = blocks * K
    ocean = lax.axis_index("grp") == groups - 1
    me = lax.axis_index("tile")

    block = dblock[...]
    line = block // cols
    col = block % cols
    group = jnp.where(ocean, dgroup[...], groups - 1)
    code = dtile[...] * 128 + col * height + line + jnp.where(ocean, dgroup[...] * blocks, 0)
    device = group * tiles + dtile[...]
    low = jnp.where(ocean, 0, (groups - 1) * tiles)
    high = jnp.where(ocean, (groups - 1) * tiles, groups * tiles)
    odd = device % 2 == 1
    beside = jnp.where(odd, device + 1, device - 1)
    reads = (line == jnp.where(odd, height - 1, 0)) & (beside >= low) & (beside < high)
    edge = (beside % tiles) * 16 + col + jnp.where(ocean, (beside // tiles) * cols, 0)
    edge = jnp.where(reads, edge, -1)

    item = iota((count, blocks), 0)
    item_k = (item // height) % K
    own = iota((count, blocks), 1) == (item % height) * cols + item // (height * K)
    up, down = iota((count, count), 0), iota((count, count), 1)

    def column(values):
        spread = jnp.broadcast_to(values[:1, :], (count, blocks))
        for k in range(1, K):
            spread = jnp.where(item_k == k, values[k : k + 1, :], spread)
        return jnp.sum(jnp.where(own, spread, 0), 1, keepdims=True)

    def turned(values):
        return jnp.sum(jnp.where(up == down, values, 0), 0, keepdims=True)

    def place_of(tile):
        return ((tile // 2) ^ (me // 2)) * 2 + tile % 2

    code_col, edge_row = column(code), turned(column(edge))
    code_row = turned(code_col)
    tile_row, tile_col, tag_col = code_row // 128, code_col // 128, code_col % 128
    same = tile_row == tile_col
    slot_row = jnp.sum(jnp.where(same & (up < down), 1, 0), 0, keepdims=True)
    slot_col = jnp.sum(jnp.where(same & (down < up), 1, 0), 1, keepdims=True)
    place_row, place_col = place_of(tile_row), place_of(tile_col)
    chooser = jnp.where(
        iota((tiles * slots, count), 0) == place_row * slots + slot_row, 1.0, 0.0
    ).astype(jnp.bfloat16)
    to_tile = jnp.where(iota((tiles, count), 0) == place_row, 1.0, 0.0).astype(jnp.bfloat16)
    labels = jnp.where(
        iota((count, 128), 1) == (place_col // 2) * slots + slot_col,
        (tag_col + 1).astype(jnp.float32),
        0.0,
    ).astype(jnp.bfloat16)
    tags = jnp.dot(to_tile, labels, preferred_element_type=jnp.float32)
    rim = cols * (groups - 1)
    rim_id = iota((tiles * 16, count), 0)
    rim_place, rim_id = rim_id // 16, rim_id % 16
    rim_tile = ((rim_place // 2) ^ (me // 2)) * 2 + rim_place % 2
    rim_id = jnp.where(
        rim_id < rim, rim_tile * 16 + jnp.where(ocean, rim_id, rim_id % cols), -2
    )
    rim_chooser = jnp.where(rim_id == edge_row, 1.0, 0.0).astype(jnp.bfloat16)

    for copy in small[3:]:
        copy.wait()
    send = coupling[...] * (state[...][None] - surface[...]) * wet_of(ocean, mask[...])[None]
    row_of = iota((F * height, 128), 0) % height
    for c in range(cols):
        piece = send[:, :, c * 128 : (c + 1) * 128].reshape(F * height, 128)
        left = jnp.concatenate(
            [jnp.where(row_of == r, piece, 0.0).astype(jnp.bfloat16) for r in range(height)], 1
        )
        large[c].wait()
        for k in range(K):
            right = w_here[c, :, k].reshape(height * 128, 128)
            made = jnp.dot(left, right, preferred_element_type=jnp.float32)
            at = (c * K + k) * height
            for f in range(F):
                terms[at : at + height, f * 128 : (f + 1) * 128] = made[
                    f * height : (f + 1) * height, :
                ]
    total = terms[:, :128]
    for f in range(1, F):
        total = total + terms[:, f * 128 : (f + 1) * 128]
    hi, lo = split(terms[...])
    packed = jnp.dot(
        jnp.concatenate([chooser, chooser], 1),
        jnp.concatenate([hi, lo], 0),
        preferred_element_type=jnp.float32,
    )
    hi, lo = split(total)
    rims = jnp.dot(
        jnp.concatenate([rim_chooser, rim_chooser], 1),
        jnp.concatenate([hi, lo], 0),
        preferred_element_type=jnp.float32,
    )
    size = F * slots + 16
    for t in range(tiles):
        out, at = outs[t // 2], (t % 2) * size
        for f in range(F):
            out[at + f * slots : at + (f + 1) * slots, :] = packed[
                t * slots : (t + 1) * slots, f * 128 : (f + 1) * 128
            ]
        at = at + F * slots
        out[at : at + 16, :] = rims[t * 16 : (t + 1) * 16, :]
        out[at + rim : at + rim + 1, :] = tags[t : t + 1, :]


def merge_kernel(slots, height, cols, groups, *refs):
    got, (mine, theirs) = refs[:-2], refs[-2:]
    blocks = height * cols
    size = F * slots + 16
    rim = cols * (groups - 1)
    rows = (groups - 1) * blocks
    ocean = lax.axis_index("grp") == groups - 1
    core = lax.axis_index("tile") % 2
    ids = iota((rows, 128), 0)
    ids = jnp.where(ocean, ids, ids % blocks) + 1

    def merged(which, out):
        first = which * size
        tail = got[0][pl.ds(first + F * slots, 16), :]
        for chunk in got[1:]:
            tail = tail + chunk[pl.ds(first + F * slots, 16), :]
        label = tail[rim : rim + 1, :].astype(jnp.int32)
        chooser = jnp.where(ids == label, 1.0, 0.0).astype(jnp.bfloat16)
        chooser = jnp.concatenate([chooser, chooser], 1)
        total = jnp.zeros((rows, 128), jnp.float32)
        for f in range(F):
            data = jnp.concatenate([chunk[pl.ds(first + f * slots, slots), :] for chunk in got], 0)
            hi, lo = split(data)
            part = jnp.dot(chooser, jnp.concatenate([hi, lo], 0), preferred_element_type=jnp.float32)
            total = total + part
            for g in range(groups - 1):
                at = (g * F + f) * blocks
                out[at : at + blocks, :] = part[g * blocks : (g + 1) * blocks, :]
        out[rows * F : rows * F + rim, :] = tail[:rim, :]
        return total.reshape(rim, height, 128)

    own = merged(core, mine)
    sibling = merged(1 - core, theirs)
    even = core == 0
    at = rows * F + rim
    theirs[at : at + rim, :] = jnp.where(even, own[:, height - 1, :], own[:, 0, :])
    mine[at : at + rim, :] = jnp.where(even, sibling[:, 0, :], sibling[:, height - 1, :])


def add_kernel(cols, mine, theirs, *outs):
    even = lax.axis_index("tile") % 2 == 0
    rows = outs[0].shape[0] - 2 * cols
    groups = len(outs)
    tail = groups * rows
    rims = mine[tail:, :] + theirs[tail:, :]
    for g, out in enumerate(outs):
        out[:rows, :] = mine[g * rows : (g + 1) * rows, :] + theirs[g * rows : (g + 1) * rows, :]
        far = rims[g * cols : (g + 1) * cols, :]
        near = rims[(groups + g) * cols : (groups + g + 1) * cols, :]
        out[rows : rows + cols, :] = jnp.where(even, far, near)
        out[rows + cols :, :] = jnp.where(even, near, far)


def edge_kernel(groups, state, vert, horiz, mask, *refs):
    chip, core = refs[-2:]
    levels, height, width = state.shape
    half = levels // 2
    cols = width // 128
    last = height - 1
    wet = wet_of(lax.axis_index("grp") == groups - 1, mask[...])

    def fill(down, up):
        for c in range(cols):
            at = slice(c * 128, (c + 1) * 128)
            for out, beside, behind, one, two in (
                (down, last, last - 1, c, cols + c),
                (up, 0, 1, cols + c, c),
            ):
                out[:levels, one, :] = state[:, beside, at]
                out[:levels, two, :] = state[:, behind, at]
                out[levels + half, one : one + 1, :] = wet[beside : beside + 1, at]
                out[levels + half, two : two + 1, :] = wet[behind : behind + 1, at]
                out[levels : levels + half, c, :] = vert[:half, beside, at]
                out[levels : levels + half - 1, cols + c, :] = vert[half:, beside, at]
                out[levels + half - 1, cols + c : cols + c + 1, :] = jnp.zeros((1, 128), jnp.float32)
                for row in (c, cols + c):
                    out[levels + half + 1, row : row + 1, :] = horiz[beside : beside + 1, at]

    even = lax.axis_index("tile") % 2 == 0
    pl.when(even)(lambda: fill(core, chip))
    pl.when(jnp.logical_not(even))(lambda: fill(chip, core))


def weights_of(horiz, wet):
    height, width = wet.shape
    row, column = iota((height, width), 0), iota((height, width), 1)
    left, right, above, below = around(wet)
    scale = horiz * wet
    return (
        scale * jnp.where(column == 0, 0.0, left),
        scale * jnp.where(column == width - 1, 0.0, right),
        scale * jnp.where(row == 0, 0.0, above),
        scale * jnp.where(row == height - 1, 0.0, below),
    )


def around(field):
    height, width = field.shape
    return (
        pltpu.roll(field, 1, 1),
        pltpu.roll(field, width - 1, 1),
        pltpu.roll(field, 1, 0),
        pltpu.roll(field, height - 1, 0),
    )


def stencil(field, weights):
    total = field
    for other, weight in zip(around(field), weights):
        total = total + weight * (other - field)
    return total


def inverse_of(x):
    y = pl.reciprocal(x, approx=True)
    return y * (2.0 - x * y)


def early_kernel(
    groups, state, vert, horiz, mask, chunk, packs, chunk_out, upper, gain, ratio, base, impulse, sem,
):
    levels, height, width = state.shape
    cols = width // 128
    copy = pltpu.make_async_copy(chunk, chunk_out, sem)
    copy.start()
    wet = wet_of(lax.axis_index("grp") == groups - 1, mask[...])
    zero = jnp.zeros((height, width), jnp.float32)
    weights = weights_of(horiz[...], wet)

    def forward(level, carry, last=False, first=False):
        low, c, r, e = carry
        upp = zero if last else vert[level] * wet
        inverse = inverse_of(1.0 + low + upp + low * c)
        c = -upp * inverse
        step = low * inverse
        r = stencil(state[level], weights) * inverse + step * r
        e = inverse if first else step * e
        upper[level] = c
        gain[level] = inverse
        ratio[level] = step
        base[level] = r
        impulse[level] = e
        return upp, c, r, e

    carry = forward(0, (zero,) * 4, first=True)
    carry = lax.fori_loop(1, levels - 1, forward, carry, unroll=31)
    _, _, r, e = forward(levels - 1, carry, last=True)

    def backward(i, carry):
        level = levels - 2 - i
        c = upper[level]
        r = base[level] - c * carry[0]
        e = impulse[level] - c * carry[1]
        base[level] = r
        impulse[level] = e
        return r, e

    lax.fori_loop(0, levels - 1, backward, (r, e), unroll=9)
    for i, (source, low, high) in enumerate(
        [(x, 0, height - 1) for x in (upper, gain, ratio)]
        + [(x, 1, height - 2) for x in (upper, gain, ratio)]
        + [(x, 0, height - 1) for x in (impulse, base, state)]
    ):
        for c in range(cols):
            at = slice(c * 128, (c + 1) * 128)
            packs[i, :, c, :] = source[:, low, at]
            packs[i, :, cols + c, :] = source[:, high, at]
    copy.wait()


def parts_kernel(groups, horiz, mask, upper, gain, ratio, base, impulse, _, parts):
    levels = base.shape[0]
    weights = weights_of(horiz[...], wet_of(lax.axis_index("grp") == groups - 1, mask[...]))
    rest = 1.0 - weights[0] - weights[1] - weights[2] - weights[3]

    def forward_parts(level, carry, first=False):
        g = impulse[level]
        rhs = [stencil(base[level], weights), rest * g + (1.0 if first else 0.0)]
        rhs += [w * x for w, x in zip(weights, around(g))]
        inverse, step = gain[level], ratio[level]
        made = tuple(x * inverse + step * r for x, r in zip(rhs, carry))
        for i in range(6):
            parts[i, level] = made[i]
        return made

    carry = forward_parts(0, (jnp.zeros(mask.shape, jnp.float32),) * 6, first=True)
    carry = lax.fori_loop(1, levels, forward_parts, carry, unroll=21)
    back_parts(parts, upper, carry)


def back_parts(parts, upper, carry):
    count, levels = parts.shape[:2]

    def backward(i, carry):
        level = levels - 2 - i
        c = upper[level]
        made = tuple(parts[j, level] - c * carry[j] for j in range(count))
        for j in range(count):
            parts[j, level] = made[j]
        return made

    lax.fori_loop(0, levels - 1, backward, carry, unroll=21)


def late_kernel(
    groups, horiz, mask, chip, core, packs, _, fixes, halo_wet,
    delta, halo_base, halo_impulse, halo_vert, halo_upper,
):
    levels = packs.shape[1]
    height, width = mask.shape
    cols = width // 128
    half = levels // 2
    shape = (2 * cols, 128)
    low_half = iota(shape, 0) < cols
    lane = iota(shape, 1)
    place = iota(shape, 0) % cols
    parity = lax.axis_index("tile") % 2
    from_chip = iota(shape, 0) // cols == parity

    def turn(x):
        return pltpu.roll(x, cols, 0)

    def beside(i):
        return jnp.where(from_chip, chip[i], core[i])

    def behind(i):
        return turn(jnp.where(from_chip, core[i], chip[i]))

    def packed(x, low, high):
        return jnp.concatenate(
            [x[r : r + 1, c * 128 : (c + 1) * 128] for r in (low, high) for c in range(cols)], 0
        )

    def shifted(x):
        rows = x.shape[0]
        to_right, to_left = pltpu.roll(x, 1, 1), pltpu.roll(x, 127, 1)
        return (
            jnp.where(lane == 0, pltpu.roll(to_right, 1, 0), to_right),
            jnp.where(lane == 127, pltpu.roll(to_left, rows - 1, 0), to_left),
        )

    def along(scale, wet):
        left, right = shifted(wet)
        return (
            scale * jnp.where((place == 0) & (lane == 0), 0.0, left),
            scale * jnp.where((place == cols - 1) & (lane == 127), 0.0, right),
        )

    wet = wet_of(lax.axis_index("grp") == groups - 1, mask[...])
    nu = horiz[...]
    rim_wet, next_wet = packed(wet, 0, height - 1), packed(wet, 1, height - 2)
    wet_halo = beside(levels + half)
    halo_wet[...] = wet_halo
    scale = beside(levels + half + 1) * wet_halo
    halo_left, halo_right = along(scale, wet_halo)
    halo_behind = scale * behind(levels + half)
    halo_inside = scale * rim_wet
    scale = packed(nu, 0, height - 1) * rim_wet
    rim_left, rim_right = along(scale, rim_wet)
    rim_inside = scale * next_wet
    outside = scale * wet_halo
    next_outside = packed(nu, 1, height - 2) * next_wet * rim_wet

    zero = jnp.zeros(shape, jnp.float32)
    halo_vert[0] = zero

    def spread(i, _):
        x, y = chip[levels + i], core[levels + i]
        a, b = jnp.where(parity == 0, x, y), jnp.where(parity == 0, y, x)
        halo_vert[i + 1] = jnp.where(low_half, a, turn(b)) * wet_halo
        halo_vert[half + i + 1] = jnp.where(low_half, turn(a), b) * wet_halo
        return 0

    lax.fori_loop(0, half, spread, 0, unroll=4)

    def moved(level):
        halo = beside(level)
        left, right = shifted(halo)
        return (
            halo
            + halo_left * (left - halo)
            + halo_right * (right - halo)
            + halo_behind * (behind(level) - halo)
            + halo_inside * (packs[8, level] - halo)
        )

    def forward(i, carry):
        c, x, e, b, y, d = carry
        j = levels - 1 - i
        low, upp = halo_vert[i], halo_vert[i + 1]
        inverse = inverse_of(1.0 + low + upp + low * c)
        c = -upp * inverse
        step = low * inverse
        x = moved(i) * inverse + step * x
        e = jnp.where(i == 0, inverse, 0.0) + step * e
        halo_upper[i] = c
        halo_base[i] = x
        halo_impulse[i] = e
        low, upp = halo_vert[j], halo_vert[j + 1]
        inverse = inverse_of(1.0 + low + upp + upp * b)
        b = -low * inverse
        y = moved(j) * inverse + upp * inverse * y
        halo_upper[j] = b
        halo_base[j] = y
        for level in (2 * i, 2 * i + 1):
            rhs = outside * (beside(level) - packs[8, level])
            d = rhs * packs[1, level] + packs[2, level] * d
            delta[level] = d
        return c, x, e, b, y, d

    c, x, e, b, y, d = lax.fori_loop(0, half, forward, (zero,) * 6, unroll=16)
    inverse = 1.0 / (1.0 - c * b)
    x = (x - c * y) * inverse
    e = e * inverse
    y = y - b * x
    h = -b * e
    for level, base, impulse in ((half - 1, x, e), (half, y, h)):
        halo_base[level] = base
        halo_impulse[level] = impulse

    def backward(i, carry):
        x, e, y, h, d = carry
        at, j = half - 2 - i, half + 1 + i
        c, b = halo_upper[at], halo_upper[j]
        x = halo_base[at] - c * x
        e = halo_impulse[at] - c * e
        y = halo_base[j] - b * y
        h = -b * h
        halo_base[at] = x
        halo_impulse[at] = e
        halo_base[j] = y
        halo_impulse[j] = h
        for level in (levels - 2 - 2 * i, levels - 3 - 2 * i):
            d = delta[level] - packs[0, level] * d
            delta[level] = d
        return x, e, y, h, d

    *_, d = lax.fori_loop(0, half - 1, backward, (x, e, y, h, d), unroll=31)
    delta[0] = delta[0] - packs[0, 0] * d

    def forward_fixes(level, carry):
        d = delta[level]
        left, right = shifted(d)
        rhs = (
            d
            + rim_left * (left - d)
            + rim_right * (right - d)
            - rim_inside * d
            + outside * (halo_base[level] - (packs[7, level] + d)),
            outside * halo_impulse[level],
            outside * packs[6, level],
            next_outside * d,
        )
        made = tuple(
            x * packs[1 if i < 3 else 4, level] + packs[2 if i < 3 else 5, level] * r
            for i, (x, r) in enumerate(zip(rhs, carry))
        )
        for i in range(4):
            fixes[i, level] = made[i]
        return made

    carry = lax.fori_loop(0, levels, forward_fixes, (zero,) * 4, unroll=16)

    def backward_fixes(i, carry):
        level = levels - 2 - i
        made = tuple(
            fixes[j, level] - packs[0 if j < 3 else 3, level] * carry[j] for j in range(4)
        )
        for j in range(4):
            fixes[j, level] = made[j]
        return made

    lax.fori_loop(0, levels - 1, backward_fixes, carry, unroll=21)


def last_kernel(cols, groups, mask, parts, fixes, halo_wet, *refs):
    arrived = refs[: groups - 1]
    out, received_out, field, received, rims, sem = refs[groups - 1 :]
    _, levels, height, width = parts.shape
    group = lax.axis_index("grp")
    total = jnp.zeros(arrived[0].shape, jnp.float32)
    for g, other in enumerate(arrived):
        total = total + jnp.where((group == groups - 1) | (group == g), other[...], 0.0)
    for f in range(F):
        for c in range(cols):
            at = (f * cols + c) * height
            received[f, :, c * 128 : (c + 1) * 128] = total[at : at + height, :]
    copies = [pltpu.make_async_copy(received, received_out, sem.at[0])]
    copies[0].start()
    wet = wet_of(lax.axis_index("grp") == groups - 1, mask[...])
    force = FORCING_GAIN * wet * jnp.sum(received[...], 0)
    force_halo = FORCING_GAIN * halo_wet[...] * total[F * cols * height :, :]
    factors = (force,) + around(force)
    force_rim = jnp.concatenate(
        [force[r : r + 1, c * 128 : (c + 1) * 128] for r in (0, height - 1) for c in range(cols)], 0
    )

    rims[...] = fixes[0] + fixes[1] * force_halo[None] - fixes[2] * force_rim[None]
    row = iota((height, 128), 0)

    def level_of(level, _):
        for c in range(cols):
            at = slice(c * 128, (c + 1) * 128)
            x = parts[0, level, :, at]
            for i in range(5):
                x = x + parts[i + 1, level, :, at] * factors[i][:, at]
            one, two = slice(c, c + 1), slice(cols + c, cols + c + 1)
            fix = jnp.where(row == 0, rims[level, one, :], rims[level, two, :])
            near = jnp.where(row == 1, fixes[3, level, one, :], fixes[3, level, two, :])
            x = x + jnp.where((row == 0) | (row == height - 1), fix, 0.0)
            field[level, :, at] = x + jnp.where((row == 1) | (row == height - 2), near, 0.0)
        return 0

    chunks = 8
    size = levels // chunks
    for i in range(chunks):
        lax.fori_loop(i * size, (i + 1) * size, level_of, 0, unroll=8)
        at = pl.ds(i * size, size)
        copies.append(pltpu.make_async_copy(field.at[at], out.at[at], sem.at[i + 1]))
        copies[-1].start()
    for copy in copies:
        copy.wait()


def f32(*shape):
    return jax.ShapeDtypeStruct(shape, jnp.float32)


def cost(us):
    return pl.CostEstimate(flops=0, bytes_accessed=int(us * 3e6), transcendentals=0)


def edges_of(groups, state, vert_coef, horiz_coef, wet_mask, *after):
    levels, height, width = state.shape
    return pl.pallas_call(
        functools.partial(edge_kernel, groups),
        out_shape=(f32(levels + levels // 2 + 2, width // 64, 128),) * 2,
        in_specs=[VM] * 4 + [HBM] * len(after),
        compiler_params=params(8),
        cost_estimate=cost(1),
    )(state, vert_coef, horiz_coef, wet_mask, *after)


def pack(groups, tiles, slots, state, coupling, surface, mask, dtile, dblock, dgroup, w):
    height, width = mask.shape
    cols = width // 128
    blocks = height * cols
    return pl.pallas_call(
        functools.partial(pack_kernel, tiles, slots, groups),
        out_shape=(f32(2 * (F * slots + 16), 128),) * (tiles // 2),
        in_specs=[HBM] * 8,
        scratch_shapes=[
            pltpu.VMEM((blocks * K, F * 128), jnp.float32),
            pltpu.VMEM((cols, height, K, 128, 128), jnp.bfloat16),
        ]
        + [pltpu.VMEM((K, blocks), jnp.int32)] * 3
        + [pltpu.VMEM((height, width), jnp.float32)]
        + [pltpu.VMEM((F, height, width), jnp.float32)] * 2
        + [
            pltpu.VMEM((height, width), jnp.int32),
            pltpu.SemaphoreType.DMA((cols,)),
            pltpu.SemaphoreType.DMA((7,)),
        ],
        compiler_params=params(60),
        cost_estimate=cost(3),
    )(state, coupling, surface, mask, dtile.T, dblock.T, dgroup.T, w.reshape(height, cols, K, 128, 128))


def early(groups, state, vert_coef, horiz_coef, wet_mask, chunk):
    levels, height, width = state.shape
    return pl.pallas_call(
        functools.partial(early_kernel, groups),
        out_shape=(f32(9, levels, width // 64, 128), f32(*chunk.shape))
        + (f32(levels, height, width),) * 5,
        in_specs=[VM] * 4 + [HBM],
        scratch_shapes=[pltpu.SemaphoreType.DMA],
        compiler_params=params(16),
        cost_estimate=cost(3),
    )(state, vert_coef, horiz_coef, wet_mask, chunk)


def parts_of(groups, horiz_coef, wet_mask, solved, after):
    return pl.pallas_call(
        functools.partial(parts_kernel, groups),
        out_shape=f32(6, *solved[0].shape),
        in_specs=[VM] * 8,
        compiler_params=params(16),
        cost_estimate=cost(3),
    )(horiz_coef, wet_mask, *solved, after)


def late(groups, horiz_coef, wet_mask, chip, core, packs, after):
    _, levels, rows, lanes = packs.shape
    return pl.pallas_call(
        functools.partial(late_kernel, groups),
        out_shape=(f32(4, levels, rows, lanes), f32(rows, lanes)),
        in_specs=[VM] * 6,
        scratch_shapes=[pltpu.VMEM((levels, rows, lanes), jnp.float32)] * 3
        + [pltpu.VMEM((levels + 1, rows, lanes), jnp.float32)]
        + [pltpu.VMEM((levels, rows, lanes), jnp.float32)],
        compiler_params=params(12),
        cost_estimate=cost(2),
    )(horiz_coef, wet_mask, chip, core, packs, after)


def finish(groups, wet_mask, parts, fixes, halo_wet, arrived):
    _, levels, height, width = parts.shape
    return pl.pallas_call(
        functools.partial(last_kernel, width // 128, groups),
        out_shape=(f32(levels, height, width), f32(F, height, width)),
        out_specs=(HBM, HBM),
        scratch_shapes=[
            pltpu.VMEM((levels, height, width), jnp.float32),
            pltpu.VMEM((F, height, width), jnp.float32),
            pltpu.VMEM((levels, width // 64, 128), jnp.float32),
            pltpu.SemaphoreType.DMA((8 + 1,)),
        ],
        compiler_params=params(16),
    )(wet_mask, parts, fixes, halo_wet, *arrived)


def local(
    state, vert_coef, horiz_coef, wet_mask, coupling, surface_in, remap_w, dest_tile, dest_block, dest_group
):
    levels, height, width = state.shape
    groups, tiles = lax.axis_size("grp"), lax.axis_size("tile")
    cols = width // 128
    blocks = height * cols
    slots = max(8, 2 * blocks * K // tiles)
    rim = 2 * cols
    devices = groups * tiles
    start = (groups - 1) * tiles
    axes = ("grp", "tile")
    across = [(i, i + 1) for i in range(1, devices - 1, 2) if i + 1 != start]
    across = across + [(j, i) for i, j in across]
    packed = pack(
        groups, tiles, slots, state, coupling, surface_in, wet_mask, dest_tile, dest_block, dest_group, remap_w
    )
    chips = tiles // 2
    moved = {
        k: lax.ppermute(packed[k], "tile", [(i, ((i // 2) ^ k) * 2 + i % 2) for i in range(tiles)])
        for k in sorted(range(1, chips), key=lambda k: (k != chips // 2, k))
    }
    got = [moved[k] for k in range(1, chips)]
    packs, chunk, *solved = early(groups, state, vert_coef, horiz_coef, wet_mask, packed[0])
    chip, core = edges_of(groups, state, vert_coef, horiz_coef, wet_mask, chunk, got[2])
    chip = lax.ppermute(chip, axes, across)
    core = lax.ppermute(core, axes, [(i, i ^ 1) for i in range(devices)])
    rows = (groups - 1) * (F * blocks + rim)
    mine, theirs = pl.pallas_call(
        functools.partial(merge_kernel, slots, height, cols, groups),
        out_shape=(f32(rows, 128),) * 2,
        compiler_params=params(8),
        cost_estimate=cost(1),
    )(chunk, *got)
    parts = parts_of(groups, horiz_coef, wet_mask, solved, mine)
    theirs = lax.ppermute(theirs, "tile", [(i, i ^ 1) for i in range(tiles)])
    merged = pl.pallas_call(
        functools.partial(add_kernel, cols),
        out_shape=(f32(F * blocks + rim, 128),) * (groups - 1),
        compiler_params=params(8),
        cost_estimate=cost(1),
    )(mine, theirs)
    arrived = [
        lax.ppermute(merged[g], "grp", [(j, (j + g + 1) % groups) for j in range(groups)])
        for g in range(groups - 1)
    ]
    fixes, halo_wet = late(groups, horiz_coef, wet_mask, chip, core, packs, merged[0])
    return finish(groups, wet_mask, parts, fixes, halo_wet, arrived)


def solution(mesh):
    in_specs = (
        P(None, ("grp", "tile"), None),
        P(None, ("grp", "tile"), None),
        P(("grp", "tile"), None),
        P("tile", None),
        P(None, ("grp", "tile"), None),
        P(None, ("grp", "tile"), None),
        P(("grp", "tile"), None, None, None),
        P(("grp", "tile"), None),
        P(("grp", "tile"), None),
        P(("grp", "tile"), None),
    )
    out_specs = (P(None, ("grp", "tile"), None), P(None, ("grp", "tile"), None))
    return jax.shard_map(local, mesh=mesh, in_specs=in_specs, out_specs=out_specs, check_vma=False)
```
